128 devices in a mesh: row: 8 (over y, x_lo), col: 16 (over z, x_hi, core).
Axes of the slice: x: 4 (x_hi: 2, x_lo: 2; x = x_hi * 2 + x_lo), y: 4, z: 4, core: 2. Of those that a mesh axis runs over, the one named last changes fastest.
Arguments:
- image: bfloat16 [128, 512, 256], P('row', 'col'), may hold values from -6 to 6
- na_qkv: bfloat16 [256, 768], replicated, as said below
- na_out: bfloat16 [256, 256], replicated, may hold values from -0.375 to 0.375
- merge_one: bfloat16 [1024, 512], replicated, may hold values from -0.1875 to 0.1875
- merge_two: bfloat16 [2048, 1024], replicated, may hold values from -0.125 to 0.125
- attn_qkv: bfloat16 [1024, 3072], replicated, as said below
- attn_out: bfloat16 [1024, 1024], replicated, may hold values from -0.1875 to 0.1875
- cotangent: bfloat16 [32, 128, 1024], P('row', 'col'), may hold values from -6 to 6
Outputs:
- merged_out: bfloat16 [32, 128, 1024], P('row', 'col')
- grad_image: bfloat16 [128, 512, 256], P('row', 'col')
- grad_attn_out: float32 [1024, 1024], P(('row', 'col'))
The draws below stay inside these ranges and needn't reach their ends.
Inputs may be any that keep to these rules, and one draw needn't show every extreme that they name: `na_qkv`: columns hold the query, key and value projections in this order, each split into heads of consecutive columns. `attn_qkv`: columns hold the query, key and value projections in this order, each split into heads of consecutive columns.
All inputs are finite; a program needn't handle non-finite values.
Results may differ from the reference program's by a relative error of at most 0.027.
Values may be sent and summed in bfloat16 or wider, within the bound.
No kernel may reach another device: no remote copies, remote signals or barrier semaphores. Data moves between devices by JAX's collectives and lax.ppermute only.
A program may use at most 128 MiB of HBM per device.

```python
import math
import jax
import jax.numpy as jnp
from jax import lax

C0 = 256
C1 = 512
C2 = 1024
NA_HEADS = 4
GHEADS = 8
KERNEL = 7
H0 = 128
W0 = 512
H2 = 32
W2 = 128


def drawn_projection(key, rows, width):
    base = jax.random.normal(key, (rows, 3, width), jnp.float32) * rows ** (-0.5)
    query = base[:, 0]
    keys = base[:, 1]
    return jnp.stack([query, keys, base[:, 2]], 1).reshape(rows, 3 * width).astype(jnp.bfloat16)


def draw_na_qkv(key, part):
    key = jax.random.fold_in(key, 11)
    return drawn_projection(key, C0, C0)


def draw_attn_qkv(key, part):
    key = jax.random.fold_in(key, 23)
    return drawn_projection(key, C2, C2)


def block_levels(rng, shape, pieces, low, high):
    def one(axis_at, parts):
        draws = jax.random.uniform(jax.random.fold_in(jax.random.fold_in(rng, 6), axis_at), (parts,), jnp.float32, low / len(pieces), high / len(pieces))
        return jnp.repeat(jnp.exp(draws), shape[axis_at] // parts).reshape((-1,) + (1,) * (len(shape) - axis_at - 1))

    factor_of = one(*pieces[0])
    for cut in pieces[1:]:
        factor_of = factor_of * one(*cut)
    return factor_of


def normal_values(key, dims, scale, most, pieces=(), kind=jnp.bfloat16):
    result = scale * jax.random.normal(key, dims, jnp.float32)
    if pieces:
        result = result * block_levels(key, dims, pieces, -0.22, 0.18)
    return jnp.clip(result, -most, most).astype(kind)


def setup_inputs(seed: int = 0) -> dict:
    seeds = jax.random.split(jax.random.key(seed), 9)
    image = normal_values(seeds[0], (H0, W0, C0), 1.0, 6.0, ((0, 8), (1, 16)))
    na_qkv = draw_na_qkv(jax.random.fold_in(seeds[8], 71), 0)
    na_out = normal_values(seeds[2], (C0, C0), C0 ** -0.5, 0.375)
    merge_one = normal_values(seeds[3], (4 * C0, C1), (4 * C0) ** -0.5, 0.1875)
    merge_two = normal_values(seeds[4], (4 * C1, C2), (4 * C1) ** -0.5, 0.125)
    attn_qkv = draw_attn_qkv(jax.random.fold_in(seeds[8], 71), 0)
    attn_out = normal_values(seeds[6], (C2, C2), C2 ** -0.5, 0.1875)
    cotangent = normal_values(seeds[7], (H2, W2, C2), 1.0, 6.0, ((0, 8), (1, 16)))
    return {"image": image, "na_qkv": na_qkv, "na_out": na_out, "merge_one": merge_one, "merge_two": merge_two, "attn_qkv": attn_qkv, "attn_out": attn_out, "cotangent": cotangent}


f32 = jnp.float32
bf16 = jnp.bfloat16
EPSILON = 1e-06

def rms_stat(x):
    return lax.rsqrt(lax.optimization_barrier(jnp.mean(x * x, -1, keepdims=True)) + EPSILON)

def rms_back(x, scale, grad):
    return scale * grad - x * scale ** 3 * lax.optimization_barrier(jnp.mean(grad * x, -1, keepdims=True))

def unshuffle(grid):
    rows, cols, width = grid.shape
    return grid.reshape(rows // 2, 2, cols // 2, 2, width).transpose(0, 2, 1, 3, 4).reshape(rows // 2, cols // 2, 4 * width)

def shuffle(grid):
    rows, cols, width = grid.shape
    return grid.reshape(rows, cols, 2, 2, width // 4).transpose(0, 2, 1, 3, 4).reshape(2 * rows, 2 * cols, width // 4)

def pad_mask(rows, cols, row_first, col_first, total_rows, total_cols):
    row_ids = row_first + jnp.arange(rows + 6, dtype=jnp.int32)
    col_ids = col_first + jnp.arange(cols + 6, dtype=jnp.int32)
    inside_rows = (row_ids >= 0) & (row_ids < total_rows)
    inside_cols = (col_ids >= 0) & (col_ids < total_cols)
    return inside_rows[:, None] & inside_cols[None, :]

def window_scores(query, padded, valid, offset, width):
    rows, cols = (query.shape[0], query.shape[1])
    shift_row = (offset // KERNEL).astype(jnp.int32)
    shift_col = (offset % KERNEL).astype(jnp.int32)
    zero = jnp.zeros((), jnp.int32)
    block = lax.dynamic_slice(padded, (shift_row, shift_col, zero), (rows, cols, padded.shape[2]))
    mask = lax.dynamic_slice(valid, (shift_row, shift_col), (rows, cols))
    return (block, mask)

def split_heads(array):
    return array.reshape(array.shape[0], array.shape[1], NA_HEADS, array.shape[2] // NA_HEADS).astype(f32)

def na_forward(query, kvpad, valid):
    rows, cols, width = query.shape
    scale = 1.0 / math.sqrt(width // NA_HEADS)
    heads_q = split_heads(query)

    def scores_at(offset):
        block, mask = window_scores(query, kvpad, valid, offset, width)
        keys = split_heads(block[..., :width])
        score = lax.optimization_barrier(jnp.sum(heads_q * keys, -1)) * scale
        return jnp.where(mask[..., None], score, -jnp.inf)
    scores = lax.map(scores_at, jnp.arange(KERNEL * KERNEL, dtype=jnp.int32))
    top = lax.optimization_barrier(jnp.max(scores, 0))
    lse = top + jnp.log(lax.optimization_barrier(jnp.sum(jnp.exp(scores - top), 0)))

    def accumulate(offset, acc):
        block, mask = window_scores(query, kvpad, valid, offset, width)
        values = split_heads(block[..., width:])
        prob = jnp.exp(scores[offset] - lse).astype(bf16).astype(f32)
        return acc + prob[..., None] * values
    acc = lax.fori_loop(0, KERNEL * KERNEL, accumulate, jnp.zeros((rows, cols, NA_HEADS, width // NA_HEADS), f32))
    return (acc.reshape(rows, cols, width).astype(bf16), lse)

def na_query_grad(query, kvpad, valid, lse, delta, dout):
    rows, cols, width = query.shape
    scale = 1.0 / math.sqrt(width // NA_HEADS)
    heads_q = split_heads(query)
    heads_d = split_heads(dout)

    def accumulate(offset, acc):
        block, mask = window_scores(query, kvpad, valid, offset, width)
        keys = split_heads(block[..., :width])
        values = split_heads(block[..., width:])
        score = lax.optimization_barrier(jnp.sum(heads_q * keys, -1)) * scale
        prob = jnp.where(mask[..., None], jnp.exp(score - lse), 0.0)
        dprob = lax.optimization_barrier(jnp.sum(heads_d * values, -1))
        dscore = (prob * (dprob - delta)).astype(bf16).astype(f32)
        return acc + dscore[..., None] * keys
    acc = lax.fori_loop(0, KERNEL * KERNEL, accumulate, jnp.zeros((rows, cols, NA_HEADS, width // NA_HEADS), f32))
    return (acc * scale).reshape(rows, cols, width).astype(bf16)

def na_key_grad(keys, values, qdpad, statpad, valid):
    rows, cols, width = keys.shape
    scale = 1.0 / math.sqrt(width // NA_HEADS)
    heads_k = split_heads(keys)
    heads_v = split_heads(values)
    last = jnp.asarray(KERNEL * KERNEL - 1, jnp.int32)

    def accumulate(offset, carry):
        grad_k, grad_v = carry
        block, mask = window_scores(keys, qdpad, valid, last - offset, width)
        stats = window_scores(keys, statpad, valid, last - offset, width)[0]
        queries = split_heads(block[..., :width])
        douts = split_heads(block[..., width:])
        score = lax.optimization_barrier(jnp.sum(queries * heads_k, -1)) * scale
        prob = jnp.where(mask[..., None], jnp.exp(score - stats[..., :NA_HEADS]), 0.0)
        dprob = lax.optimization_barrier(jnp.sum(douts * heads_v, -1))
        dscore = (prob * (dprob - stats[..., NA_HEADS:])).astype(bf16).astype(f32)
        grad_k = grad_k + dscore[..., None] * queries
        grad_v = grad_v + prob.astype(bf16).astype(f32)[..., None] * douts
        return (grad_k, grad_v)
    zeros = jnp.zeros((rows, cols, NA_HEADS, width // NA_HEADS), f32)
    grad_k, grad_v = lax.fori_loop(0, KERNEL * KERNEL, accumulate, (zeros, zeros))
    return ((grad_k * scale).reshape(rows, cols, width).astype(bf16), grad_v.reshape(rows, cols, width).astype(bf16))

def pad_three(array):
    return jnp.pad(array, ((3, 3), (3, 3), (0, 0)))

def reference(image, na_qkv, na_out, merge_one, merge_two, attn_qkv, attn_out, cotangent):
    x = image.astype(f32)
    r0 = rms_stat(x)
    xn = (x * r0).astype(bf16)
    qkv0 = jnp.dot(xn.reshape(-1, C0), na_qkv, preferred_element_type=f32).astype(bf16).reshape(H0, W0, 3 * C0)
    q0 = qkv0[..., :C0]
    kv0 = qkv0[..., C0:]
    valid = pad_mask(H0, W0, -3, -3, H0, W0)
    kvpad = pad_three(kv0)
    a0, lse0 = na_forward(q0, kvpad, valid)
    y0 = (x + jnp.dot(a0.reshape(-1, C0), na_out, preferred_element_type=f32).reshape(H0, W0, C0)).astype(bf16)
    m1 = jnp.dot(unshuffle(y0).reshape(-1, 4 * C0), merge_one, preferred_element_type=f32).astype(bf16).reshape(H0 // 2, W0 // 2, C1)
    m2 = jnp.dot(unshuffle(m1).reshape(-1, 4 * C1), merge_two, preferred_element_type=f32).astype(bf16)
    total = m2.shape[0]
    head = C2 // GHEADS
    scale = 1.0 / math.sqrt(head)
    m2f = m2.astype(f32)
    r2 = rms_stat(m2f)
    mn = (m2f * r2).astype(bf16)
    qkv = jnp.dot(mn, attn_qkv, preferred_element_type=f32).astype(bf16).reshape(total, 3, GHEADS, head)
    query = qkv[:, 0].astype(f32)
    keys = qkv[:, 1].astype(f32)
    values = qkv[:, 2].astype(f32)
    block = math.gcd(total, 512)
    count = total // block

    def forward_block(qb):
        score = jnp.einsum('qhd,khd->qhk', qb, keys) * scale
        top = lax.optimization_barrier(jnp.max(score, -1))
        weight = jnp.exp(score - top[..., None])
        norm = lax.optimization_barrier(jnp.sum(weight, -1))
        out = jnp.einsum('qhk,khd->qhd', weight.astype(bf16).astype(f32), values) / norm[..., None]
        return (out.astype(bf16), top + jnp.log(norm))
    out_heads, lse = lax.map(forward_block, query.reshape(count, block, GHEADS, head))
    out_heads = out_heads.reshape(total, GHEADS, head)
    lse = lse.reshape(total, GHEADS)
    out_tok = out_heads.reshape(total, C2)
    merged = (m2f + jnp.dot(out_tok, attn_out, preferred_element_type=f32)).astype(bf16)
    grad = cotangent.reshape(total, C2)
    grad_wo = jnp.dot(out_tok.T, grad, preferred_element_type=f32)
    dout = jnp.dot(grad, attn_out.T, preferred_element_type=f32).astype(bf16).reshape(total, GHEADS, head)
    delta = lax.optimization_barrier(jnp.sum(dout.astype(f32) * out_heads.astype(f32), -1))

    def backward_block(carry, items):
        grad_k, grad_v = carry
        qb, db, lb, eb = items
        score = jnp.einsum('qhd,khd->qhk', qb, keys) * scale
        prob = jnp.exp(score - lb[..., None])
        dprob = jnp.einsum('qhd,khd->qhk', db, values)
        dscore = (prob * (dprob - eb[..., None])).astype(bf16).astype(f32)
        grad_q = (jnp.einsum('qhk,khd->qhd', dscore, keys) * scale).astype(bf16)
        grad_k = grad_k + jnp.einsum('qhk,qhd->khd', dscore, qb) * scale
        grad_v = grad_v + jnp.einsum('qhk,qhd->khd', prob.astype(bf16).astype(f32), db)
        return ((grad_k, grad_v), grad_q)
    zeros = jnp.zeros((total, GHEADS, head), f32)
    items = (query.reshape(count, block, GHEADS, head), dout.astype(f32).reshape(count, block, GHEADS, head), lse.reshape(count, block, GHEADS), delta.reshape(count, block, GHEADS))
    (grad_k, grad_v), grad_q = lax.scan(backward_block, (zeros, zeros), items)
    dqkv = jnp.stack([grad_q.reshape(total, GHEADS, head), grad_k.astype(bf16), grad_v.astype(bf16)], 1).reshape(total, 3 * C2)
    dmn = jnp.dot(dqkv, attn_qkv.T, preferred_element_type=f32)
    dm2 = (grad.astype(f32) + rms_back(m2f, r2, dmn)).astype(bf16)
    du2 = jnp.dot(dm2, merge_two.T, preferred_element_type=f32).astype(bf16).reshape(H2, W2, 4 * C1)
    dm1 = shuffle(du2)
    du1 = jnp.dot(dm1.reshape(-1, C1), merge_one.T, preferred_element_type=f32).astype(bf16).reshape(H0 // 2, W0 // 2, 4 * C0)
    dy0 = shuffle(du1)
    da0 = jnp.dot(dy0.reshape(-1, C0), na_out.T, preferred_element_type=f32).astype(bf16).reshape(H0, W0, C0)
    delta0 = lax.optimization_barrier(jnp.sum(split_heads(da0) * split_heads(a0), -1))
    dq0 = na_query_grad(q0, kvpad, valid, lse0, delta0, da0)
    qdpad = pad_three(jnp.concatenate([q0, da0], -1))
    statpad = pad_three(jnp.concatenate([lse0, delta0], -1))
    dk0, dv0 = na_key_grad(kv0[..., :C0], kv0[..., C0:], qdpad, statpad, valid)
    dxn = jnp.dot(jnp.concatenate([dq0, dk0, dv0], -1).reshape(-1, 3 * C0), na_qkv.T, preferred_element_type=f32).reshape(H0, W0, C0)
    grad_image = (dy0.astype(f32) + rms_back(x, r0, dxn)).astype(bf16)
    return (merged.reshape(H2, W2, C2), grad_image, grad_wo)
```

```python
import math

import jax
import jax.numpy as jnp
from jax import lax
from jax.sharding import PartitionSpec as P

C0 = 256
C1 = 512
C2 = 1024
NA_HEADS = 4
GHEADS = 8
KERNEL = 7


f32 = jnp.float32
bf16 = jnp.bfloat16
EPSILON = 1e-06


def extended(shard, sides, width):
    for axis, dim in sides:
        count, length = (lax.axis_size(axis), shard.shape[dim])
        up = [(i, (i + 1) % count) for i in range(count - 1)]
        down = [(j, i) for i, j in up]
        last = lax.slice_in_dim(shard, length - width, length, axis=dim)
        leading = lax.slice_in_dim(shard, 0, width, axis=dim)
        before = lax.ppermute(last, axis, up)
        after = lax.ppermute(leading, axis, down)
        shard = jnp.concatenate([before, shard, after], axis=dim)
    return shard


def shifted(array, axis, count, move):
    return lax.ppermute(array, axis, [(i, move(i)) for i in range(count)])


def gather_columns(shard):
    count = lax.axis_size("col")
    shard = jnp.concatenate([shard, shifted(shard, "col", count, lambda i: i ^ 2)], 0)
    pieces = [shard]
    for step in (1, 2, 3):
        pieces.append(shifted(shard, "col", count, lambda i: (i + 4 * step) % count))
    shard = jnp.concatenate(pieces, 0)
    return jnp.concatenate([shard, shifted(shard, "col", count, lambda i: i ^ 1)], 0)


def column_order(count):
    me = lax.axis_index("col")
    place = jnp.arange(count, dtype=jnp.int32)
    source = (me + count - 4 * ((place // 2) % 4)) % count
    return source ^ (2 * (place % 2)) ^ (place // 8)


def rms_stat(x):
    return lax.rsqrt(jnp.mean(x * x, -1, keepdims=True) + EPSILON)


def rms_back(x, scale, grad):
    return scale * grad - x * scale**3 * jnp.mean(grad * x, -1, keepdims=True)


def unshuffle(grid):
    rows, cols, width = grid.shape
    return (
        grid.reshape(rows // 2, 2, cols // 2, 2, width)
        .transpose(0, 2, 1, 3, 4)
        .reshape(rows // 2, cols // 2, 4 * width)
    )


def shuffle(grid):
    rows, cols, width = grid.shape
    return (
        grid.reshape(rows, cols, 2, 2, width // 4)
        .transpose(0, 2, 1, 3, 4)
        .reshape(2 * rows, 2 * cols, width // 4)
    )


def pad_mask(rows, cols, row_first, col_first, total_rows, total_cols):
    row_ids = row_first + jnp.arange(rows + 6, dtype=jnp.int32)
    col_ids = col_first + jnp.arange(cols + 6, dtype=jnp.int32)
    inside_rows = (row_ids >= 0) & (row_ids < total_rows)
    inside_cols = (col_ids >= 0) & (col_ids < total_cols)
    return inside_rows[:, None] & inside_cols[None, :]


def window_mask(rows, cols, valid):
    padded_cols = cols + KERNEL - 1
    own = jnp.arange(rows * cols, dtype=jnp.int32)
    own_row = own // cols
    own_col = own % cols
    padded = jnp.arange((rows + KERNEL - 1) * padded_cols, dtype=jnp.int32)
    pad_row = padded // padded_cols
    pad_col = padded % padded_cols
    row_gap = pad_row[None, :] - own_row[:, None]
    col_gap = pad_col[None, :] - own_col[:, None]
    inside = (row_gap >= 0) & (row_gap < KERNEL) & (col_gap >= 0) & (col_gap < KERNEL)
    return inside & valid.reshape(-1)[None, :]


def split_heads(array):
    return array.reshape(
        array.shape[0], array.shape[1], NA_HEADS, array.shape[2] // NA_HEADS
    ).astype(f32)


def flat_heads(array, width):
    return array.reshape(-1, NA_HEADS, width // NA_HEADS)


def na_forward(query, kvpad, mask):
    rows, cols, width = query.shape
    scale = 1.0 / math.sqrt(width // NA_HEADS)
    flat = kvpad.reshape(-1, 2 * width)
    keys = flat_heads(flat[:, :width], width)
    values = flat_heads(flat[:, width:], width)
    score = (
        jnp.einsum("qhd,khd->hqk", flat_heads(query, width), keys, preferred_element_type=f32)
        * scale
    )
    score = jnp.where(mask[None], score, -jnp.inf)
    top = jnp.max(score, -1)
    lse = top + jnp.log(jnp.sum(jnp.exp(score - top[..., None]), -1))
    prob = jnp.exp(score - lse[..., None]).astype(bf16)
    out = jnp.einsum("hqk,khd->qhd", prob, values, preferred_element_type=f32)
    return (out.reshape(rows, cols, width).astype(bf16), lse.T.reshape(rows, cols, NA_HEADS))


def na_query_grad(query, kvpad, mask, lse, delta, dout):
    rows, cols, width = query.shape
    scale = 1.0 / math.sqrt(width // NA_HEADS)
    flat = kvpad.reshape(-1, 2 * width)
    keys = flat_heads(flat[:, :width], width)
    values = flat_heads(flat[:, width:], width)
    lse_heads = lse.reshape(-1, NA_HEADS).T
    delta_heads = delta.reshape(-1, NA_HEADS).T
    score = (
        jnp.einsum("qhd,khd->hqk", flat_heads(query, width), keys, preferred_element_type=f32)
        * scale
    )
    prob = jnp.where(mask[None], jnp.exp(score - lse_heads[..., None]), 0.0)
    dprob = jnp.einsum("qhd,khd->hqk", flat_heads(dout, width), values, preferred_element_type=f32)
    dscore = (prob * (dprob - delta_heads[..., None])).astype(bf16)
    grad_q = jnp.einsum("hqk,khd->qhd", dscore, keys, preferred_element_type=f32) * scale
    return grad_q.reshape(rows, cols, width).astype(bf16)


def na_key_grad(keys, values, qdpad, statpad, mask):
    rows, cols, width = keys.shape
    scale = 1.0 / math.sqrt(width // NA_HEADS)
    flat = qdpad.reshape(-1, 2 * width)
    queries = flat_heads(flat[:, :width], width)
    douts = flat_heads(flat[:, width:], width)
    stats = statpad.reshape(-1, 2 * NA_HEADS)
    lse_heads = stats[:, :NA_HEADS].T
    delta_heads = stats[:, NA_HEADS:].T
    score = (
        jnp.einsum("khd,qhd->hkq", flat_heads(keys, width), queries, preferred_element_type=f32)
        * scale
    )
    prob = jnp.where(mask[None], jnp.exp(score - lse_heads[:, None, :]), 0.0)
    dprob = jnp.einsum("khd,qhd->hkq", flat_heads(values, width), douts, preferred_element_type=f32)
    dscore = (prob * (dprob - delta_heads[:, None, :])).astype(bf16)
    grad_k = jnp.einsum("hkq,qhd->khd", dscore, queries, preferred_element_type=f32) * scale
    grad_v = jnp.einsum("hkq,qhd->khd", prob.astype(bf16), douts, preferred_element_type=f32)
    return (
        grad_k.reshape(rows, cols, width).astype(bf16),
        grad_v.reshape(rows, cols, width).astype(bf16),
    )


def contract_last(left, right):
    return lax.dot_general(left, right, (((1,), (1,)), ((), ())), preferred_element_type=f32)


def per_device(image, na_qkv, na_out, merge_one, merge_two, attn_qkv, attn_out, cotangent):
    rows, cols, width = image.shape
    n_row = lax.axis_size("row")
    n_col = lax.axis_size("col")
    grad = cotangent.reshape(-1, C2)
    head = C2 // GHEADS
    grad_row = lax.all_gather(grad, "row", axis=0, tiled=True)
    own_out = lax.dynamic_slice_in_dim(attn_out, lax.axis_index("row") * head, head, 0)
    dout = contract_last(grad_row, own_out).astype(bf16)
    all_dout = lax.all_gather(dout, "col", axis=0, tiled=True)
    x = image.astype(f32)
    r0 = rms_stat(x)
    xn = (x * r0).astype(bf16)
    qkv0 = (
        jnp.dot(xn.reshape(-1, width), na_qkv, preferred_element_type=f32)
        .astype(bf16)
        .reshape(rows, cols, 3 * width)
    )
    q0 = qkv0[..., :width]
    kv0 = qkv0[..., width:]
    valid = pad_mask(
        rows,
        cols,
        lax.axis_index("row") * rows - 3,
        lax.axis_index("col") * cols - 3,
        rows * n_row,
        cols * n_col,
    )
    mask = window_mask(rows, cols, valid)
    kvpad = extended(kv0, (("row", 0), ("col", 1)), 3)
    a0, lse0 = na_forward(q0, kvpad, mask)
    y0 = (
        x
        + jnp.dot(a0.reshape(-1, width), na_out, preferred_element_type=f32).reshape(
            rows, cols, width
        )
    ).astype(bf16)
    m1 = (
        jnp.dot(unshuffle(y0).reshape(-1, 4 * C0), merge_one, preferred_element_type=f32)
        .astype(bf16)
        .reshape(rows // 2, cols // 2, C1)
    )
    m2 = jnp.dot(unshuffle(m1).reshape(-1, 4 * C1), merge_two, preferred_element_type=f32).astype(
        bf16
    )
    tokens = m2.shape[0]
    scale = 1.0 / math.sqrt(head)
    m2f = m2.astype(f32)
    r2 = rms_stat(m2f)
    mn = (m2f * r2).astype(bf16)
    qkv = (
        jnp.dot(mn, attn_qkv, preferred_element_type=f32)
        .astype(bf16)
        .reshape(tokens, 3, GHEADS, head)
    )
    gathered = lax.all_to_all(
        qkv.transpose(2, 0, 1, 3).reshape(GHEADS, tokens, 3 * head),
        "row",
        split_axis=0,
        concat_axis=0,
        tiled=True,
    ).reshape(-1, 3 * head)
    owned = gathered.shape[0]
    query = gathered[:, :head]
    every = gather_columns(gathered)
    keys = every[:, head : 2 * head]
    values = every[:, 2 * head :]
    score = jnp.einsum("qd,kd->qk", query, keys, preferred_element_type=f32) * scale
    top = jnp.max(score, -1, keepdims=True)
    weight = jnp.exp(score - top)
    norm = jnp.sum(weight, -1, keepdims=True)
    acc = jnp.dot(weight.astype(bf16), values, preferred_element_type=f32)
    lse = top + jnp.log(norm)
    out_heads = (acc / norm).astype(bf16)
    delta = jnp.sum(dout.astype(f32) * out_heads.astype(f32), -1, keepdims=True)
    stats = jnp.concatenate([lse, delta], 1).T
    all_stats = gather_columns(jnp.pad(stats, ((0, 6), (0, 0))))
    out_tok = (
        lax.all_to_all(
            out_heads.reshape(n_row, tokens, head), "row", split_axis=0, concat_axis=0, tiled=True
        )
        .transpose(1, 0, 2)
        .reshape(tokens, C2)
    )
    merged = (m2f + jnp.dot(out_tok, attn_out, preferred_element_type=f32)).astype(bf16)
    partial = lax.dot_general(
        out_heads, grad_row, (((0,), (0,)), ((), ())), preferred_element_type=f32
    )
    partial = lax.all_to_all(
        partial.astype(bf16).reshape(n_col, head // n_col, C2),
        "col",
        split_axis=0,
        concat_axis=0,
        tiled=True,
    )
    grad_wo = jnp.sum(partial.astype(f32), 0)
    score = jnp.einsum("qd,kd->qk", query, keys, preferred_element_type=f32) * scale
    prob = jnp.exp(score - lse)
    dprob = jnp.einsum("qd,kd->qk", dout, values, preferred_element_type=f32)
    dscore = (prob * (dprob - delta)).astype(bf16)
    grad_q = jnp.dot(dscore, keys, preferred_element_type=f32) * scale
    own_keys = gathered[:, head : 2 * head]
    own_values = gathered[:, 2 * head :]
    queries = every[:, :head]
    order = column_order(n_col)
    douts = jnp.take(all_dout.reshape(n_col, owned, head), order, axis=0).reshape(-1, head)
    all_lse = all_stats.reshape(n_col, 8, owned)[:, 0].reshape(1, -1)
    all_delta = all_stats.reshape(n_col, 8, owned)[:, 1].reshape(1, -1)
    score = jnp.einsum("kd,qd->kq", own_keys, queries, preferred_element_type=f32) * scale
    prob = jnp.exp(score - all_lse)
    dprob = jnp.einsum("kd,qd->kq", own_values, douts, preferred_element_type=f32)
    dscore = (prob * (dprob - all_delta)).astype(bf16)
    grad_k = jnp.dot(dscore, queries, preferred_element_type=f32) * scale
    grad_v = jnp.dot(prob.astype(bf16), douts, preferred_element_type=f32)
    dqkv_heads = jnp.concatenate(
        [grad_q.astype(bf16), grad_k.astype(bf16), grad_v.astype(bf16)], 1
    ).reshape(n_row, tokens, 3 * head)
    dqkv = (
        lax.all_to_all(dqkv_heads, "row", split_axis=0, concat_axis=0, tiled=True)
        .reshape(GHEADS, tokens, 3, head)
        .transpose(1, 2, 0, 3)
        .reshape(tokens, 3 * C2)
    )
    dmn = contract_last(dqkv, attn_qkv)
    dm2 = (grad.astype(f32) + rms_back(m2f, r2, dmn)).astype(bf16)
    du2 = contract_last(dm2, merge_two).astype(bf16).reshape(rows // 4, cols // 4, 4 * C1)
    dm1 = shuffle(du2)
    du1 = (
        contract_last(dm1.reshape(-1, C1), merge_one)
        .astype(bf16)
        .reshape(rows // 2, cols // 2, 4 * C0)
    )
    dy0 = shuffle(du1)
    da0 = contract_last(dy0.reshape(-1, width), na_out).astype(bf16).reshape(rows, cols, width)
    delta0 = jnp.sum(split_heads(da0) * split_heads(a0), -1)
    dq0 = na_query_grad(q0, kvpad, mask, lse0, delta0, da0)
    qdpad = extended(jnp.concatenate([q0, da0], -1), (("row", 0), ("col", 1)), 3)
    statpad = extended(jnp.concatenate([lse0, delta0], -1), (("row", 0), ("col", 1)), 3)
    dk0, dv0 = na_key_grad(kv0[..., :width], kv0[..., width:], qdpad, statpad, mask)
    dxn = contract_last(
        jnp.concatenate([dq0, dk0, dv0], -1).reshape(-1, 3 * width), na_qkv
    ).reshape(rows, cols, width)
    grad_image = (dy0.astype(f32) + rms_back(x, r0, dxn)).astype(bf16)
    return (merged.reshape(rows // 4, cols // 4, C2), grad_image, grad_wo)


def solution(mesh):
    return jax.shard_map(
        per_device,
        mesh=mesh,
        in_specs=(P("row", "col", None), P(), P(), P(), P(), P(), P(), P("row", "col", None)),
        out_specs=(P("row", "col", None), P("row", "col", None), P(("row", "col"), None)),
        check_vma=False,
    )
```

```python
import functools
import math

import jax
import jax.numpy as jnp
import numpy as np
from jax import lax
from jax.experimental import pallas as pl
from jax.experimental.pallas import tpu as pltpu
from jax.sharding import PartitionSpec as P

C0 = 256
C1 = 512
C2 = 1024
NA_HEADS = 4
GHEADS = 8
KERNEL = 7
REACH = KERNEL // 2
EPSILON = 1e-06
LANES = 128
NA_DIM = C0 // NA_HEADS
WIDE = NA_HEADS * LANES
MASKED = -1e15
DELTA_LANE = 112
LSE_LANE = 114

f32 = jnp.float32
bf16 = jnp.bfloat16


def dot(left, right):
    return lax.dot_general(left, right, (((1,), (0,)), ((), ())), preferred_element_type=f32)


def dot_last(left, right):
    return lax.dot_general(left, right, (((1,), (1,)), ((), ())), preferred_element_type=f32)


def dot_first(left, right):
    return lax.dot_general(left, right, (((0,), (0,)), ((), ())), preferred_element_type=f32)


def rms_stat(x):
    return lax.rsqrt(jnp.mean(x * x, -1, keepdims=True) + EPSILON)


def rms_back(x, scale, grad):
    return scale * grad - x * scale**3 * jnp.mean(grad * x, -1, keepdims=True)


def token_tables(rows, cols):
    grid = np.arange(rows * cols).reshape(rows // 4, 2, 2, cols // 4, 2, 2)
    order = grid.transpose(2, 5, 1, 4, 0, 3).reshape(-1)
    own_row, own_col = order // cols, order % cols
    halo = []
    halo += [(r, c) for r in range(-REACH, 0) for c in range(cols)]
    halo += [(r, c) for r in range(rows, rows + REACH) for c in range(cols)]
    halo += [(r, c) for r in range(-REACH, rows + REACH) for c in range(-REACH, 0)]
    halo += [(r, c) for r in range(-REACH, rows + REACH) for c in range(cols, cols + REACH)]
    count = len(halo)
    padded = -(-count // LANES) * LANES
    halo = np.array(halo + [(-99, -99)] * (padded - count))

    def band(row, col):
        near_row = np.abs(row[:, None] - np.arange(rows)[None]) <= REACH
        near_col = np.abs(col[:, None] - np.arange(cols)[None]) <= REACH
        return np.where(np.concatenate([near_row, near_col], 1), 0.0, MASKED)

    def lanes(part):
        table = np.zeros((part.shape[0], LANES), np.float32)
        table[:, NA_DIM : NA_DIM + part.shape[1]] = part
        return table

    hot = np.concatenate(
        [own_row[:, None] == np.arange(rows)[None], own_col[:, None] == np.arange(cols)[None]], 1
    ).astype(np.float32)
    perm = np.zeros((rows * cols, rows * cols), np.float32)
    perm[np.arange(rows * cols), order] = 1.0
    place = np.argsort(order)
    natural = np.arange(rows * cols).reshape(rows, cols)
    strips = [natural[:REACH], natural[-REACH:], natural[:, :REACH], natural[:, -REACH:]]
    wanted = place[np.concatenate([s.reshape(-1) for s in strips])]
    select = np.zeros((wanted.size, rows * cols), np.float32)
    select[np.arange(wanted.size), wanted] = 1.0
    return dict(
        perm=perm,
        select=select,
        hot=lanes(hot),
        band_own=lanes(band(own_row, own_col)),
        band_halo=lanes(band(halo[:, 0], halo[:, 1])),
        halo=halo,
        count=count,
    )


def shifted(array, axis, move):
    count = lax.axis_size(axis)
    return lax.ppermute(array, axis, [(i, move(i)) for i in range(count)])


def neighbours(to_next, to_previous, axis):
    count = lax.axis_size(axis)
    up = [(i, i + 1) for i in range(count - 1)]
    down = [(j, i) for i, j in up]
    return lax.ppermute(to_next, axis, up), lax.ppermute(to_previous, axis, down)


def halo_of(top, bottom, left, right, cols, padded):
    width = top.shape[-1]
    before, after = neighbours(bottom, top, "row")
    corner = lambda strip, part: strip.reshape(REACH, cols, width)[:, part].reshape(-1, width)
    first, last = slice(0, REACH), slice(cols - REACH, cols)
    left = jnp.concatenate([corner(before, first), left, corner(after, first)], 0)
    right = jnp.concatenate([corner(before, last), right, corner(after, last)], 0)
    from_left, from_right = neighbours(right, left, "col")
    parts = [before, after, from_left, from_right]
    spare = padded - sum(p.shape[0] for p in parts)
    return jnp.concatenate(parts + [jnp.zeros((spare, width), top.dtype)], 0)


def gather_columns(shard):
    count = lax.axis_size("col")
    shard = jnp.concatenate([shard, shifted(shard, "col", lambda i: i ^ 2)], 0)
    pieces = [shard]
    for step in (1, 2, 3):
        pieces.append(shifted(shard, "col", lambda i: (i + 4 * step) % count))
    shard = jnp.concatenate(pieces, 0)
    return jnp.concatenate([shard, shifted(shard, "col", lambda i: i ^ 1)], 0)


def column_order():
    count = lax.axis_size("col")
    place = jnp.arange(count, dtype=jnp.int32)
    source = (lax.axis_index("col") + count - 4 * ((place // 2) % 4)) % count
    return source ^ (2 * (place % 2)) ^ (place // 8)


def all_to_all(array, axis):
    return lax.all_to_all(array, axis, split_axis=0, concat_axis=0, tiled=True)


def call(kernel, outs, args, scratch=(), smem=0, manual=0, megabytes=50):
    specs = [pl.BlockSpec(memory_space=pltpu.SMEM)] * smem
    specs += [pl.BlockSpec(memory_space=pltpu.VMEM)] * (len(args) - smem - manual)
    specs += [pl.BlockSpec(memory_space=pl.ANY)] * manual
    return pl.pallas_call(
        kernel,
        out_shape=[jax.ShapeDtypeStruct(shape, dtype) for shape, dtype in outs],
        in_specs=specs,
        out_specs=[pl.BlockSpec(memory_space=pltpu.VMEM)] * len(outs),
        scratch_shapes=list(scratch),
        compiler_params=pltpu.CompilerParams(vmem_limit_bytes=megabytes * 2**20),
    )(*args)


def head_lanes(head):
    return slice(head * LANES, (head + 1) * LANES)


def two_parts(value):
    high = value.astype(bf16).astype(f32)
    return high, value - high


def at_lanes(base, lane, first, value):
    high, low = two_parts(value)
    return jnp.where(lane == first, -high, jnp.where(lane == first + 1, -low, base))


def na_forward_kernel(
    x_ref,
    halo_ref,
    perm_ref,
    hot_ref,
    band_own_ref,
    band_halo_ref,
    w_ref,
    w_out_ref,
    one_hbm,
    two_hbm,
    qkv_hbm,
    qkv_out,
    m2_out,
    q_out,
    k_out,
    v_out,
    q_halo_out,
    a0_out,
    one_ref,
    two_ref,
    wqkv_ref,
    sems,
):
    copies = [
        pltpu.make_async_copy(src, dst, sems.at[i])
        for i, (src, dst) in enumerate([(one_hbm, one_ref), (two_hbm, two_ref), (qkv_hbm, wqkv_ref)])
    ]
    for copy in copies:
        copy.start()
    own = x_ref.shape[0]
    x = dot(perm_ref[...], x_ref[...])
    xn = (x * rms_stat(x)).astype(bf16)
    xh = halo_ref[...].astype(f32)
    xhn = (xh * rms_stat(xh)).astype(bf16)
    mine = dot(xn, w_ref[...])
    beside = dot(xhn, w_ref[...])
    lane = lax.broadcasted_iota(jnp.int32, (1, LANES), 1)
    is_lse = (lane == LSE_LANE) | (lane == LSE_LANE + 1)
    is_delta = (lane == DELTA_LANE) | (lane == DELTA_LANE + 1)
    one_lse = jnp.where(is_lse, 1.0, 0.0)
    one_delta = jnp.where(is_delta, 1.0, 0.0)
    hot = hot_ref[...].astype(f32)
    band_own = band_own_ref[...].astype(f32)
    band_halo = band_halo_ref[...].astype(f32)
    y = x
    for h in range(NA_HEADS):
        at = head_lanes(h)
        kat = head_lanes(NA_HEADS + h)
        vat = head_lanes(2 * NA_HEADS + h)
        q = mine[:, at] + hot
        k_out[:own, at] = (mine[:, kat] + (band_own + one_lse)).astype(bf16)
        k_out[own:, at] = (beside[:, kat] + (band_halo + one_lse)).astype(bf16)
        v_out[:own, at] = (mine[:, vat] + one_delta).astype(bf16)
        v_out[own:, at] = (beside[:, vat] + one_delta).astype(bf16)
        q_halo_out[:, at] = (beside[:, at] + band_halo).astype(bf16)
        score = dot_last(q.astype(bf16), k_out[:, at])
        top = jnp.max(score, -1, keepdims=True)
        weight = jnp.exp(score - top).astype(bf16)
        out = dot(weight, v_out[:, at])
        norm = out[:, DELTA_LANE : DELTA_LANE + 1]
        q_out[:, at] = at_lanes(q, lane, LSE_LANE, top + jnp.log(norm)).astype(bf16)
        a0 = jnp.where(lane < NA_DIM, out / norm, 0.0).astype(bf16)
        a0_out[:, at] = a0
    y = (x + dot(a0_out[...], w_out_ref[...])).astype(bf16)
    quarter = own // 4
    copies[0].wait()
    m1 = dot(y[:quarter], one_ref[:C0])
    for part in range(1, 4):
        m1 += dot(y[part * quarter : (part + 1) * quarter], one_ref[part * C0 : (part + 1) * C0])
    m1 = m1.astype(bf16)
    tokens = own // 16
    copies[1].wait()
    m2 = dot(m1[:tokens], two_ref[:C1])
    for part in range(1, 4):
        m2 += dot(m1[part * tokens : (part + 1) * tokens], two_ref[part * C1 : (part + 1) * C1])
    m2 = m2.astype(bf16)
    m2_out[...] = m2
    m2f = m2.astype(f32)
    mn = (m2f * rms_stat(m2f)).astype(bf16)
    copies[2].wait()
    qkv = dot(mn, wqkv_ref[...]).astype(bf16)
    dim = C2 // GHEADS
    for h in range(GHEADS):
        for part in range(3):
            first = part * C2 + h * dim
            qkv_out[h, :, part * dim : (part + 1) * dim] = qkv[:, first : first + dim]


def attention_kernel(scale, q_ref, dout_ref, kv_ref, out_ref, col_ref, row_ref):
    dim = q_ref.shape[1]
    score = dot_last(q_ref[...], kv_ref[:, :dim]) * scale
    top = jnp.max(score, -1, keepdims=True)
    weight = jnp.exp(score - top)
    norm = jnp.sum(weight, -1, keepdims=True)
    out = (dot(weight.astype(bf16), kv_ref[:, dim:]) / norm).astype(bf16)
    out_ref[...] = out
    lse = top + jnp.log(norm)
    delta = jnp.sum(dout_ref[...].astype(f32) * out.astype(f32), -1, keepdims=True)
    lane = lax.broadcasted_iota(jnp.int32, (1, LANES), 1)
    stats = jnp.where(lane == 0, lse, jnp.where(lane == 1, delta, 0.0))
    col_ref[...] = stats
    row_ref[...] = stats.T[:8]


def query_grad_kernel(scale, q_ref, dout_ref, kv_ref, out_ref, col_ref, grad_ref, dq_ref, part_ref):
    dim = q_ref.shape[1]
    keys, values = kv_ref[:, :dim], kv_ref[:, dim:]
    prob = jnp.exp(dot_last(q_ref[...], keys) * scale - col_ref[:, 0:1])
    dprob = dot_last(dout_ref[...], values)
    dscore = (prob * (dprob - col_ref[:, 1:2])).astype(bf16)
    dq_ref[...] = (dot(dscore, keys) * scale).astype(bf16)
    part_ref[...] = dot_first(out_ref[...], grad_ref[...]).astype(bf16)


def key_grad_kernel(scale, order_ref, own_ref, q_ref, dout_ref, stat_ref, dq_ref, out_ref, dout_in, row_in):
    dim = q_ref.shape[1]
    owned = own_ref.shape[0]
    pieces = stat_ref.shape[0]
    for i in range(pieces):
        source = order_ref[i]
        dout_in[i * owned : (i + 1) * owned, :] = dout_ref[source]
        row_in[:, i * owned : (i + 1) * owned] = stat_ref[i]
    keys, values = own_ref[:, dim : 2 * dim], own_ref[:, 2 * dim :]
    queries, douts = q_ref[...], dout_in[...]
    prob = jnp.exp(dot_last(keys, queries) * scale - row_in[0:1, :])
    dprob = dot_last(values, douts)
    dscore = (prob * (dprob - row_in[1:2, :])).astype(bf16)
    out_ref[:, :dim] = dq_ref[...]
    out_ref[:, dim : 2 * dim] = (dot(dscore, queries) * scale).astype(bf16)
    out_ref[:, 2 * dim :] = dot(prob.astype(bf16), douts).astype(bf16)


def merge_back_kernel(
    dqkv_ref,
    m2_ref,
    grad_ref,
    a0_ref,
    q_ref,
    select_ref,
    w_out_ref,
    qkv_hbm,
    two_hbm,
    one_hbm,
    dout_out,
    dy_out,
    strip_out,
    wqkv_ref,
    two_ref,
    one_ref,
    sems,
):
    copies = [
        pltpu.make_async_copy(src, dst, sems.at[i])
        for i, (src, dst) in enumerate([(qkv_hbm, wqkv_ref), (two_hbm, two_ref), (one_hbm, one_ref)])
    ]
    for copy in copies:
        copy.start()
    dim = C2 // GHEADS
    dqkv = jnp.concatenate(
        [
            dqkv_ref[h, :, part * dim : (part + 1) * dim]
            for part in range(3)
            for h in range(GHEADS)
        ],
        1,
    )
    m2 = m2_ref[...].astype(f32)
    copies[0].wait()
    dmn = dot_last(dqkv, wqkv_ref[...])
    dm2 = (grad_ref[...].astype(f32) + rms_back(m2, rms_stat(m2), dmn)).astype(bf16)
    copies[1].wait()
    du2 = dot_last(dm2, two_ref[...]).astype(bf16)
    dm1 = jnp.concatenate([du2[:, part * C1 : (part + 1) * C1] for part in range(4)], 0)
    copies[2].wait()
    du1 = dot_last(dm1, one_ref[...]).astype(bf16)
    dy = jnp.concatenate([du1[:, part * C0 : (part + 1) * C0] for part in range(4)], 0)
    dy_out[...] = dy
    da0 = dot_last(dy, w_out_ref[...]).astype(bf16).astype(f32)
    lane = lax.broadcasted_iota(jnp.int32, (1, LANES), 1)
    is_lse = (lane == LSE_LANE) | (lane == LSE_LANE + 1)
    for h in range(NA_HEADS):
        at = head_lanes(h)
        mine = da0[:, at]
        delta = jnp.sum(mine * a0_ref[:, at].astype(f32), -1, keepdims=True)
        mine = jnp.where(is_lse, q_ref[:, at].astype(f32), mine)
        dout_out[:, at] = at_lanes(mine, lane, DELTA_LANE, delta).astype(bf16)
    strip_out[...] = dot(select_ref[...], dout_out[...]).astype(bf16)


def na_own_kernel(q_ref, k_ref, v_ref, dout_ref, dq_out, dk_out, dv_out):
    own = q_ref.shape[0]
    lane = lax.broadcasted_iota(jnp.int32, (1, LANES), 1)
    for h in range(NA_HEADS):
        at = head_lanes(h)
        prob = jnp.exp(dot_last(q_ref[:, at], k_ref[:, at]))
        dprob = dot_last(dout_ref[:, at], v_ref[:, at])
        dscore = (prob * dprob).astype(bf16)
        dq = dot(dscore, k_ref[:, at])
        dq_out[:, at] = jnp.where(lane < NA_DIM, dq, 0.0).astype(bf16)
        dk_out[:, at] = dot_first(dscore[:, :own], q_ref[:, at])
        dv_out[:, at] = dot_first(prob[:, :own].astype(bf16), dout_ref[:, at])


def na_beside_kernel(
    x_ref,
    perm_ref,
    perm_back_ref,
    w_ref,
    hot_ref,
    k_ref,
    v_ref,
    q_halo_ref,
    dout_halo_ref,
    dy_ref,
    dq_ref,
    dk_ref,
    dv_ref,
    grad_out,
):
    lane = lax.broadcasted_iota(jnp.int32, (1, LANES), 1)
    is_mask = (lane >= NA_DIM) & (lane < DELTA_LANE)
    is_lse = (lane == LSE_LANE) | (lane == LSE_LANE + 1)
    x = dot(perm_ref[...], x_ref[...])
    hot = hot_ref[...].astype(f32)
    dxn = dot_last(dq_ref[...], w_ref[:, : NA_HEADS * LANES])
    for h in range(NA_HEADS):
        at = head_lanes(h)
        keys = jnp.where(is_mask, hot, k_ref[:, at].astype(f32)).astype(bf16)
        douts = dout_halo_ref[:, at]
        queries = jnp.where(
            is_lse, douts.astype(f32), q_halo_ref[:, at].astype(f32)
        ).astype(bf16)
        prob = jnp.exp(dot_last(keys, queries))
        dprob = dot_last(v_ref[:, at], douts)
        dscore = (prob * dprob).astype(bf16)
        dk = dk_ref[:, at] + dot(dscore, queries)
        dv = dv_ref[:, at] + dot(prob.astype(bf16), douts)
        dk = jnp.where(lane < NA_DIM, dk, 0.0).astype(bf16)
        dv = jnp.where(lane < NA_DIM, dv, 0.0).astype(bf16)
        dxn += dot_last(dk, w_ref[:, head_lanes(NA_HEADS + h)])
        dxn += dot_last(dv, w_ref[:, head_lanes(2 * NA_HEADS + h)])
    grad = (dy_ref[...].astype(f32) + rms_back(x, rms_stat(x), dxn)).astype(bf16)
    grad_out[...] = dot(perm_back_ref[...], grad).astype(bf16)


def per_device(image, na_qkv, na_out, merge_one, merge_two, attn_qkv, attn_out, cotangent):
    rows, cols, _ = image.shape
    n_row = lax.axis_size("row")
    n_col = lax.axis_size("col")
    own = rows * cols
    tokens = own // 16
    dim = C2 // GHEADS
    owned = n_row * tokens
    scale = 1.0 / math.sqrt(dim)
    tables = token_tables(rows, cols)
    perm = jnp.asarray(tables["perm"], bf16)
    perm_back = jnp.asarray(tables["perm"].T, bf16)
    select = jnp.asarray(tables["select"], bf16)
    hot = jnp.asarray(tables["hot"], bf16)
    band_own = jnp.asarray(tables["band_own"], bf16)
    halo = tables["halo"]
    padded = halo.shape[0]

    flat = image.reshape(own, C0)
    x_halo = halo_of(
        image[:REACH].reshape(-1, C0),
        image[-REACH:].reshape(-1, C0),
        image[:, :REACH].reshape(-1, C0),
        image[:, -REACH:].reshape(-1, C0),
        cols,
        padded,
    )
    at_row = lax.axis_index("row") * rows + jnp.asarray(halo[:, 0], jnp.int32)
    at_col = lax.axis_index("col") * cols + jnp.asarray(halo[:, 1], jnp.int32)
    inside = (at_row >= 0) & (at_row < rows * n_row) & (at_col >= 0) & (at_col < cols * n_col)
    lane = jnp.arange(LANES)
    mask_lane = (lane >= NA_DIM) & (lane < NA_DIM + rows + cols)
    band_halo = jnp.where(
        ~inside[:, None] & mask_lane[None], MASKED, jnp.asarray(tables["band_halo"], f32)
    ).astype(bf16)

    na_scale = np.ones((1, 3 * NA_HEADS, 1), np.float32)
    na_scale[:, :NA_HEADS] = 1.0 / math.sqrt(NA_DIM)
    w_wide = jnp.pad(
        (na_qkv.reshape(C0, 3 * NA_HEADS, NA_DIM) * jnp.asarray(na_scale, bf16)),
        ((0, 0), (0, 0), (0, LANES - NA_DIM)),
    ).reshape(C0, 3 * WIDE)
    w_out_wide = jnp.pad(
        na_out.reshape(NA_HEADS, NA_DIM, C0), ((0, 0), (0, LANES - NA_DIM), (0, 0))
    ).reshape(WIDE, C0)

    grad = cotangent.reshape(tokens, C2)
    grad_row = all_to_all(jnp.broadcast_to(grad[None], (n_row, tokens, C2)), "row").reshape(owned, C2)
    own_out = lax.dynamic_slice_in_dim(attn_out, lax.axis_index("row") * dim, dim, 0)
    dout = dot_last(grad_row, own_out).astype(bf16)
    all_dout = lax.all_gather(dout, "col", axis=0)

    qkv, m2, q0, k0, v0, q0_halo, a0 = call(
        na_forward_kernel,
        [
            ((GHEADS, tokens, 3 * dim), bf16),
            ((tokens, C2), bf16),
            ((own, WIDE), bf16),
            ((own + padded, WIDE), bf16),
            ((own + padded, WIDE), bf16),
            ((padded, WIDE), bf16),
            ((own, WIDE), bf16),
        ],
        (flat, x_halo, perm, hot, band_own, band_halo, w_wide, w_out_wide, merge_one, merge_two, attn_qkv),
        scratch=(
            pltpu.VMEM(merge_one.shape, bf16),
            pltpu.VMEM(merge_two.shape, bf16),
            pltpu.VMEM(attn_qkv.shape, bf16),
            pltpu.SemaphoreType.DMA((3,)),
        ),
        manual=3,
    )

    mine = all_to_all(qkv, "row").reshape(owned, 3 * dim)
    query = mine[:, :dim]
    every = gather_columns(mine)
    all_query = every[:, :dim]
    keyval = every[:, dim:]
    out_heads, stat_col, stat_row = call(
        functools.partial(attention_kernel, scale),
        [((owned, dim), bf16), ((owned, LANES), f32), ((8, owned), f32)],
        (query, dout, keyval),
    )
    all_stats = gather_columns(stat_row[None])
    dq, partial = call(
        functools.partial(query_grad_kernel, scale),
        [((owned, dim), bf16), ((dim, C2), bf16)],
        (query, dout, keyval, out_heads, stat_col, grad_row),
    )
    dqkv = call(
        functools.partial(key_grad_kernel, scale),
        [((owned, 3 * dim), bf16)],
        (column_order(), mine, all_query, all_dout, all_stats, dq),
        scratch=(pltpu.VMEM((n_col * owned, dim), bf16), pltpu.VMEM((8, n_col * owned), f32)),
        smem=1,
    )[0]
    dqkv = all_to_all(dqkv.reshape(n_row, tokens, 3 * dim), "row")

    out_tok = all_to_all(out_heads.reshape(n_row, tokens, dim), "row")
    out_tok = out_tok.transpose(1, 0, 2).reshape(tokens, C2)
    merged = (m2.astype(f32) + dot(out_tok, attn_out)).astype(bf16)
    partial = all_to_all(partial.reshape(n_col, dim // n_col, C2), "col")
    grad_wo = jnp.sum(partial.astype(f32), 0)

    dout0, dy0, strips = call(
        merge_back_kernel,
        [((own, WIDE), bf16), ((own, C0), bf16), ((select.shape[0], WIDE), bf16)],
        (dqkv, m2, grad, a0, q0, select, w_out_wide, attn_qkv, merge_two, merge_one),
        scratch=(
            pltpu.VMEM(attn_qkv.shape, bf16),
            pltpu.VMEM(merge_two.shape, bf16),
            pltpu.VMEM(merge_one.shape, bf16),
            pltpu.SemaphoreType.DMA((3,)),
        ),
        manual=3,
    )
    side = REACH * cols
    edge = 2 * side + REACH * rows
    dout0_halo = halo_of(
        strips[:side], strips[side : 2 * side], strips[2 * side : edge], strips[edge:], cols, padded
    )
    dq0, dk0, dv0 = call(
        na_own_kernel,
        [((own, WIDE), bf16), ((own, WIDE), f32), ((own, WIDE), f32)],
        (q0, k0, v0, dout0),
    )
    grad_image = call(
        na_beside_kernel,
        [((own, C0), bf16)],
        (flat, perm, perm_back, w_wide, hot, k0[:own], v0[:own], q0_halo, dout0_halo, dy0, dq0, dk0, dv0),
    )[0]
    return (
        merged.reshape(rows // 4, cols // 4, C2),
        grad_image.reshape(rows, cols, C0),
        grad_wo,
    )


def solution(mesh):
    return jax.shard_map(
        per_device,
        mesh=mesh,
        in_specs=(P("row", "col", None), P(), P(), P(), P(), P(), P(), P("row", "col", None)),
        out_specs=(P("row", "col", None), P("row", "col", None), P(("row", "col"), None)),
        check_vma=False,
    )
```

```python
import functools
import math

import jax
import jax.numpy as jnp
import numpy as np
from jax import lax
from jax.experimental import pallas as pl
from jax.experimental.pallas import tpu as pltpu
from jax.sharding import PartitionSpec as P

C0 = 256
C1 = 512
C2 = 1024
NA_HEADS = 4
GHEADS = 8
KERNEL = 7
REACH = KERNEL // 2
EPSILON = 1e-06
LANES = 128
NA_DIM = C0 // NA_HEADS
WIDE = NA_HEADS * LANES
MASKED = -1e15
ROWS = 16
DELTA_LANE = 112
LSE_LANE = 114

f32 = jnp.float32
bf16 = jnp.bfloat16


def dot(left, right):
    return lax.dot_general(left, right, (((1,), (0,)), ((), ())), preferred_element_type=f32)


def dot_last(left, right):
    return lax.dot_general(left, right, (((1,), (1,)), ((), ())), preferred_element_type=f32)


def dot_first(left, right):
    return lax.dot_general(left, right, (((0,), (0,)), ((), ())), preferred_element_type=f32)


def rms_stat(x):
    return lax.rsqrt(jnp.mean(x * x, -1, keepdims=True) + EPSILON)


def rms_back(x, scale, grad):
    return scale * grad - x * scale**3 * jnp.mean(grad * x, -1, keepdims=True)


def token_tables(rows, cols):
    grid = np.arange(rows * cols).reshape(rows // 4, 2, 2, cols // 4, 2, 2)
    order = grid.transpose(2, 5, 1, 4, 0, 3).reshape(-1)
    own_row, own_col = order // cols, order % cols
    outside = [(-99, -99)]
    side = [
        ((r0, r1), pad)
        for (r0, r1), pad in [((-REACH, 0), True), ((0, rows), False), ((rows, rows + REACH), True)]
    ]
    halo = [(r, c) for r in range(-REACH, 0) for c in range(cols)]
    halo += [(r, c) for r in range(rows, rows + REACH) for c in range(cols)]
    for first in (-REACH, cols):
        for (r0, r1), pad in side:
            part = [(r, c) for r in range(r0, r1) for c in range(first, first + REACH)]
            halo += part + outside * (-len(part) % ROWS)
    count = len(halo)
    padded = -(-count // LANES) * LANES
    halo = np.array(halo + outside * (padded - count))

    def band(row, col):
        near_row = np.abs(row[:, None] - np.arange(rows)[None]) <= REACH
        near_col = np.abs(col[:, None] - np.arange(cols)[None]) <= REACH
        return np.where(np.concatenate([near_row, near_col], 1), 0.0, MASKED)

    def lanes(part):
        table = np.zeros((part.shape[0], LANES), np.float32)
        table[:, NA_DIM : NA_DIM + part.shape[1]] = part
        return table

    hot = np.concatenate(
        [own_row[:, None] == np.arange(rows)[None], own_col[:, None] == np.arange(cols)[None]], 1
    ).astype(np.float32)
    perm = np.zeros((rows * cols, rows * cols), np.float32)
    perm[np.arange(rows * cols), order] = 1.0
    place = np.argsort(order)
    natural = np.arange(rows * cols).reshape(rows, cols)
    strips = [natural[:REACH], natural[-REACH:], natural[:, :REACH], natural[:, -REACH:]]
    wanted = place[np.concatenate([s.reshape(-1) for s in strips])]
    select = np.zeros((wanted.size, rows * cols), np.float32)
    select[np.arange(wanted.size), wanted] = 1.0
    corner = np.zeros((2 * ROWS, REACH * cols), np.float32)
    for i, first in enumerate((0, cols - REACH)):
        for r in range(REACH):
            for c in range(REACH):
                corner[i * ROWS + r * REACH + c, r * cols + first + c] = 1.0
    return dict(
        corner=corner,
        perm=perm,
        select=select,
        hot=lanes(hot),
        band_own=lanes(band(own_row, own_col)),
        band_halo=lanes(band(halo[:, 0], halo[:, 1])),
        halo=halo,
        count=count,
    )


def shifted(array, axis, move):
    count = lax.axis_size(axis)
    return lax.ppermute(array, axis, [(i, move(i)) for i in range(count)])


def neighbours(to_next, to_previous, axis):
    count = lax.axis_size(axis)
    up = [(i, i + 1) for i in range(count - 1)]
    down = [(j, i) for i, j in up]
    return lax.ppermute(to_next, axis, up), lax.ppermute(to_previous, axis, down)


def row_halo(top, bottom):
    return neighbours(bottom, top, "row")


def along_z(pair):
    count = lax.axis_size("col")
    return [pair] + [shifted(pair, "col", lambda i: (i + 4 * step) % count) for step in (1, 3, 2)]


def other_core(pieces):
    return [shifted(piece, "col", lambda i: i ^ 1) for piece in pieces]


def to_heads(array):
    n_row, n_col = lax.axis_size("row"), lax.axis_size("col")
    groups = [
        [r * n_col + c + across for across in (0, 2) for r in range(n_row)]
        for c in range(n_col)
        if not c & 2
    ]
    return lax.all_to_all(
        array, ("row", "col"), split_axis=0, concat_axis=0, axis_index_groups=groups, tiled=True
    )


def column_order():
    count = lax.axis_size("col")
    me = lax.axis_index("col")
    place = jnp.arange(count, dtype=jnp.int32)
    step = jnp.asarray([0, 1, 3, 2], jnp.int32)[(place // 2) % 4]
    source = (me + count - 4 * step) % count
    source = (source & ~2) | (2 * (place % 2))
    return jnp.concatenate([source ^ (place // 8), ((me // 2) % 2).reshape(1).astype(jnp.int32)])


def all_to_all(array, axis):
    return lax.all_to_all(array, axis, split_axis=0, concat_axis=0, tiled=True)


class Rows:
    def __init__(self, array, rows):
        self.array, self.rows = array, rows
        self.shape, self.dtype = (rows, *array.shape[1:]), array.dtype


class Held:
    def __init__(self, source, target, sems, cut):
        dim, count = cut
        size = target.shape[dim] // count
        self.copies = []
        self.parts = []
        for i in range(count):
            at = tuple(pl.ds(i * size, size) if d == dim else slice(None) for d in range(dim + 1))
            part = target.at[at] if count > 1 else target
            self.copies.append(
                pltpu.make_async_copy(source.at[at] if count > 1 else source, part, sems[i])
            )
            self.parts.append(part)
        self.target = target
        self.waiting = [True] * count
        for copy in self.copies:
            copy.start()

    def chunk(self, i):
        if self.waiting[i]:
            self.waiting[i] = False
            self.copies[i].wait()
        return self.parts[i]

    def ready(self):
        for i in range(len(self.copies)):
            self.chunk(i)
        return self.target

    def __getitem__(self, index):
        return self.ready()[index]

    @property
    def shape(self):
        return self.target.shape


class Plain:
    def __init__(self, target):
        self.target = target

    def ready(self):
        return self.target

    def send(self):
        pass

    def __getitem__(self, index):
        return self.target[index]

    def __setitem__(self, index, value):
        self.target[index] = value

    @property
    def shape(self):
        return self.target.shape


class Result(Plain):
    def __init__(self, source, target, sem):
        self.copy = pltpu.make_async_copy(source, target, sem)
        self.target = source
        self.started = False

    def send(self):
        if not self.started:
            self.started = True
            self.copy.start()


def take_from(items, count):
    return [items.pop(0) for _ in range(count)]


def call(kernel, outs, args, manual=(), out_manual=(), scratch=(), smem=0, cuts={}, megabytes=16):
    manual = sorted(i % len(args) for i in manual)
    out_manual = sorted(i % len(outs) for i in out_manual)
    cuts = {i % len(args): cut for i, cut in cuts.items()}
    cuts = [cuts.get(i, (0, 1)) for i in manual]
    total = sum(n for _, n in cuts)

    def body(*refs):
        refs = list(refs)
        take = functools.partial(take_from, refs)
        given, results, extra = take(len(args)), take(len(outs)), take(len(scratch))
        here, there = take(len(manual)), take(len(out_manual))
        sems_in, sems_out = take(2)
        sems = [sems_in.at[i] for i in range(total)]
        values = given[:smem] + [Plain(ref) for ref in given[smem:]]
        writes = [Plain(ref) for ref in results]
        for i, dst, cut in zip(manual, here, cuts):
            source = given[i].at[pl.ds(0, args[i].rows)] if isinstance(args[i], Rows) else given[i]
            values[i] = Held(source, dst, take_from(sems, cut[1]), cut)
        for n, (i, src) in enumerate(zip(out_manual, there)):
            writes[i] = Result(src, results[i], sems_out.at[n])
        kernel(*values, *writes, *extra)
        for i in out_manual:
            writes[i].send()
        for i in manual:
            values[i].ready()
        for i in out_manual:
            writes[i].copy.wait()

    def spec(i, far):
        return pl.BlockSpec(memory_space=pltpu.HBM if i in far else pltpu.VMEM)

    hbm = lambda a: pltpu.with_memory_space_constraint(a, pltpu.HBM)
    return pl.pallas_call(
        body,
        out_shape=[
            pltpu.HBM(*out) if i in out_manual else jax.ShapeDtypeStruct(*out)
            for i, out in enumerate(outs)
        ],
        in_specs=[pl.BlockSpec(memory_space=pltpu.SMEM)] * smem
        + [spec(i, manual) for i in range(smem, len(args))],
        out_specs=[spec(i, out_manual) for i in range(len(outs))],
        scratch_shapes=list(scratch)
        + [pltpu.VMEM(args[i].shape, args[i].dtype) for i in manual]
        + [pltpu.VMEM(*outs[i]) for i in out_manual]
        + [pltpu.SemaphoreType.DMA((max(total, 1),)), pltpu.SemaphoreType.DMA((max(len(out_manual), 1),))],
        compiler_params=pltpu.CompilerParams(vmem_limit_bytes=megabytes * 2**20),
    )(*[hbm(getattr(a, "array", a)) if i in manual else a for i, a in enumerate(args)])


def head_lanes(head):
    return slice(head * LANES, (head + 1) * LANES)


def two_parts(value):
    high = value.astype(bf16).astype(f32)
    return high, value - high


def at_lanes(base, lane, first, value):
    high, low = two_parts(value)
    return jnp.where(lane == first, -high, jnp.where(lane == first + 1, -low, base))


def fill_halo(target, parts):
    first = 0
    for part in parts:
        rows = part.shape[0]
        target[first : first + rows, :] = part[...]
        first += rows
    rest = target.shape[0] - first
    target[first:, :] = jnp.zeros((rest, target.shape[1]), target.dtype)


def corner_kernel(corner_ref, before_ref, after_ref, left_ref, right_ref, left_out, right_out):
    for i, (side, out) in enumerate([(left_ref, left_out), (right_ref, right_out)]):
        pick = corner_ref[i * ROWS : (i + 1) * ROWS]
        rows = side.shape[0]
        out[:ROWS] = dot(pick, before_ref[...]).astype(bf16)
        out[ROWS : ROWS + rows] = side[...]
        out[ROWS + rows :] = dot(pick, after_ref[...]).astype(bf16)


def na_forward_kernel(
    x_ref,
    perm_ref,
    w_ref,
    before_ref,
    after_ref,
    left_ref,
    right_ref,
    hot_ref,
    band_own_ref,
    band_halo_ref,
    w_out_ref,
    one_ref,
    two_ref,
    wqkv_ref,
    qkv_out,
    m2_out,
    q_out,
    k_out,
    v_out,
    q_halo_out,
    a0_out,
    halo_ref,
):
    own = x_ref.shape[0]
    x = dot(perm_ref[...], x_ref[...])
    xn = (x * rms_stat(x)).astype(bf16)
    fill_halo(halo_ref, [before_ref, after_ref, left_ref, right_ref])
    xh = halo_ref[...].astype(f32)
    xhn = (xh * rms_stat(xh)).astype(bf16)
    mine = dot(xn, w_ref[...])
    beside = dot(xhn, w_ref[...])
    lane = lax.broadcasted_iota(jnp.int32, (1, LANES), 1)
    is_lse = (lane == LSE_LANE) | (lane == LSE_LANE + 1)
    is_delta = (lane == DELTA_LANE) | (lane == DELTA_LANE + 1)
    one_lse = jnp.where(is_lse, 1.0, 0.0)
    one_delta = jnp.where(is_delta, 1.0, 0.0)
    hot = hot_ref[...].astype(f32)
    band_own = band_own_ref[...].astype(f32)
    band_halo = band_halo_ref[...].astype(f32)
    for h in range(NA_HEADS):
        at = head_lanes(h)
        kat = head_lanes(NA_HEADS + h)
        vat = head_lanes(2 * NA_HEADS + h)
        q = mine[:, at] + hot
        k_out[:own, at] = (mine[:, kat] + (band_own + one_lse)).astype(bf16)
        k_out[own:, at] = (beside[:, kat] + (band_halo + one_lse)).astype(bf16)
        v_out[:own, at] = (mine[:, vat] + one_delta).astype(bf16)
        v_out[own:, at] = (beside[:, vat] + one_delta).astype(bf16)
        q_halo_out[:, at] = (beside[:, at] + band_halo).astype(bf16)
        score = dot_last(q.astype(bf16), k_out[:, at])
        top = jnp.max(score, -1, keepdims=True)
        weight = jnp.exp(score - top).astype(bf16)
        out = dot(weight, v_out[:, at])
        norm = out[:, DELTA_LANE : DELTA_LANE + 1]
        q_out[:, at] = at_lanes(q, lane, LSE_LANE, top + jnp.log(norm)).astype(bf16)
        a0 = jnp.where(lane < NA_DIM, out / norm, 0.0).astype(bf16)
        a0_out[:, at] = a0
    for result in (q_out, k_out, v_out, q_halo_out, a0_out):
        result.send()
    y = (x + dot(a0_out[...], w_out_ref[...])).astype(bf16)
    quarter = own // 4
    m1 = dot(y[:quarter], one_ref[:C0])
    for part in range(1, 4):
        m1 += dot(y[part * quarter : (part + 1) * quarter], one_ref[part * C0 : (part + 1) * C0])
    m1 = m1.astype(bf16)
    tokens = own // 16
    m2 = dot(m1[:tokens], two_ref[:C1])
    for part in range(1, 4):
        m2 += dot(m1[part * tokens : (part + 1) * tokens], two_ref[part * C1 : (part + 1) * C1])
    m2 = m2.astype(bf16)
    m2_out[...] = m2
    m2f = m2.astype(f32)
    mn = (m2f * rms_stat(m2f)).astype(bf16)
    qkv = dot(mn, wqkv_ref[...]).astype(bf16)
    dim = C2 // GHEADS
    for h in range(GHEADS):
        for part in range(3):
            first = part * C2 + h * dim
            for copy in range(2):
                qkv_out[copy, h, :, part * dim : (part + 1) * dim] = qkv[:, first : first + dim]


def own_rows(order_ref, pair_ref, owned):
    first = pl.multiple_of(order_ref[order_ref.shape[0] - 1] * owned, owned)
    return pair_ref.ready().at[pl.ds(first, owned)]


def attention_kernel(scale, order_ref, dout_ref, grad_ref, *refs):
    pieces, (out_ref, col_ref, send_ref) = refs[:-3], refs[-3:]
    dim = dout_ref.shape[1]
    query = own_rows(order_ref, pieces[0], dout_ref.shape[0])[:, :dim]
    scores = [dot_last(query, piece[:, dim : 2 * dim]) * scale for piece in pieces]
    top = functools.reduce(jnp.maximum, [jnp.max(s, -1, keepdims=True) for s in scores])
    norm, out = 0.0, 0.0
    for score, piece in zip(scores, pieces):
        weight = jnp.exp(score - top)
        norm += jnp.sum(weight, -1, keepdims=True)
        out += dot(weight.astype(bf16), piece[:, 2 * dim :])
    out = (out / norm).astype(bf16)
    out_ref[...] = out
    lse = top + jnp.log(norm)
    delta = jnp.sum(dout_ref[...].astype(f32) * out.astype(f32), -1, keepdims=True)
    lane = lax.broadcasted_iota(jnp.int32, (1, LANES), 1)
    col_ref[...] = jnp.where(lane == 0, lse, jnp.where(lane == 1, delta, 0.0))
    parts = [*two_parts(lse), *two_parts(delta)]
    table = jnp.zeros((query.shape[0], LANES), f32)
    for i, part in enumerate(parts):
        table = jnp.where(lane == i, part, table)
    table = table.T
    halves = query.shape[0] // LANES
    stats = [
        table[i : i + 1, half * LANES : (half + 1) * LANES]
        for i in range(len(parts))
        for half in range(halves)
    ]
    stats = jnp.concatenate(stats, 0).astype(bf16)
    partial = dot_first(out, grad_ref[...])
    count, rows = send_ref.shape[0], send_ref.shape[1]
    for i in range(count):
        send_ref[i, :, :C2] = partial[i * rows : (i + 1) * rows].astype(bf16)
        send_ref[i, :, C2:] = stats


def query_grad_kernel(scale, order_ref, dout_ref, col_ref, *refs):
    pieces, dq_ref = refs[:-1], refs[-1]
    dim = dout_ref.shape[1]
    query = own_rows(order_ref, pieces[0], dout_ref.shape[0])[:, :dim]
    dout = dout_ref[...]
    lse, delta = col_ref[:, 0:1], col_ref[:, 1:2]
    total = 0.0
    for piece in pieces:
        keys = piece[:, dim : 2 * dim]
        prob = jnp.exp(dot_last(query, keys) * scale - lse)
        dprob = dot_last(dout, piece[:, 2 * dim :])
        total += dot((prob * (dprob - delta)).astype(bf16), keys)
    dq_ref[...] = (total * scale).astype(bf16)


def key_grad_kernel(scale, order_ref, dout_ref, stat_ref, dq_ref, heads_ref, *refs):
    pieces, (out_ref, dout_in, lse_in, delta_in) = refs[:-4], refs[-4:]
    owned, dim = dq_ref.shape
    halves = owned // LANES
    own = own_rows(order_ref, pieces[0], owned)
    keys, values = own[:, dim : 2 * dim], own[:, 2 * dim :]
    stat_ref = stat_ref.ready()
    dk, dv = 0.0, 0.0
    for i, piece in enumerate(pieces):
        queries = piece[:, :dim]
        score = dot_last(keys, queries) * scale
        for j in range(2):
            source = order_ref[2 * i + j]
            dout_in[j * owned : (j + 1) * owned, :] = dout_ref[source]
            stats = stat_ref[source].astype(f32)
            for half in range(halves):
                at = slice(j * owned + half * LANES, j * owned + (half + 1) * LANES)
                take = lambda n: stats[n * halves + half : n * halves + half + 1]
                lse_in[:, at] = take(0) + take(1)
                delta_in[:, at] = take(2) + take(3)
        douts = dout_in[...]
        prob = jnp.exp(score - lse_in[...])
        dprob = dot_last(values, douts)
        dk += dot((prob * (dprob - delta_in[...])).astype(bf16), queries)
        dv += dot(prob.astype(bf16), douts)
    out_ref[:, :dim] = dq_ref[...]
    out_ref[:, dim : 2 * dim] = (dk * scale).astype(bf16)
    out_ref[:, 2 * dim : 3 * dim] = dv.astype(bf16)
    out_ref[:, 3 * dim :] = heads_ref[...]


def merge_back_kernel(
    dqkv_ref,
    wqkv_ref,
    m2_ref,
    grad_ref,
    two_ref,
    one_ref,
    w_out_ref,
    a0_ref,
    q_ref,
    select_ref,
    dout_out,
    dy_out,
    *strip_outs,
):
    dim = C2 // GHEADS
    dmn = 0.0
    for part in range(3):
        at = slice(part * dim, (part + 1) * dim)
        grads = jnp.concatenate([dqkv_ref[h, :, at] for h in range(GHEADS)], 1)
        dmn += dot_last(grads, wqkv_ref.chunk(part)[...])
    m2 = m2_ref[...].astype(f32)
    dm2 = (grad_ref[...].astype(f32) + rms_back(m2, rms_stat(m2), dmn)).astype(bf16)
    dm1 = [dot_last(dm2, two_ref.chunk(part)[...]).astype(bf16) for part in range(4)]
    du1 = dot_last(jnp.concatenate(dm1, 0), one_ref[...]).astype(bf16)
    dy = jnp.concatenate([du1[:, part * C0 : (part + 1) * C0] for part in range(4)], 0)
    dy_out[...] = dy
    da0 = dot_last(dy, w_out_ref[...]).astype(bf16).astype(f32)
    lane = lax.broadcasted_iota(jnp.int32, (1, LANES), 1)
    is_lse = (lane == LSE_LANE) | (lane == LSE_LANE + 1)
    for h in range(NA_HEADS):
        at = head_lanes(h)
        mine = da0[:, at]
        delta = jnp.sum(mine * a0_ref[:, at].astype(f32), -1, keepdims=True)
        mine = jnp.where(is_lse, q_ref[:, at].astype(f32), mine)
        dout_out[:, at] = at_lanes(mine, lane, DELTA_LANE, delta).astype(bf16)
    dout_out.send()
    strips = dot(select_ref[...], dout_out[...]).astype(bf16)
    first = 0
    for out in strip_outs:
        out[...] = strips[first : first + out.shape[0]]
        first += out.shape[0]


def own_channels(value):
    lane = lax.broadcasted_iota(jnp.int32, (1, LANES), 1)
    return jnp.where(lane < NA_DIM, value, 0.0).astype(bf16)


def through_projection(grads, first, w_ref):
    at = slice(first * LANES, (first + len(grads)) * LANES)
    return dot_last(jnp.concatenate(grads, 1), w_ref[:, at])


def na_own_kernel(heads, q_ref, k_ref, dout_ref, v_ref, w_ref, dxn_out):
    own = dout_ref.shape[0]
    dq, dk, dv = [], [], []
    for h in heads:
        at = head_lanes(h)
        prob = jnp.exp(dot_last(q_ref[:, at], k_ref[:, at]))
        dprob = dot_last(dout_ref[:, at], v_ref[:, at])
        dscore = (prob * dprob).astype(bf16)
        dq.append(own_channels(dot(dscore, k_ref[:, at])))
        dk.append(own_channels(dot_first(dscore[:, :own], q_ref[:, at])))
        dv.append(own_channels(dot_first(prob[:, :own].astype(bf16), dout_ref[:, at])))
    dxn = through_projection(dq, heads[0], w_ref)
    dxn += through_projection(dk, NA_HEADS + heads[0], w_ref)
    dxn_out[...] = dxn + through_projection(dv, 2 * NA_HEADS + heads[0], w_ref)


def na_rest_kernel(
    heads,
    q_ref,
    k_ref,
    dout_ref,
    v_ref,
    w_ref,
    heads_ref,
    wo_ref,
    m2_ref,
    part_ref,
    dxn_out,
    merged_out,
    grad_out,
):
    na_own_kernel(heads, q_ref, k_ref, dout_ref, v_ref, w_ref, dxn_out)
    merged = m2_ref[...].astype(f32)
    dim = C2 // GHEADS
    for h in range(GHEADS):
        merged += dot(heads_ref[h, :, 3 * dim :], wo_ref[h * dim : (h + 1) * dim])
    merged_out[...] = merged.astype(bf16)
    grad_out[...] = jnp.sum(part_ref[:, :, :C2].astype(f32), 0)


def na_beside_kernel(
    k_ref,
    v_ref,
    hot_ref,
    before_ref,
    after_ref,
    left_ref,
    right_ref,
    q_halo_ref,
    w_ref,
    x_ref,
    perm_ref,
    dxn_one,
    dxn_two,
    dy_ref,
    perm_back_ref,
    grad_out,
    dout_halo_ref,
):
    lane = lax.broadcasted_iota(jnp.int32, (1, LANES), 1)
    is_mask = (lane >= NA_DIM) & (lane < DELTA_LANE)
    is_lse = (lane == LSE_LANE) | (lane == LSE_LANE + 1)
    fill_halo(dout_halo_ref, [before_ref, after_ref, left_ref, right_ref])
    hot = hot_ref[...].astype(f32)
    dk, dv = [], []
    for h in range(NA_HEADS):
        at = head_lanes(h)
        keys = jnp.where(is_mask, hot, k_ref.chunk(0)[:, at].astype(f32)).astype(bf16)
        douts = dout_halo_ref[:, at]
        queries = jnp.where(
            is_lse, douts.astype(f32), q_halo_ref[:, at].astype(f32)
        ).astype(bf16)
        prob = jnp.exp(dot_last(keys, queries))
        dprob = dot_last(v_ref.chunk(0)[:, at], douts)
        dk.append(own_channels(dot((prob * dprob).astype(bf16), queries)))
        dv.append(own_channels(dot(prob.astype(bf16), douts)))
    dxn = dxn_one[...] + dxn_two[...] + through_projection(dk, NA_HEADS, w_ref)
    dxn += through_projection(dv, 2 * NA_HEADS, w_ref)
    x = dot(perm_ref[...], x_ref[...])
    grad = (dy_ref[...].astype(f32) + rms_back(x, rms_stat(x), dxn)).astype(bf16)
    grad_out[...] = dot(perm_back_ref[...], grad).astype(bf16)


def per_device(image, na_qkv, na_out, merge_one, merge_two, attn_qkv, attn_out, cotangent):
    rows, cols, _ = image.shape
    n_row = lax.axis_size("row")
    n_col = lax.axis_size("col")
    own = rows * cols
    tokens = own // 16
    dim = C2 // GHEADS
    owned = n_row * tokens
    scale = 1.0 / math.sqrt(dim)
    tables = token_tables(rows, cols)
    perm = jnp.asarray(tables["perm"], bf16)
    perm_back = jnp.asarray(tables["perm"].T, bf16)
    select = jnp.asarray(tables["select"], bf16)
    hot = jnp.asarray(tables["hot"], bf16)
    corner = jnp.asarray(tables["corner"], bf16)
    band_own = jnp.asarray(tables["band_own"], bf16)
    halo = tables["halo"]
    padded = halo.shape[0]

    flat = image.reshape(own, C0)
    before, after = row_halo(image[:REACH].reshape(-1, C0), image[-REACH:].reshape(-1, C0))
    left, right = call(
        corner_kernel,
        [((REACH * rows + 2 * ROWS, C0), bf16)] * 2,
        (
            corner,
            before,
            after,
            image[:, :REACH].reshape(-1, C0),
            image[:, -REACH:].reshape(-1, C0),
        ),
        megabytes=8,
    )
    left, right = neighbours(right, left, "col")
    at_row = lax.axis_index("row") * rows + jnp.asarray(halo[:, 0], jnp.int32)
    at_col = lax.axis_index("col") * cols + jnp.asarray(halo[:, 1], jnp.int32)
    inside = (at_row >= 0) & (at_row < rows * n_row) & (at_col >= 0) & (at_col < cols * n_col)
    lane = jnp.arange(LANES)
    mask_lane = (lane >= NA_DIM) & (lane < NA_DIM + rows + cols)
    band_halo = jnp.where(
        ~inside[:, None] & mask_lane[None], MASKED, jnp.asarray(tables["band_halo"], f32)
    ).astype(bf16)

    grad = cotangent.reshape(tokens, C2)
    band_halo, grad = lax.optimization_barrier((band_halo, grad))
    grad_row = all_to_all(jnp.broadcast_to(grad[None], (n_row, tokens, C2)), "row").reshape(owned, C2)
    own_out = lax.dynamic_slice_in_dim(attn_out, lax.axis_index("row") * dim, dim, 0)

    na_scale = np.ones((1, 3 * NA_HEADS, 1), np.float32)
    na_scale[:, :NA_HEADS] = 1.0 / math.sqrt(NA_DIM)
    w_wide = jnp.pad(
        (na_qkv.reshape(C0, 3 * NA_HEADS, NA_DIM) * jnp.asarray(na_scale, bf16)),
        ((0, 0), (0, 0), (0, LANES - NA_DIM)),
    ).reshape(C0, 3 * WIDE)
    w_out_wide = jnp.pad(
        na_out.reshape(NA_HEADS, NA_DIM, C0), ((0, 0), (0, LANES - NA_DIM), (0, 0))
    ).reshape(WIDE, C0)

    qkv, m2, q0, k0, v0, q0_halo, a0 = call(
        na_forward_kernel,
        [
            ((2, GHEADS, tokens, 3 * dim), bf16),
            ((tokens, C2), bf16),
            ((own, WIDE), bf16),
            ((own + padded, WIDE), bf16),
            ((own + padded, WIDE), bf16),
            ((padded, WIDE), bf16),
            ((own, WIDE), bf16),
        ],
        (
            flat,
            perm,
            w_wide,
            before,
            after,
            left,
            right,
            hot,
            band_own,
            band_halo,
            w_out_wide,
            merge_one,
            merge_two,
            attn_qkv,
        ),
        manual=(0, 1, 2, 7, 8, 9, 10, 11, 12, 13),
        out_manual=(1, 2, 3, 4, 5, 6),
        scratch=(pltpu.VMEM((padded, C0), bf16),),
        megabytes=40,
    )

    qkv, grad_row = lax.optimization_barrier((qkv, grad_row))
    dout = dot_last(grad_row, own_out).astype(bf16)
    all_dout = lax.all_gather(dout, "col", axis=0)
    order = column_order()
    pair = to_heads(qkv.reshape(2 * GHEADS, tokens, 3 * dim)).reshape(2 * owned, 3 * dim)
    pieces = along_z(pair)
    pieces += other_core(pieces)
    out_heads, stats, send = call(
        functools.partial(attention_kernel, scale),
        [((owned, dim), bf16), ((owned, LANES), f32), ((n_col, dim // n_col, C2 + LANES), bf16)],
        (order, dout, grad_row, *pieces),
        smem=1,
    )
    shares = all_to_all(send, "col")
    dq = call(
        functools.partial(query_grad_kernel, scale),
        [((owned, dim), bf16)],
        (order, dout, stats, *pieces),
        smem=1,
    )[0]
    two = 2 * owned
    back = call(
        functools.partial(key_grad_kernel, scale),
        [((owned, 4 * dim), bf16)],
        (order, all_dout, shares[:, :, C2:], dq, out_heads, *pieces),
        manual=(1,),
        scratch=(pltpu.VMEM((two, dim), bf16), pltpu.VMEM((1, two), f32), pltpu.VMEM((1, two), f32)),
        smem=1,
    )[0]
    back = all_to_all(back.reshape(n_row, tokens, 4 * dim), "row")

    dout0, dy0, top, bottom, left, right = call(
        merge_back_kernel,
        [((own, WIDE), bf16), ((own, C0), bf16)]
        + [((REACH * n, WIDE), bf16) for n in (cols, cols, rows, rows)],
        (back, attn_qkv, m2, grad, merge_two, merge_one, w_out_wide, a0, q0, select),
        manual=range(1, 10),
        out_manual=(1,),
        cuts={1: (1, 3), 4: (0, 4)},
        megabytes=32,
    )
    before, after = row_halo(top, bottom)
    half = NA_HEADS // 2
    dxn_one = call(
        functools.partial(na_own_kernel, range(half)),
        [((own, C0), f32)],
        (q0, k0, dout0, v0, w_wide),
        manual=(0, 1, 3, 4),
    )[0]
    before, after, dxn_one = lax.optimization_barrier((before, after, dxn_one))
    left, right = call(
        corner_kernel,
        [((left.shape[0] + 2 * ROWS, WIDE), bf16)] * 2,
        (corner, before, after, left, right),
        megabytes=8,
    )
    left, right, q0 = lax.optimization_barrier((left, right, q0))
    left, right = neighbours(right, left, "col")
    dxn_two, merged, grad_wo = call(
        functools.partial(na_rest_kernel, range(half, NA_HEADS)),
        [((own, C0), f32), ((tokens, C2), bf16), ((dim // n_col, C2), f32)],
        (q0, k0, dout0, v0, w_wide, back, attn_out, m2, shares),
        manual=(0, 1, 3, 4, 6, 7),
        megabytes=24,
    )
    grad_image = call(
        na_beside_kernel,
        [((own, C0), bf16)],
        (
            Rows(k0, own),
            Rows(v0, own),
            hot,
            before,
            after,
            left,
            right,
            q0_halo,
            w_wide,
            flat,
            perm,
            dxn_one,
            dxn_two,
            dy0,
            perm_back,
        ),
        manual=(0, 1, 2, 7, 8, 9, 10, 13, 14),
        scratch=(pltpu.VMEM((padded, WIDE), bf16),),
    )[0]
    return (
        merged.reshape(rows // 4, cols // 4, C2),
        grad_image.reshape(rows, cols, C0),
        grad_wo,
    )


def solution(mesh):
    return jax.shard_map(
        per_device,
        mesh=mesh,
        in_specs=(P("row", "col", None), P(), P(), P(), P(), P(), P(), P("row", "col", None)),
        out_specs=(P("row", "col", None), P("row", "col", None), P(("row", "col"), None)),
        check_vma=False,
    )
```

```python
import functools
import math

import jax
import jax.numpy as jnp
import numpy as np
from jax import lax
from jax.experimental import pallas as pl
from jax.experimental.pallas import tpu as pltpu
from jax.sharding import PartitionSpec as P

C0 = 256
C1 = 512
C2 = 1024
NA_HEADS = 4
GHEADS = 8
KERNEL = 7
REACH = KERNEL // 2
EPSILON = 1e-06
LANES = 128
NA_DIM = C0 // NA_HEADS
WIDE = NA_HEADS * LANES
MASKED = -1e15
ROWS = 16
DELTA_LANE = 112
LSE_LANE = 114

f32 = jnp.float32
bf16 = jnp.bfloat16


def dot(left, right):
    return lax.dot_general(left, right, (((1,), (0,)), ((), ())), preferred_element_type=f32)


def dot_last(left, right):
    return lax.dot_general(left, right, (((1,), (1,)), ((), ())), preferred_element_type=f32)


def dot_first(left, right):
    return lax.dot_general(left, right, (((0,), (0,)), ((), ())), preferred_element_type=f32)


def rms_stat(x):
    return lax.rsqrt(jnp.mean(x * x, -1, keepdims=True) + EPSILON)


def rms_back(x, scale, grad):
    return scale * grad - x * scale**3 * jnp.mean(grad * x, -1, keepdims=True)


def token_tables(rows, cols):
    grid = np.arange(rows * cols).reshape(rows // 4, 2, 2, cols // 4, 2, 2)
    order = grid.transpose(2, 5, 1, 4, 0, 3).reshape(-1)
    own_row, own_col = order // cols, order % cols
    outside = [(-99, -99)]
    side = [
        ((r0, r1), pad)
        for (r0, r1), pad in [((-REACH, 0), True), ((0, rows), False), ((rows, rows + REACH), True)]
    ]
    halo = [(r, c) for r in range(-REACH, 0) for c in range(cols)]
    halo += [(r, c) for r in range(rows, rows + REACH) for c in range(cols)]
    for first in (-REACH, cols):
        for (r0, r1), pad in side:
            part = [(r, c) for r in range(r0, r1) for c in range(first, first + REACH)]
            halo += part + outside * (-len(part) % ROWS)
    count = len(halo)
    padded = -(-count // LANES) * LANES
    halo = np.array(halo + outside * (padded - count))

    def band(row, col):
        near_row = np.abs(row[:, None] - np.arange(rows)[None]) <= REACH
        near_col = np.abs(col[:, None] - np.arange(cols)[None]) <= REACH
        return np.where(np.concatenate([near_row, near_col], 1), 0.0, MASKED)

    def lanes(part):
        table = np.zeros((part.shape[0], LANES), np.float32)
        table[:, NA_DIM : NA_DIM + part.shape[1]] = part
        return table

    hot = np.concatenate(
        [own_row[:, None] == np.arange(rows)[None], own_col[:, None] == np.arange(cols)[None]], 1
    ).astype(np.float32)
    perm = np.zeros((rows * cols, rows * cols), np.float32)
    perm[np.arange(rows * cols), order] = 1.0
    place = np.argsort(order)
    natural = np.arange(rows * cols).reshape(rows, cols)
    strips = [natural[:REACH], natural[-REACH:], natural[:, :REACH], natural[:, -REACH:]]
    wanted = place[np.concatenate([s.reshape(-1) for s in strips])]
    select = np.zeros((wanted.size, rows * cols), np.float32)
    select[np.arange(wanted.size), wanted] = 1.0
    corner = np.zeros((2 * ROWS, REACH * cols), np.float32)
    for i, first in enumerate((0, cols - REACH)):
        for r in range(REACH):
            for c in range(REACH):
                corner[i * ROWS + r * REACH + c, r * cols + first + c] = 1.0
    return dict(
        corner=corner,
        perm=perm,
        select=select,
        hot=lanes(hot),
        band_own=lanes(band(own_row, own_col)),
        band_halo=lanes(band(halo[:, 0], halo[:, 1])),
        halo=halo,
        count=count,
    )


def shifted(array, axis, move):
    count = lax.axis_size(axis)
    return lax.ppermute(array, axis, [(i, move(i)) for i in range(count)])


def neighbours(to_next, to_previous, axis):
    count = lax.axis_size(axis)
    up = [(i, i + 1) for i in range(count - 1)]
    down = [(j, i) for i, j in up]
    return lax.ppermute(to_next, axis, up), lax.ppermute(to_previous, axis, down)


def row_halo(top, bottom):
    return neighbours(bottom, top, "row")


def along_z(pair):
    count = lax.axis_size("col")
    return [pair] + [shifted(pair, "col", lambda i: (i + 4 * step) % count) for step in (1, 3, 2)]


def other_core(pieces):
    return [shifted(piece, "col", lambda i: i ^ 1) for piece in pieces]


def across(shard):
    return shifted(shard, "col", lambda i: i ^ 2)


def column_order():
    count = lax.axis_size("col")
    place = jnp.arange(count, dtype=jnp.int32)
    step = jnp.asarray([0, 1, 3, 2], jnp.int32)[place % 4]
    source = (lax.axis_index("col") + count - 4 * step) % count
    return source ^ (2 * ((place // 4) % 2)) ^ (place // 8)


def all_to_all(array, axis):
    return lax.all_to_all(array, axis, split_axis=0, concat_axis=0, tiled=True)


class Rows:
    def __init__(self, array, rows):
        self.array, self.rows = array, rows
        self.shape, self.dtype = (rows, *array.shape[1:]), array.dtype


class Held:
    def __init__(self, source, target, sems, cut):
        dim, count = cut
        size = target.shape[dim] // count
        self.copies = []
        self.parts = []
        for i in range(count):
            at = tuple(pl.ds(i * size, size) if d == dim else slice(None) for d in range(dim + 1))
            part = target.at[at] if count > 1 else target
            self.copies.append(
                pltpu.make_async_copy(source.at[at] if count > 1 else source, part, sems[i])
            )
            self.parts.append(part)
        self.target = target
        self.waiting = [True] * count
        for copy in self.copies:
            copy.start()

    def chunk(self, i):
        if self.waiting[i]:
            self.waiting[i] = False
            self.copies[i].wait()
        return self.parts[i]

    def ready(self):
        for i in range(len(self.copies)):
            self.chunk(i)
        return self.target

    def __getitem__(self, index):
        return self.ready()[index]

    @property
    def shape(self):
        return self.target.shape


class Plain:
    def __init__(self, target):
        self.target = target

    def ready(self):
        return self.target

    def send(self):
        pass

    def __getitem__(self, index):
        return self.target[index]

    def __setitem__(self, index, value):
        self.target[index] = value

    @property
    def shape(self):
        return self.target.shape


class Result(Plain):
    def __init__(self, source, target, sem):
        self.copy = pltpu.make_async_copy(source, target, sem)
        self.target = source
        self.started = False

    def send(self):
        if not self.started:
            self.started = True
            self.copy.start()


def take_from(items, count):
    return [items.pop(0) for _ in range(count)]


def call(kernel, outs, args, manual=(), out_manual=(), scratch=(), smem=0, cuts={}, megabytes=16):
    manual = sorted(i % len(args) for i in manual)
    out_manual = sorted(i % len(outs) for i in out_manual)
    cuts = {i % len(args): cut for i, cut in cuts.items()}
    cuts = [cuts.get(i, (0, 1)) for i in manual]
    total = sum(n for _, n in cuts)

    def body(*refs):
        refs = list(refs)
        take = functools.partial(take_from, refs)
        given, results, extra = take(len(args)), take(len(outs)), take(len(scratch))
        here, there = take(len(manual)), take(len(out_manual))
        sems_in, sems_out = take(2)
        sems = [sems_in.at[i] for i in range(total)]
        values = given[:smem] + [Plain(ref) for ref in given[smem:]]
        writes = [Plain(ref) for ref in results]
        for i, dst, cut in zip(manual, here, cuts):
            source = given[i].at[pl.ds(0, args[i].rows)] if isinstance(args[i], Rows) else given[i]
            values[i] = Held(source, dst, take_from(sems, cut[1]), cut)
        for n, (i, src) in enumerate(zip(out_manual, there)):
            writes[i] = Result(src, results[i], sems_out.at[n])
        kernel(*values, *writes, *extra)
        for i in out_manual:
            writes[i].send()
        for i in manual:
            values[i].ready()
        for i in out_manual:
            writes[i].copy.wait()

    def spec(i, far):
        return pl.BlockSpec(memory_space=pltpu.HBM if i in far else pltpu.VMEM)

    hbm = lambda a: pltpu.with_memory_space_constraint(a, pltpu.HBM)
    return pl.pallas_call(
        body,
        out_shape=[
            pltpu.HBM(*out) if i in out_manual else jax.ShapeDtypeStruct(*out)
            for i, out in enumerate(outs)
        ],
        in_specs=[pl.BlockSpec(memory_space=pltpu.SMEM)] * smem
        + [spec(i, manual) for i in range(smem, len(args))],
        out_specs=[spec(i, out_manual) for i in range(len(outs))],
        scratch_shapes=list(scratch)
        + [pltpu.VMEM(args[i].shape, args[i].dtype) for i in manual]
        + [pltpu.VMEM(*outs[i]) for i in out_manual]
        + [pltpu.SemaphoreType.DMA((max(total, 1),)), pltpu.SemaphoreType.DMA((max(len(out_manual), 1),))],
        compiler_params=pltpu.CompilerParams(vmem_limit_bytes=megabytes * 2**20),
    )(*[hbm(getattr(a, "array", a)) if i in manual else a for i, a in enumerate(args)])


def head_lanes(head):
    return slice(head * LANES, (head + 1) * LANES)


def two_parts(value):
    high = value.astype(bf16).astype(f32)
    return high, value - high


def at_lanes(base, lane, first, value):
    high, low = two_parts(value)
    return jnp.where(lane == first, -high, jnp.where(lane == first + 1, -low, base))


def fill_halo(target, parts):
    first = 0
    for part in parts:
        rows = part.shape[0]
        target[first : first + rows, :] = part[...]
        first += rows
    rest = target.shape[0] - first
    target[first:, :] = jnp.zeros((rest, target.shape[1]), target.dtype)


def corner_kernel(corner_ref, before_ref, after_ref, left_ref, right_ref, left_out, right_out):
    for i, (side, out) in enumerate([(left_ref, left_out), (right_ref, right_out)]):
        pick = corner_ref[i * ROWS : (i + 1) * ROWS]
        rows = side.shape[0]
        out[:ROWS] = dot(pick, before_ref[...]).astype(bf16)
        out[ROWS : ROWS + rows] = side[...]
        out[ROWS + rows :] = dot(pick, after_ref[...]).astype(bf16)


def na_forward_kernel(
    x_ref,
    perm_ref,
    w_ref,
    before_ref,
    after_ref,
    left_ref,
    right_ref,
    hot_ref,
    band_own_ref,
    band_halo_ref,
    w_out_ref,
    one_ref,
    two_ref,
    wqkv_ref,
    dout_ref,
    head_out,
    m2_out,
    q_out,
    k_out,
    v_out,
    q_halo_out,
    a0_out,
    halo_ref,
):
    own = x_ref.shape[0]
    x = dot(perm_ref[...], x_ref[...])
    xn = (x * rms_stat(x)).astype(bf16)
    fill_halo(halo_ref, [before_ref, after_ref, left_ref, right_ref])
    xh = halo_ref[...].astype(f32)
    xhn = (xh * rms_stat(xh)).astype(bf16)
    mine = dot(xn, w_ref[...])
    beside = dot(xhn, w_ref[...])
    lane = lax.broadcasted_iota(jnp.int32, (1, LANES), 1)
    is_lse = (lane == LSE_LANE) | (lane == LSE_LANE + 1)
    is_delta = (lane == DELTA_LANE) | (lane == DELTA_LANE + 1)
    one_lse = jnp.where(is_lse, 1.0, 0.0)
    one_delta = jnp.where(is_delta, 1.0, 0.0)
    hot = hot_ref[...].astype(f32)
    band_own = band_own_ref[...].astype(f32)
    band_halo = band_halo_ref[...].astype(f32)
    for h in range(NA_HEADS):
        at = head_lanes(h)
        kat = head_lanes(NA_HEADS + h)
        vat = head_lanes(2 * NA_HEADS + h)
        q = mine[:, at] + hot
        k_out[:own, at] = (mine[:, kat] + (band_own + one_lse)).astype(bf16)
        k_out[own:, at] = (beside[:, kat] + (band_halo + one_lse)).astype(bf16)
        v_out[:own, at] = (mine[:, vat] + one_delta).astype(bf16)
        v_out[own:, at] = (beside[:, vat] + one_delta).astype(bf16)
        q_halo_out[:, at] = (beside[:, at] + band_halo).astype(bf16)
        score = dot_last(q.astype(bf16), k_out[:, at])
        top = jnp.max(score, -1, keepdims=True)
        weight = jnp.exp(score - top).astype(bf16)
        out = dot(weight, v_out[:, at])
        norm = out[:, DELTA_LANE : DELTA_LANE + 1]
        q_out[:, at] = at_lanes(q, lane, LSE_LANE, top + jnp.log(norm)).astype(bf16)
        a0 = jnp.where(lane < NA_DIM, out / norm, 0.0).astype(bf16)
        a0_out[:, at] = a0
    for result in (q_out, k_out, v_out, q_halo_out, a0_out):
        result.send()
    y = (x + dot(a0_out[...], w_out_ref[...])).astype(bf16)
    quarter = own // 4
    m1 = dot(y[:quarter], one_ref[:C0])
    for part in range(1, 4):
        m1 += dot(y[part * quarter : (part + 1) * quarter], one_ref[part * C0 : (part + 1) * C0])
    m1 = m1.astype(bf16)
    tokens = own // 16
    m2 = dot(m1[:tokens], two_ref[:C1])
    for part in range(1, 4):
        m2 += dot(m1[part * tokens : (part + 1) * tokens], two_ref[part * C1 : (part + 1) * C1])
    m2 = m2.astype(bf16)
    m2_out[...] = m2
    m2f = m2.astype(f32)
    mn = (m2f * rms_stat(m2f)).astype(bf16)
    dim = C2 // GHEADS
    for part, place in enumerate((2, 0, 1, 3)):
        if part < 3:
            value = dot(mn, wqkv_ref.chunk(part)[...]).astype(bf16)
        else:
            value = dout_ref[...]
        for h in range(GHEADS):
            head_out[h, :, place * dim : (place + 1) * dim] = value[:, h * dim : (h + 1) * dim]


def attention_kernel(scale, grad_ref, query_ref, *refs):
    pieces, (out_ref, col_ref, send_ref) = refs[:-3], refs[-3:]
    owned, dim = out_ref.shape
    query, dout = query_ref[:owned, :dim], query_ref[:owned, dim:]
    scores = [dot_last(query, piece[:, :dim]) * scale for piece in pieces]
    top = functools.reduce(jnp.maximum, [jnp.max(s, -1, keepdims=True) for s in scores])
    norm, out = 0.0, 0.0
    for score, piece in zip(scores, pieces):
        weight = jnp.exp(score - top)
        norm += jnp.sum(weight, -1, keepdims=True)
        out += dot(weight.astype(bf16), piece[:, dim:])
    out = (out / norm).astype(bf16)
    out_ref[...] = out
    lse = top + jnp.log(norm)
    delta = jnp.sum(dout.astype(f32) * out.astype(f32), -1, keepdims=True)
    lane = lax.broadcasted_iota(jnp.int32, (1, LANES), 1)
    col_ref[...] = jnp.where(lane == 0, lse, jnp.where(lane == 1, delta, 0.0))
    parts = [*two_parts(lse), *two_parts(delta)]
    table = jnp.zeros((query.shape[0], LANES), f32)
    for i, part in enumerate(parts):
        table = jnp.where(lane == i, part, table)
    table = table.T
    halves = query.shape[0] // LANES
    stats = [
        table[i : i + 1, half * LANES : (half + 1) * LANES]
        for i in range(len(parts))
        for half in range(halves)
    ]
    stats = jnp.concatenate(stats, 0).astype(bf16)
    partial = dot_first(out, grad_ref[...])
    count, rows = send_ref.shape[0], send_ref.shape[1]
    for i in range(count):
        send_ref[i, :, :C2] = partial[i * rows : (i + 1) * rows].astype(bf16)
        send_ref[i, :, C2:] = stats


def query_grad_kernel(scale, col_ref, query_ref, *refs):
    pieces, dq_ref = refs[:-1], refs[-1]
    owned, dim = dq_ref.shape
    query, dout = query_ref[:owned, :dim], query_ref[:owned, dim:]
    lse, delta = col_ref[:, 0:1], col_ref[:, 1:2]
    total = 0.0
    for piece in pieces:
        keys = piece[:, :dim]
        prob = jnp.exp(dot_last(query, keys) * scale - lse)
        dprob = dot_last(dout, piece[:, dim:])
        total += dot((prob * (dprob - delta)).astype(bf16), keys)
    dq_ref[...] = (total * scale).astype(bf16)


def key_grad_kernel(scale, order_ref, stat_ref, dq_ref, heads_ref, pair_ref, *refs):
    pieces, (out_ref, lse_in, delta_in) = refs[:-3], refs[-3:]
    owned, dim = dq_ref.shape
    halves = owned // LANES
    keys, values = pair_ref[:owned, :dim], pair_ref[:owned, dim:]
    stat_ref = stat_ref.ready()
    dk, dv = 0.0, 0.0
    for i, piece in enumerate(pieces):
        each = piece.shape[0] // owned
        for j in range(each):
            stats = stat_ref[order_ref[each * i + j]].astype(f32)
            for half in range(halves):
                at = slice(j * owned + half * LANES, j * owned + (half + 1) * LANES)
                take = lambda n: stats[n * halves + half : n * halves + half + 1]
                lse_in[:, at] = take(0) + take(1)
                delta_in[:, at] = take(2) + take(3)
        queries, douts = piece[:, :dim], piece[:, dim:]
        prob = jnp.exp(dot_last(keys, queries) * scale - lse_in[...])
        dprob = dot_last(values, douts)
        dk += dot((prob * (dprob - delta_in[...])).astype(bf16), queries)
        dv += dot(prob.astype(bf16), douts)
    out_ref[:, :dim] = dq_ref[...]
    out_ref[:, dim : 2 * dim] = (dk * scale).astype(bf16)
    out_ref[:, 2 * dim : 3 * dim] = dv.astype(bf16)
    out_ref[:, 3 * dim :] = heads_ref[...]


def merge_back_kernel(
    dqkv_ref,
    wqkv_ref,
    m2_ref,
    grad_ref,
    two_ref,
    one_ref,
    w_out_ref,
    a0_ref,
    q_ref,
    select_ref,
    dout_out,
    dy_out,
    *strip_outs,
):
    dim = C2 // GHEADS
    dmn = 0.0
    for part in range(3):
        at = slice(part * dim, (part + 1) * dim)
        grads = jnp.concatenate([dqkv_ref[h, :, at] for h in range(GHEADS)], 1)
        dmn += dot_last(grads, wqkv_ref.chunk(part)[...])
    m2 = m2_ref[...].astype(f32)
    dm2 = (grad_ref[...].astype(f32) + rms_back(m2, rms_stat(m2), dmn)).astype(bf16)
    dm1 = [dot_last(dm2, two_ref.chunk(part)[...]).astype(bf16) for part in range(4)]
    du1 = dot_last(jnp.concatenate(dm1, 0), one_ref[...]).astype(bf16)
    dy = jnp.concatenate([du1[:, part * C0 : (part + 1) * C0] for part in range(4)], 0)
    dy_out[...] = dy
    da0 = dot_last(dy, w_out_ref[...]).astype(bf16).astype(f32)
    lane = lax.broadcasted_iota(jnp.int32, (1, LANES), 1)
    is_lse = (lane == LSE_LANE) | (lane == LSE_LANE + 1)
    for h in range(NA_HEADS):
        at = head_lanes(h)
        mine = da0[:, at]
        delta = jnp.sum(mine * a0_ref[:, at].astype(f32), -1, keepdims=True)
        mine = jnp.where(is_lse, q_ref[:, at].astype(f32), mine)
        dout_out[:, at] = at_lanes(mine, lane, DELTA_LANE, delta).astype(bf16)
    dout_out.send()
    strips = dot(select_ref[...], dout_out[...]).astype(bf16)
    first = 0
    for out in strip_outs:
        out[...] = strips[first : first + out.shape[0]]
        first += out.shape[0]


def own_channels(value):
    lane = lax.broadcasted_iota(jnp.int32, (1, LANES), 1)
    return jnp.where(lane < NA_DIM, value, 0.0).astype(bf16)


def through_projection(grads, first, w_ref):
    at = slice(first * LANES, (first + len(grads)) * LANES)
    return dot_last(jnp.concatenate(grads, 1), w_ref[:, at])


def na_own_kernel(heads, q_ref, k_ref, dout_ref, v_ref, w_ref, dxn_out):
    own = dout_ref.shape[0]
    dq, dk, dv = [], [], []
    for h in heads:
        at = head_lanes(h)
        prob = jnp.exp(dot_last(q_ref[:, at], k_ref[:, at]))
        dprob = dot_last(dout_ref[:, at], v_ref[:, at])
        dscore = (prob * dprob).astype(bf16)
        dq.append(own_channels(dot(dscore, k_ref[:, at])))
        dk.append(own_channels(dot_first(dscore[:, :own], q_ref[:, at])))
        dv.append(own_channels(dot_first(prob[:, :own].astype(bf16), dout_ref[:, at])))
    dxn = through_projection(dq, heads[0], w_ref)
    dxn += through_projection(dk, NA_HEADS + heads[0], w_ref)
    dxn_out[...] = dxn + through_projection(dv, 2 * NA_HEADS + heads[0], w_ref)


def na_rest_kernel(
    heads,
    q_ref,
    k_ref,
    dout_ref,
    v_ref,
    w_ref,
    heads_ref,
    wo_ref,
    m2_ref,
    dxn_out,
    merged_out,
):
    na_own_kernel(heads, q_ref, k_ref, dout_ref, v_ref, w_ref, dxn_out)
    merged = m2_ref[...].astype(f32)
    dim = C2 // GHEADS
    for h in range(GHEADS):
        merged += dot(heads_ref[h, :, 3 * dim :], wo_ref[h * dim : (h + 1) * dim])
    merged_out[...] = merged.astype(bf16)


def na_beside_kernel(
    k_ref,
    v_ref,
    hot_ref,
    before_ref,
    after_ref,
    left_ref,
    right_ref,
    q_halo_ref,
    w_ref,
    x_ref,
    perm_ref,
    dxn_one,
    dxn_two,
    dy_ref,
    perm_back_ref,
    grad_out,
    dout_halo_ref,
):
    lane = lax.broadcasted_iota(jnp.int32, (1, LANES), 1)
    is_mask = (lane >= NA_DIM) & (lane < DELTA_LANE)
    is_lse = (lane == LSE_LANE) | (lane == LSE_LANE + 1)
    fill_halo(dout_halo_ref, [before_ref, after_ref, left_ref, right_ref])
    hot = hot_ref[...].astype(f32)
    dk, dv = [], []
    for h in range(NA_HEADS):
        at = head_lanes(h)
        keys = jnp.where(is_mask, hot, k_ref.chunk(0)[:, at].astype(f32)).astype(bf16)
        douts = dout_halo_ref[:, at]
        queries = jnp.where(
            is_lse, douts.astype(f32), q_halo_ref[:, at].astype(f32)
        ).astype(bf16)
        prob = jnp.exp(dot_last(keys, queries))
        dprob = dot_last(v_ref.chunk(0)[:, at], douts)
        dk.append(own_channels(dot((prob * dprob).astype(bf16), queries)))
        dv.append(own_channels(dot(prob.astype(bf16), douts)))
    dxn = dxn_one[...] + dxn_two[...] + through_projection(dk, NA_HEADS, w_ref)
    dxn += through_projection(dv, 2 * NA_HEADS, w_ref)
    x = dot(perm_ref[...], x_ref[...])
    grad = (dy_ref[...].astype(f32) + rms_back(x, rms_stat(x), dxn)).astype(bf16)
    grad_out[...] = dot(perm_back_ref[...], grad).astype(bf16)


def per_device(image, na_qkv, na_out, merge_one, merge_two, attn_qkv, attn_out, cotangent):
    rows, cols, _ = image.shape
    n_row = lax.axis_size("row")
    n_col = lax.axis_size("col")
    own = rows * cols
    tokens = own // 16
    dim = C2 // GHEADS
    owned = n_row * tokens
    scale = 1.0 / math.sqrt(dim)
    tables = token_tables(rows, cols)
    perm = jnp.asarray(tables["perm"], bf16)
    perm_back = jnp.asarray(tables["perm"].T, bf16)
    select = jnp.asarray(tables["select"], bf16)
    hot = jnp.asarray(tables["hot"], bf16)
    corner = jnp.asarray(tables["corner"], bf16)
    band_own = jnp.asarray(tables["band_own"], bf16)
    halo = tables["halo"]
    padded = halo.shape[0]

    flat = image.reshape(own, C0)
    before, after = row_halo(image[:REACH].reshape(-1, C0), image[-REACH:].reshape(-1, C0))
    left, right = call(
        corner_kernel,
        [((REACH * rows + 2 * ROWS, C0), bf16)] * 2,
        (
            corner,
            before,
            after,
            image[:, :REACH].reshape(-1, C0),
            image[:, -REACH:].reshape(-1, C0),
        ),
        megabytes=8,
    )
    left, right = neighbours(right, left, "col")
    at_row = lax.axis_index("row") * rows + jnp.asarray(halo[:, 0], jnp.int32)
    at_col = lax.axis_index("col") * cols + jnp.asarray(halo[:, 1], jnp.int32)
    inside = (at_row >= 0) & (at_row < rows * n_row) & (at_col >= 0) & (at_col < cols * n_col)
    lane = jnp.arange(LANES)
    mask_lane = (lane >= NA_DIM) & (lane < NA_DIM + rows + cols)
    band_halo = jnp.where(
        ~inside[:, None] & mask_lane[None], MASKED, jnp.asarray(tables["band_halo"], f32)
    ).astype(bf16)

    grad = cotangent.reshape(tokens, C2)
    dout = dot_last(grad, attn_out).astype(bf16)

    na_scale = np.ones((1, 3 * NA_HEADS, 1), np.float32)
    na_scale[:, :NA_HEADS] = 1.0 / math.sqrt(NA_DIM)
    w_wide = jnp.pad(
        (na_qkv.reshape(C0, 3 * NA_HEADS, NA_DIM) * jnp.asarray(na_scale, bf16)),
        ((0, 0), (0, 0), (0, LANES - NA_DIM)),
    ).reshape(C0, 3 * WIDE)
    w_out_wide = jnp.pad(
        na_out.reshape(NA_HEADS, NA_DIM, C0), ((0, 0), (0, LANES - NA_DIM), (0, 0))
    ).reshape(WIDE, C0)

    heads, m2, q0, k0, v0, q0_halo, a0 = call(
        na_forward_kernel,
        [
            ((GHEADS, tokens, 4 * dim), bf16),
            ((tokens, C2), bf16),
            ((own, WIDE), bf16),
            ((own + padded, WIDE), bf16),
            ((own + padded, WIDE), bf16),
            ((padded, WIDE), bf16),
            ((own, WIDE), bf16),
        ],
        (
            flat,
            perm,
            w_wide,
            before,
            after,
            left,
            right,
            hot,
            band_own,
            band_halo,
            w_out_wide,
            merge_one,
            merge_two,
            attn_qkv,
            dout,
        ),
        manual=(0, 1, 2, 7, 8, 9, 10, 11, 12, 13),
        cuts={13: (1, 3)},
        out_manual=(1, 2, 3, 4, 5, 6),
        scratch=(pltpu.VMEM((padded, C0), bf16),),
        megabytes=40,
    )

    mine = all_to_all(heads, "row").reshape(owned, 4 * dim)
    keyval, queries = mine[:, : 2 * dim], mine[:, 2 * dim :]
    keyval = jnp.concatenate([keyval, across(keyval)], 0)
    queries = jnp.concatenate(along_z(queries), 0)
    keyval, share = lax.optimization_barrier((keyval, grad))
    share = jnp.broadcast_to(share[None], (n_row, tokens, C2))
    grad_row = all_to_all(share, "row").reshape(owned, C2)
    keyval = along_z(keyval)
    keyval_core = other_core(keyval)
    queries = [queries, across(queries)]
    keyval += keyval_core
    out_heads, stats, send = call(
        functools.partial(attention_kernel, scale),
        [((owned, dim), bf16), ((owned, LANES), f32), ((n_col, dim // n_col, C2 + LANES), bf16)],
        (grad_row, queries[0], *keyval),
    )
    shares = all_to_all(send, "col")
    dq = call(
        functools.partial(query_grad_kernel, scale),
        [((owned, dim), bf16)],
        (stats, queries[0], *keyval),
    )[0]
    queries += other_core(queries)
    part = queries[0].shape[0]
    back = call(
        functools.partial(key_grad_kernel, scale),
        [((owned, 4 * dim), bf16)],
        (column_order(), shares[:, :, C2:], dq, out_heads, keyval[0], *queries),
        scratch=(pltpu.VMEM((1, part), f32), pltpu.VMEM((1, part), f32)),
        smem=1,
    )[0]
    grad_wo = jnp.sum(shares[:, :, :C2].astype(f32), 0)
    back = all_to_all(back.reshape(n_row, tokens, 4 * dim), "row")

    dout0, dy0, top, bottom, left, right = call(
        merge_back_kernel,
        [((own, WIDE), bf16), ((own, C0), bf16)]
        + [((REACH * n, WIDE), bf16) for n in (cols, cols, rows, rows)],
        (back, attn_qkv, m2, grad, merge_two, merge_one, w_out_wide, a0, q0, select),
        manual=range(1, 10),
        out_manual=(1,),
        cuts={1: (1, 3), 4: (0, 4)},
        megabytes=32,
    )
    before, after = row_halo(top, bottom)
    half = NA_HEADS // 2
    dxn_one = call(
        functools.partial(na_own_kernel, range(half)),
        [((own, C0), f32)],
        (q0, k0, dout0, v0, w_wide),
        manual=(0, 1, 3, 4),
    )[0]
    before, after, dxn_one = lax.optimization_barrier((before, after, dxn_one))
    left, right = call(
        corner_kernel,
        [((left.shape[0] + 2 * ROWS, WIDE), bf16)] * 2,
        (corner, before, after, left, right),
        megabytes=8,
    )
    left, right, q0 = lax.optimization_barrier((left, right, q0))
    left, right = neighbours(right, left, "col")
    dxn_two, merged = call(
        functools.partial(na_rest_kernel, range(half, NA_HEADS)),
        [((own, C0), f32), ((tokens, C2), bf16)],
        (q0, k0, dout0, v0, w_wide, back, attn_out, m2),
        manual=(0, 1, 3, 4, 6, 7),
        megabytes=20,
    )
    grad_image = call(
        na_beside_kernel,
        [((own, C0), bf16)],
        (
            Rows(k0, own),
            Rows(v0, own),
            hot,
            before,
            after,
            left,
            right,
            q0_halo,
            w_wide,
            flat,
            perm,
            dxn_one,
            dxn_two,
            dy0,
            perm_back,
        ),
        manual=(0, 1, 2, 7, 8, 9, 10, 13, 14),
        scratch=(pltpu.VMEM((padded, WIDE), bf16),),
    )[0]
    return (
        merged.reshape(rows // 4, cols // 4, C2),
        grad_image.reshape(rows, cols, C0),
        grad_wo,
    )


def solution(mesh):
    return jax.shard_map(
        per_device,
        mesh=mesh,
        in_specs=(P("row", "col", None), P(), P(), P(), P(), P(), P(), P("row", "col", None)),
        out_specs=(P("row", "col", None), P("row", "col", None), P(("row", "col"), None)),
        check_vma=False,
    )
```

```python
import functools
import math

import jax
import jax.numpy as jnp
import numpy as np
from jax import lax
from jax.experimental import pallas as pl
from jax.experimental.pallas import tpu as pltpu
from jax.sharding import PartitionSpec as P

C0 = 256
C1 = 512
C2 = 1024
NA_HEADS = 4
GHEADS = 8
KERNEL = 7
REACH = KERNEL // 2
EPSILON = 1e-06
LANES = 128
NA_DIM = C0 // NA_HEADS
WIDE = NA_HEADS * LANES
MASKED = -1e15
ROWS = 16
DELTA_LANE = 112
LSE_LANE = 114

f32 = jnp.float32
bf16 = jnp.bfloat16


def dot(left, right):
    return lax.dot_general(left, right, (((1,), (0,)), ((), ())), preferred_element_type=f32)


def dot_last(left, right):
    return lax.dot_general(left, right, (((1,), (1,)), ((), ())), preferred_element_type=f32)


def dot_first(left, right):
    return lax.dot_general(left, right, (((0,), (0,)), ((), ())), preferred_element_type=f32)


def rms_stat(x):
    return lax.rsqrt(jnp.mean(x * x, -1, keepdims=True) + EPSILON)


def rms_back(x, scale, grad):
    return scale * grad - x * scale**3 * jnp.mean(grad * x, -1, keepdims=True)


def token_tables(rows, cols):
    grid = np.arange(rows * cols).reshape(rows // 4, 2, 2, cols // 4, 2, 2)
    order = grid.transpose(2, 5, 1, 4, 0, 3).reshape(-1)
    own_row, own_col = order // cols, order % cols
    outside = [(-99, -99)]
    side = [
        ((r0, r1), pad)
        for (r0, r1), pad in [((-REACH, 0), True), ((0, rows), False), ((rows, rows + REACH), True)]
    ]
    halo = [(r, c) for r in range(-REACH, 0) for c in range(cols)]
    halo += [(r, c) for r in range(rows, rows + REACH) for c in range(cols)]
    for first in (-REACH, cols):
        for (r0, r1), pad in side:
            part = [(r, c) for r in range(r0, r1) for c in range(first, first + REACH)]
            halo += part + outside * (-len(part) % ROWS)
    count = len(halo)
    padded = -(-count // LANES) * LANES
    halo = np.array(halo + outside * (padded - count))

    def band(row, col):
        near_row = np.abs(row[:, None] - np.arange(rows)[None]) <= REACH
        near_col = np.abs(col[:, None] - np.arange(cols)[None]) <= REACH
        return np.where(np.concatenate([near_row, near_col], 1), 0.0, MASKED)

    def lanes(part):
        table = np.zeros((part.shape[0], LANES), np.float32)
        table[:, NA_DIM : NA_DIM + part.shape[1]] = part
        return table

    hot = np.concatenate(
        [own_row[:, None] == np.arange(rows)[None], own_col[:, None] == np.arange(cols)[None]], 1
    ).astype(np.float32)
    perm = np.zeros((rows * cols, rows * cols), np.float32)
    perm[np.arange(rows * cols), order] = 1.0
    place = np.argsort(order)
    natural = np.arange(rows * cols).reshape(rows, cols)
    strips = [natural[:REACH], natural[-REACH:], natural[:, :REACH], natural[:, -REACH:]]
    wanted = place[np.concatenate([s.reshape(-1) for s in strips])]
    select = np.zeros((wanted.size, rows * cols), np.float32)
    select[np.arange(wanted.size), wanted] = 1.0
    corner = np.zeros((2 * ROWS, REACH * cols), np.float32)
    for i, first in enumerate((0, cols - REACH)):
        for r in range(REACH):
            for c in range(REACH):
                corner[i * ROWS + r * REACH + c, r * cols + first + c] = 1.0
    return dict(
        corner=corner,
        perm=perm,
        select=select,
        hot=lanes(hot),
        band_own=lanes(band(own_row, own_col)),
        band_halo=lanes(band(halo[:, 0], halo[:, 1])),
        halo=halo,
        count=count,
    )


def shifted(array, axis, move):
    count = lax.axis_size(axis)
    return lax.ppermute(array, axis, [(i, move(i)) for i in range(count)])


def neighbours(to_next, to_previous, axis):
    count = lax.axis_size(axis)
    up = [(i, i + 1) for i in range(count - 1)]
    down = [(j, i) for i, j in up]
    return lax.ppermute(to_next, axis, up), lax.ppermute(to_previous, axis, down)


def row_halo(top, bottom):
    return neighbours(bottom, top, "row")


def along_z(pair):
    count = lax.axis_size("col")
    return [pair] + [shifted(pair, "col", lambda i: (i + 4 * step) % count) for step in (1, 3, 2)]


def other_core(pieces):
    return [shifted(piece, "col", lambda i: i ^ 1) for piece in pieces]


def across(shard):
    return shifted(shard, "col", lambda i: i ^ 2)


def column_order():
    count = lax.axis_size("col")
    place = jnp.arange(count, dtype=jnp.int32)
    step = jnp.asarray([0, 1, 3, 2], jnp.int32)[place % 4]
    source = (lax.axis_index("col") + count - 4 * step) % count
    return source ^ (2 * ((place // 4) % 2)) ^ (place // 8)


def all_to_all(array, axis):
    return lax.all_to_all(array, axis, split_axis=0, concat_axis=0, tiled=True)


class Rows:
    def __init__(self, array, rows):
        self.array, self.rows = array, rows
        self.shape, self.dtype = (rows, *array.shape[1:]), array.dtype


class Held:
    def __init__(self, source, target, sems, cut):
        dim, count = cut
        size = target.shape[dim] // count
        self.copies = []
        self.parts = []
        for i in range(count):
            at = tuple(pl.ds(i * size, size) if d == dim else slice(None) for d in range(dim + 1))
            part = target.at[at] if count > 1 else target
            self.copies.append(
                pltpu.make_async_copy(source.at[at] if count > 1 else source, part, sems[i])
            )
            self.parts.append(part)
        self.target = target
        self.waiting = [True] * count
        for copy in self.copies:
            copy.start()

    def chunk(self, i):
        if self.waiting[i]:
            self.waiting[i] = False
            self.copies[i].wait()
        return self.parts[i]

    def ready(self):
        for i in range(len(self.copies)):
            self.chunk(i)
        return self.target

    def __getitem__(self, index):
        return self.ready()[index]

    @property
    def shape(self):
        return self.target.shape


class Plain:
    def __init__(self, target):
        self.target = target

    def ready(self):
        return self.target

    def send(self):
        pass

    def __getitem__(self, index):
        return self.target[index]

    def __setitem__(self, index, value):
        self.target[index] = value

    @property
    def shape(self):
        return self.target.shape


class Result(Plain):
    def __init__(self, source, target, sem):
        self.copy = pltpu.make_async_copy(source, target, sem)
        self.target = source
        self.started = False

    def send(self):
        if not self.started:
            self.started = True
            self.copy.start()


def take_from(items, count):
    return [items.pop(0) for _ in range(count)]


def call(kernel, outs, args, manual=(), out_manual=(), scratch=(), smem=0, cuts={}, megabytes=16):
    manual = sorted(i % len(args) for i in manual)
    out_manual = sorted(i % len(outs) for i in out_manual)
    cuts = {i % len(args): cut for i, cut in cuts.items()}
    cuts = [cuts.get(i, (0, 1)) for i in manual]
    total = sum(n for _, n in cuts)

    def body(*refs):
        refs = list(refs)
        take = functools.partial(take_from, refs)
        given, results, extra = take(len(args)), take(len(outs)), take(len(scratch))
        here, there = take(len(manual)), take(len(out_manual))
        sems_in, sems_out = take(2)
        sems = [sems_in.at[i] for i in range(total)]
        values = given[:smem] + [Plain(ref) for ref in given[smem:]]
        writes = [Plain(ref) for ref in results]
        for i, dst, cut in zip(manual, here, cuts):
            source = given[i].at[pl.ds(0, args[i].rows)] if isinstance(args[i], Rows) else given[i]
            values[i] = Held(source, dst, take_from(sems, cut[1]), cut)
        for n, (i, src) in enumerate(zip(out_manual, there)):
            writes[i] = Result(src, results[i], sems_out.at[n])
        kernel(*values, *writes, *extra)
        for i in out_manual:
            writes[i].send()
        for i in manual:
            values[i].ready()
        for i in out_manual:
            writes[i].copy.wait()

    def spec(i, far):
        return pl.BlockSpec(memory_space=pltpu.HBM if i in far else pltpu.VMEM)

    hbm = lambda a: pltpu.with_memory_space_constraint(a, pltpu.HBM)
    return pl.pallas_call(
        body,
        out_shape=[
            pltpu.HBM(*out) if i in out_manual else jax.ShapeDtypeStruct(*out)
            for i, out in enumerate(outs)
        ],
        in_specs=[pl.BlockSpec(memory_space=pltpu.SMEM)] * smem
        + [spec(i, manual) for i in range(smem, len(args))],
        out_specs=[spec(i, out_manual) for i in range(len(outs))],
        scratch_shapes=list(scratch)
        + [pltpu.VMEM(args[i].shape, args[i].dtype) for i in manual]
        + [pltpu.VMEM(*outs[i]) for i in out_manual]
        + [pltpu.SemaphoreType.DMA((max(total, 1),)), pltpu.SemaphoreType.DMA((max(len(out_manual), 1),))],
        compiler_params=pltpu.CompilerParams(vmem_limit_bytes=megabytes * 2**20),
    )(*[hbm(getattr(a, "array", a)) if i in manual else a for i, a in enumerate(args)])


def head_lanes(head):
    return slice(head * LANES, (head + 1) * LANES)


def two_parts(value):
    high = value.astype(bf16).astype(f32)
    return high, value - high


def at_lanes(base, lane, first, value):
    high, low = two_parts(value)
    return jnp.where(lane == first, -high, jnp.where(lane == first + 1, -low, base))


def head_of(pairs, head, section=0):
    first = section * C0 + (head // 2) * LANES
    pair = pairs[:, first : first + LANES]
    return pltpu.roll(pair, NA_DIM, 1) if head % 2 else pair


def as_pairs(heads):
    lane = lax.broadcasted_iota(jnp.int32, (1, LANES), 1)
    pairs = [
        jnp.where(lane < NA_DIM, heads[i], pltpu.roll(heads[i + 1], NA_DIM, 1))
        for i in range(0, len(heads), 2)
    ]
    return jnp.concatenate(pairs, 1).astype(bf16)


def fill_halo(target, parts):
    first = 0
    for part in parts:
        rows = part.shape[0]
        target[first : first + rows, :] = part[...]
        first += rows
    rest = target.shape[0] - first
    target[first:, :] = jnp.zeros((rest, target.shape[1]), target.dtype)


def corner_kernel(corner_ref, before_ref, after_ref, left_ref, right_ref, left_out, right_out):
    for i, (side, out) in enumerate([(left_ref, left_out), (right_ref, right_out)]):
        pick = corner_ref[i * ROWS : (i + 1) * ROWS]
        rows = side.shape[0]
        out[:ROWS] = dot(pick, before_ref[...]).astype(bf16)
        out[ROWS : ROWS + rows] = side[...]
        out[ROWS + rows :] = dot(pick, after_ref[...]).astype(bf16)


def na_forward_kernel(
    x_ref,
    perm_ref,
    w_ref,
    before_ref,
    after_ref,
    left_ref,
    right_ref,
    hot_ref,
    band_own_ref,
    band_halo_ref,
    w_out_ref,
    one_ref,
    two_ref,
    wqkv_ref,
    dout_ref,
    head_out,
    m2_out,
    q_out,
    k_out,
    v_out,
    q_halo_out,
    a0_out,
    halo_ref,
):
    own = x_ref.shape[0]
    x = dot(perm_ref[...], x_ref[...])
    xn = (x * rms_stat(x)).astype(bf16)
    fill_halo(halo_ref, [before_ref, after_ref, left_ref, right_ref])
    xh = halo_ref[...].astype(f32)
    xhn = (xh * rms_stat(xh)).astype(bf16)
    mine = dot(xn, w_ref[...])
    beside = dot(xhn, w_ref[...])
    lane = lax.broadcasted_iota(jnp.int32, (1, LANES), 1)
    is_lse = (lane == LSE_LANE) | (lane == LSE_LANE + 1)
    is_delta = (lane == DELTA_LANE) | (lane == DELTA_LANE + 1)
    one_lse = jnp.where(is_lse, 1.0, 0.0)
    one_delta = jnp.where(is_delta, 1.0, 0.0)
    hot = hot_ref[...].astype(f32)
    band_own = band_own_ref[...].astype(f32) + one_lse
    band_halo = band_halo_ref[...].astype(f32)
    channel = lane < NA_DIM
    scale = 1.0 / math.sqrt(NA_DIM)
    outs = []
    for h in range(NA_HEADS):
        at = head_lanes(h)
        q = jnp.where(channel, head_of(mine, h) * scale, hot)
        k_out[:own, at] = jnp.where(channel, head_of(mine, h, 1), band_own).astype(bf16)
        k_out[own:, at] = jnp.where(channel, head_of(beside, h, 1), band_halo + one_lse).astype(bf16)
        v_out[:own, at] = jnp.where(channel, head_of(mine, h, 2), one_delta).astype(bf16)
        v_out[own:, at] = jnp.where(channel, head_of(beside, h, 2), one_delta).astype(bf16)
        q_halo_out[:, at] = jnp.where(channel, head_of(beside, h) * scale, band_halo).astype(bf16)
        score = dot_last(q.astype(bf16), k_out[:, at])
        top = jnp.max(score, -1, keepdims=True)
        weight = jnp.exp(score - top).astype(bf16)
        out = dot(weight, v_out[:, at])
        norm = out[:, DELTA_LANE : DELTA_LANE + 1]
        q_out[:, at] = at_lanes(q, lane, LSE_LANE, top + jnp.log(norm)).astype(bf16)
        out = jnp.where(channel, out / norm, 0.0)
        a0_out[:, at] = out.astype(bf16)
        outs.append(out)
    for result in (q_out, k_out, v_out, q_halo_out, a0_out):
        result.send()
    y = (x + dot(as_pairs(outs), w_out_ref[...])).astype(bf16)
    quarter = own // 4
    m1 = dot(y[:quarter], one_ref[:C0])
    for part in range(1, 4):
        m1 += dot(y[part * quarter : (part + 1) * quarter], one_ref[part * C0 : (part + 1) * C0])
    m1 = m1.astype(bf16)
    tokens = own // 16
    m2 = dot(m1[:tokens], two_ref[:C1])
    for part in range(1, 4):
        m2 += dot(m1[part * tokens : (part + 1) * tokens], two_ref[part * C1 : (part + 1) * C1])
    m2 = m2.astype(bf16)
    m2_out[...] = m2
    m2f = m2.astype(f32)
    mn = (m2f * rms_stat(m2f)).astype(bf16)
    dim = C2 // GHEADS
    for part, place in enumerate((2, 0, 1, 3)):
        if part < 3:
            value = dot(mn, wqkv_ref.chunk(part)[...]).astype(bf16)
        else:
            value = dout_ref[...]
        for h in range(GHEADS):
            head_out[h, :, place * dim : (place + 1) * dim] = value[:, h * dim : (h + 1) * dim]


def attention_kernel(scale, grad_ref, query_ref, *refs):
    pieces, (out_ref, col_ref, send_ref) = refs[:-3], refs[-3:]
    owned, dim = out_ref.shape
    query, dout = query_ref[:owned, :dim], query_ref[:owned, dim:]
    scores = [dot_last(query, piece[:, :dim]) * scale for piece in pieces]
    top = functools.reduce(jnp.maximum, [jnp.max(s, -1, keepdims=True) for s in scores])
    norm, out = 0.0, 0.0
    for score, piece in zip(scores, pieces):
        weight = jnp.exp(score - top)
        norm += jnp.sum(weight, -1, keepdims=True)
        out += dot(weight.astype(bf16), piece[:, dim:])
    out = (out / norm).astype(bf16)
    out_ref[...] = out
    lse = top + jnp.log(norm)
    delta = jnp.sum(dout.astype(f32) * out.astype(f32), -1, keepdims=True)
    lane = lax.broadcasted_iota(jnp.int32, (1, LANES), 1)
    col_ref[...] = jnp.where(lane == 0, lse, jnp.where(lane == 1, delta, 0.0))
    parts = [*two_parts(lse), *two_parts(delta)]
    table = jnp.zeros((query.shape[0], LANES), f32)
    for i, part in enumerate(parts):
        table = jnp.where(lane == i, part, table)
    table = table.T
    halves = query.shape[0] // LANES
    stats = [
        table[i : i + 1, half * LANES : (half + 1) * LANES]
        for i in range(len(parts))
        for half in range(halves)
    ]
    stats = jnp.concatenate(stats, 0).astype(bf16)
    partial = dot_first(out, grad_ref[...])
    count, rows = send_ref.shape[0], send_ref.shape[1]
    for i in range(count):
        send_ref[i, :, :C2] = partial[i * rows : (i + 1) * rows].astype(bf16)
        send_ref[i, :, C2:] = stats


def query_grad_kernel(scale, col_ref, query_ref, *refs):
    pieces, dq_ref = refs[:-1], refs[-1]
    owned, dim = dq_ref.shape
    query, dout = query_ref[:owned, :dim], query_ref[:owned, dim:]
    lse, delta = col_ref[:, 0:1], col_ref[:, 1:2]
    total = 0.0
    for piece in pieces:
        keys = piece[:, :dim]
        prob = jnp.exp(dot_last(query, keys) * scale - lse)
        dprob = dot_last(dout, piece[:, dim:])
        total += dot((prob * (dprob - delta)).astype(bf16), keys)
    dq_ref[...] = (total * scale).astype(bf16)


def key_grad_kernel(scale, order_ref, stat_ref, dq_ref, heads_ref, pair_ref, *refs):
    pieces, (out_ref, lse_in, delta_in) = refs[:-3], refs[-3:]
    owned, dim = dq_ref.shape
    halves = owned // LANES
    keys, values = pair_ref[:owned, :dim], pair_ref[:owned, dim:]
    stat_ref = stat_ref.ready()
    dk, dv = 0.0, 0.0
    for i, piece in enumerate(pieces):
        each = piece.shape[0] // owned
        for j in range(each):
            stats = stat_ref[order_ref[each * i + j]][:, C2:].astype(f32)
            for half in range(halves):
                at = slice(j * owned + half * LANES, j * owned + (half + 1) * LANES)
                take = lambda n: stats[n * halves + half : n * halves + half + 1]
                lse_in[:, at] = take(0) + take(1)
                delta_in[:, at] = take(2) + take(3)
        queries, douts = piece[:, :dim], piece[:, dim:]
        prob = jnp.exp(dot_last(keys, queries) * scale - lse_in[...])
        dprob = dot_last(values, douts)
        dk += dot((prob * (dprob - delta_in[...])).astype(bf16), queries)
        dv += dot(prob.astype(bf16), douts)
    out_ref[:, :dim] = dq_ref[...]
    out_ref[:, dim : 2 * dim] = (dk * scale).astype(bf16)
    out_ref[:, 2 * dim : 3 * dim] = dv.astype(bf16)
    out_ref[:, 3 * dim :] = heads_ref[...]


def merge_back_kernel(
    dqkv_ref,
    wqkv_ref,
    m2_ref,
    grad_ref,
    two_ref,
    one_ref,
    w_out_ref,
    a0_ref,
    q_ref,
    select_ref,
    dout_out,
    dy_out,
    *strip_outs,
):
    dim = C2 // GHEADS
    dmn = 0.0
    for part in range(3):
        at = slice(part * dim, (part + 1) * dim)
        grads = jnp.concatenate([dqkv_ref[h, :, at] for h in range(GHEADS)], 1)
        dmn += dot_last(grads, wqkv_ref.chunk(part)[...])
    m2 = m2_ref[...].astype(f32)
    dm2 = (grad_ref[...].astype(f32) + rms_back(m2, rms_stat(m2), dmn)).astype(bf16)
    dm1 = [dot_last(dm2, two_ref.chunk(part)[...]).astype(bf16) for part in range(4)]
    du1 = dot_last(jnp.concatenate(dm1, 0), one_ref[...]).astype(bf16)
    dy = jnp.concatenate([du1[:, part * C0 : (part + 1) * C0] for part in range(4)], 0)
    dy_out[...] = dy
    da0 = dot_last(dy, w_out_ref[...]).astype(bf16).astype(f32)
    lane = lax.broadcasted_iota(jnp.int32, (1, LANES), 1)
    is_lse = (lane == LSE_LANE) | (lane == LSE_LANE + 1)
    for h in range(NA_HEADS):
        at = head_lanes(h)
        mine = jnp.where(lane < NA_DIM, head_of(da0, h), 0.0)
        delta = jnp.sum(mine * a0_ref[:, at].astype(f32), -1, keepdims=True)
        mine = jnp.where(is_lse, q_ref[:, at].astype(f32), mine)
        dout_out[:, at] = at_lanes(mine, lane, DELTA_LANE, delta).astype(bf16)
    dout_out.send()
    strips = dot(select_ref[...], dout_out[...]).astype(bf16)
    first = 0
    for out in strip_outs:
        out[...] = strips[first : first + out.shape[0]]
        first += out.shape[0]


def through_projection(grads, section, first, w_ref):
    start = section * C0 + first * NA_DIM
    return dot_last(as_pairs(grads), w_ref[:, start : start + len(grads) * NA_DIM])


def na_own_kernel(heads, q_ref, k_ref, dout_ref, v_ref, w_ref, dxn_out):
    own = dout_ref.shape[0]
    dq, dk, dv = [], [], []
    for h in heads:
        at = head_lanes(h)
        prob = jnp.exp(dot_last(q_ref[:, at], k_ref[:, at]))
        dprob = dot_last(dout_ref[:, at], v_ref[:, at])
        dscore = (prob * dprob).astype(bf16)
        dq.append(dot(dscore, k_ref[:, at]) * (1.0 / math.sqrt(NA_DIM)))
        dk.append(dot_first(dscore[:, :own], q_ref[:, at]))
        dv.append(dot_first(prob[:, :own].astype(bf16), dout_ref[:, at]))
    dxn = through_projection(dq, 0, heads[0], w_ref)
    dxn += through_projection(dk, 1, heads[0], w_ref)
    dxn_out[...] = dxn + through_projection(dv, 2, heads[0], w_ref)


def na_rest_kernel(
    heads,
    q_ref,
    k_ref,
    dout_ref,
    v_ref,
    w_ref,
    heads_ref,
    wo_ref,
    m2_ref,
    dxn_out,
    merged_out,
):
    na_own_kernel(heads, q_ref, k_ref, dout_ref, v_ref, w_ref, dxn_out)
    merged = m2_ref[...].astype(f32)
    dim = C2 // GHEADS
    for h in range(GHEADS):
        merged += dot(heads_ref[h, :, 3 * dim :], wo_ref[h * dim : (h + 1) * dim])
    merged_out[...] = merged.astype(bf16)


def na_beside_kernel(
    k_ref,
    v_ref,
    hot_ref,
    before_ref,
    after_ref,
    left_ref,
    right_ref,
    q_halo_ref,
    w_ref,
    x_ref,
    perm_ref,
    dxn_one,
    dxn_two,
    dy_ref,
    perm_back_ref,
    grad_out,
    dout_halo_ref,
):
    lane = lax.broadcasted_iota(jnp.int32, (1, LANES), 1)
    is_mask = (lane >= NA_DIM) & (lane < DELTA_LANE)
    is_lse = (lane == LSE_LANE) | (lane == LSE_LANE + 1)
    fill_halo(dout_halo_ref, [before_ref, after_ref, left_ref, right_ref])
    hot = hot_ref[...].astype(f32)
    dk, dv = [], []
    for h in range(NA_HEADS):
        at = head_lanes(h)
        keys = jnp.where(is_mask, hot, k_ref.chunk(0)[:, at].astype(f32)).astype(bf16)
        douts = dout_halo_ref[:, at]
        queries = jnp.where(
            is_lse, douts.astype(f32), q_halo_ref[:, at].astype(f32)
        ).astype(bf16)
        prob = jnp.exp(dot_last(keys, queries))
        dprob = dot_last(v_ref.chunk(0)[:, at], douts)
        dk.append(dot((prob * dprob).astype(bf16), queries))
        dv.append(dot(prob.astype(bf16), douts))
    dxn = dxn_one[...] + dxn_two[...] + through_projection(dk, 1, 0, w_ref)
    dxn += through_projection(dv, 2, 0, w_ref)
    x = dot(perm_ref[...], x_ref[...])
    grad = (dy_ref[...].astype(f32) + rms_back(x, rms_stat(x), dxn)).astype(bf16)
    grad_out[...] = dot(perm_back_ref[...], grad).astype(bf16)


def per_device(image, na_qkv, na_out, merge_one, merge_two, attn_qkv, attn_out, cotangent):
    rows, cols, _ = image.shape
    n_row = lax.axis_size("row")
    n_col = lax.axis_size("col")
    own = rows * cols
    tokens = own // 16
    dim = C2 // GHEADS
    owned = n_row * tokens
    scale = 1.0 / math.sqrt(dim)
    tables = token_tables(rows, cols)
    perm = jnp.asarray(tables["perm"], bf16)
    perm_back = jnp.asarray(tables["perm"].T, bf16)
    select = jnp.asarray(tables["select"], bf16)
    hot = jnp.asarray(tables["hot"], bf16)
    corner = jnp.asarray(tables["corner"], bf16)
    band_own = jnp.asarray(tables["band_own"], bf16)
    halo = tables["halo"]
    padded = halo.shape[0]

    flat = image.reshape(own, C0)
    before, after = row_halo(image[:REACH].reshape(-1, C0), image[-REACH:].reshape(-1, C0))
    left, right = call(
        corner_kernel,
        [((REACH * rows + 2 * ROWS, C0), bf16)] * 2,
        (
            corner,
            before,
            after,
            image[:, :REACH].reshape(-1, C0),
            image[:, -REACH:].reshape(-1, C0),
        ),
        megabytes=8,
    )
    left, right = neighbours(right, left, "col")
    at_row = lax.axis_index("row") * rows + jnp.asarray(halo[:, 0], jnp.int32)
    at_col = lax.axis_index("col") * cols + jnp.asarray(halo[:, 1], jnp.int32)
    inside = (at_row >= 0) & (at_row < rows * n_row) & (at_col >= 0) & (at_col < cols * n_col)
    lane = jnp.arange(LANES)
    mask_lane = (lane >= NA_DIM) & (lane < NA_DIM + rows + cols)
    band_halo = jnp.where(
        ~inside[:, None] & mask_lane[None], MASKED, jnp.asarray(tables["band_halo"], f32)
    ).astype(bf16)

    grad = cotangent.reshape(tokens, C2)
    dout = dot_last(grad, attn_out).astype(bf16)

    heads, m2, q0, k0, v0, q0_halo, a0 = call(
        na_forward_kernel,
        [
            ((GHEADS, tokens, 4 * dim), bf16),
            ((tokens, C2), bf16),
            ((own, WIDE), bf16),
            ((own + padded, WIDE), bf16),
            ((own + padded, WIDE), bf16),
            ((padded, WIDE), bf16),
            ((own, WIDE), bf16),
        ],
        (
            flat,
            perm,
            na_qkv,
            before,
            after,
            left,
            right,
            hot,
            band_own,
            band_halo,
            na_out,
            merge_one,
            merge_two,
            attn_qkv,
            dout,
        ),
        manual=(0, 1, 2, 7, 8, 9, 10, 11, 12, 13),
        cuts={13: (1, 3)},
        out_manual=(1, 2, 3, 4, 5, 6),
        scratch=(pltpu.VMEM((padded, C0), bf16),),
        megabytes=40,
    )

    mine = all_to_all(heads, "row").reshape(owned, 4 * dim)
    keyval, queries = mine[:, : 2 * dim], mine[:, 2 * dim :]
    keyval = jnp.concatenate([keyval, across(keyval)], 0)
    queries = jnp.concatenate(along_z(queries), 0)
    keyval, share = lax.optimization_barrier((keyval, grad))
    share = jnp.broadcast_to(share[None], (n_row, tokens, C2))
    grad_row = all_to_all(share, "row").reshape(owned, C2)
    keyval = along_z(keyval)
    keyval_core = other_core(keyval)
    queries = [queries, across(queries)]
    keyval += keyval_core
    out_heads, stats, send = call(
        functools.partial(attention_kernel, scale),
        [((owned, dim), bf16), ((owned, LANES), f32), ((n_col, dim // n_col, C2 + LANES), bf16)],
        (grad_row, queries[0], *keyval),
    )
    shares = all_to_all(send, "col")
    dq = call(
        functools.partial(query_grad_kernel, scale),
        [((owned, dim), bf16)],
        (stats, queries[0], *keyval),
    )[0]
    queries += other_core(queries)
    part = queries[0].shape[0]
    back = call(
        functools.partial(key_grad_kernel, scale),
        [((owned, 4 * dim), bf16)],
        (column_order(), shares, dq, out_heads, keyval[0], *queries),
        scratch=(pltpu.VMEM((1, part), f32), pltpu.VMEM((1, part), f32)),
        smem=1,
    )[0]
    grad_wo = jnp.sum(shares[:, :, :C2].astype(f32), 0)
    back = all_to_all(back.reshape(n_row, tokens, 4 * dim), "row")

    dout0, dy0, top, bottom, left, right = call(
        merge_back_kernel,
        [((own, WIDE), bf16), ((own, C0), bf16)]
        + [((REACH * n, WIDE), bf16) for n in (cols, cols, rows, rows)],
        (back, attn_qkv, m2, grad, merge_two, merge_one, na_out, a0, q0, select),
        manual=range(1, 10),
        out_manual=(1,),
        cuts={1: (1, 3), 4: (0, 4)},
        megabytes=32,
    )
    before, after = row_halo(top, bottom)
    half = NA_HEADS // 2
    dxn_one = call(
        functools.partial(na_own_kernel, range(half)),
        [((own, C0), f32)],
        (q0, k0, dout0, v0, na_qkv),
        manual=(0, 1, 3, 4),
    )[0]
    before, after, dxn_one = lax.optimization_barrier((before, after, dxn_one))
    left, right = call(
        corner_kernel,
        [((left.shape[0] + 2 * ROWS, WIDE), bf16)] * 2,
        (corner, before, after, left, right),
        megabytes=8,
    )
    left, right, q0 = lax.optimization_barrier((left, right, q0))
    left, right = neighbours(right, left, "col")
    dxn_two, merged = call(
        functools.partial(na_rest_kernel, range(half, NA_HEADS)),
        [((own, C0), f32), ((tokens, C2), bf16)],
        (q0, k0, dout0, v0, na_qkv, back, attn_out, m2),
        manual=(0, 1, 3, 4, 6, 7),
        megabytes=20,
    )
    grad_image = call(
        na_beside_kernel,
        [((own, C0), bf16)],
        (
            Rows(k0, own),
            Rows(v0, own),
            hot,
            before,
            after,
            left,
            right,
            q0_halo,
            na_qkv,
            flat,
            perm,
            dxn_one,
            dxn_two,
            dy0,
            perm_back,
        ),
        manual=(0, 1, 2, 7, 8, 9, 10, 13, 14),
        scratch=(pltpu.VMEM((padded, WIDE), bf16),),
    )[0]
    return (
        merged.reshape(rows // 4, cols // 4, C2),
        grad_image.reshape(rows, cols, C0),
        grad_wo,
    )


def solution(mesh):
    return jax.shard_map(
        per_device,
        mesh=mesh,
        in_specs=(P("row", "col", None), P(), P(), P(), P(), P(), P(), P("row", "col", None)),
        out_specs=(P("row", "col", None), P("row", "col", None), P(("row", "col"), None)),
        check_vma=False,
    )
```

```python
import functools
import math

import jax
import jax.numpy as jnp
import numpy as np
from jax import lax
from jax.experimental import pallas as pl
from jax.experimental.pallas import tpu as pltpu
from jax.sharding import PartitionSpec as P

C0 = 256
C1 = 512
C2 = 1024
NA_HEADS = 4
GHEADS = 8
KERNEL = 7
REACH = KERNEL // 2
EPSILON = 1e-06
LANES = 128
NA_DIM = C0 // NA_HEADS
WIDE = NA_HEADS * LANES
MASKED = -1e15
ROWS = 16
DELTA_LANE = 112
LSE_LANE = 114

f32 = jnp.float32
bf16 = jnp.bfloat16


def dot(left, right):
    return lax.dot_general(left, right, (((1,), (0,)), ((), ())), preferred_element_type=f32)


def dot_last(left, right):
    return lax.dot_general(left, right, (((1,), (1,)), ((), ())), preferred_element_type=f32)


def dot_first(left, right):
    return lax.dot_general(left, right, (((0,), (0,)), ((), ())), preferred_element_type=f32)


def rms_stat(x):
    return lax.rsqrt(jnp.mean(x * x, -1, keepdims=True) + EPSILON)


def rms_back(x, scale, grad):
    return scale * grad - x * scale**3 * jnp.mean(grad * x, -1, keepdims=True)


def token_tables(rows, cols):
    grid = np.arange(rows * cols).reshape(rows // 4, 2, 2, cols // 4, 2, 2)
    order = grid.transpose(2, 5, 1, 4, 0, 3).reshape(-1)
    own_row, own_col = order // cols, order % cols
    outside = [(-99, -99)]
    side = [
        ((r0, r1), pad)
        for (r0, r1), pad in [((-REACH, 0), True), ((0, rows), False), ((rows, rows + REACH), True)]
    ]
    halo = [(r, c) for r in range(-REACH, 0) for c in range(cols)]
    halo += [(r, c) for r in range(rows, rows + REACH) for c in range(cols)]
    for first in (-REACH, cols):
        for (r0, r1), pad in side:
            part = [(r, c) for r in range(r0, r1) for c in range(first, first + REACH)]
            halo += part + outside * (-len(part) % ROWS)
    count = len(halo)
    padded = -(-count // LANES) * LANES
    halo = np.array(halo + outside * (padded - count))

    def band(row, col):
        near_row = np.abs(row[:, None] - np.arange(rows)[None]) <= REACH
        near_col = np.abs(col[:, None] - np.arange(cols)[None]) <= REACH
        return np.where(np.concatenate([near_row, near_col], 1), 0.0, MASKED)

    def lanes(part):
        table = np.zeros((part.shape[0], LANES), np.float32)
        table[:, NA_DIM : NA_DIM + part.shape[1]] = part
        return table

    hot = np.concatenate(
        [own_row[:, None] == np.arange(rows)[None], own_col[:, None] == np.arange(cols)[None]], 1
    ).astype(np.float32)
    perm = np.zeros((rows * cols, rows * cols), np.float32)
    perm[np.arange(rows * cols), order] = 1.0
    place = np.argsort(order)
    natural = np.arange(rows * cols).reshape(rows, cols)
    strips = [natural[:REACH], natural[-REACH:], natural[:, :REACH], natural[:, -REACH:]]
    wanted = place[np.concatenate([s.reshape(-1) for s in strips])]
    select = np.zeros((wanted.size, rows * cols), np.float32)
    select[np.arange(wanted.size), wanted] = 1.0
    corner = np.zeros((2 * ROWS, REACH * cols), np.float32)
    for i, first in enumerate((0, cols - REACH)):
        for r in range(REACH):
            for c in range(REACH):
                corner[i * ROWS + r * REACH + c, r * cols + first + c] = 1.0
    return dict(
        corner=corner,
        perm=perm,
        select=select,
        hot=lanes(hot),
        band_own=lanes(band(own_row, own_col)),
        band_halo=lanes(band(halo[:, 0], halo[:, 1])),
        halo=halo,
        count=count,
    )


def shifted(array, axis, move):
    count = lax.axis_size(axis)
    return lax.ppermute(array, axis, [(i, move(i)) for i in range(count)])


def neighbours(to_next, to_previous, axis):
    count = lax.axis_size(axis)
    up = [(i, i + 1) for i in range(count - 1)]
    down = [(j, i) for i, j in up]
    return lax.ppermute(to_next, axis, up), lax.ppermute(to_previous, axis, down)


def row_halo(top, bottom):
    return neighbours(bottom, top, "row")


def along_z(pair):
    count = lax.axis_size("col")
    return [pair] + [shifted(pair, "col", lambda i: (i + 4 * step) % count) for step in (1, 3, 2)]


def other_core(pieces):
    return [shifted(piece, "col", lambda i: i ^ 1) for piece in pieces]


def across(shard):
    return shifted(shard, "col", lambda i: i ^ 2)


def column_order():
    count = lax.axis_size("col")
    place = jnp.arange(count, dtype=jnp.int32)
    step = jnp.asarray([0, 1, 3, 2], jnp.int32)[place % 4]
    source = (lax.axis_index("col") + count - 4 * step) % count
    return source ^ (2 * ((place // 4) % 2)) ^ (place // 8)


def all_to_all(array, axis):
    return lax.all_to_all(array, axis, split_axis=0, concat_axis=0, tiled=True)


class Rows:
    def __init__(self, array, rows):
        self.array, self.rows = array, rows
        self.shape, self.dtype = (rows, *array.shape[1:]), array.dtype


class Held:
    def __init__(self, source, target, sems, cut):
        dim, count = cut
        size = target.shape[dim] // count
        self.copies = []
        self.parts = []
        for i in range(count):
            at = tuple(pl.ds(i * size, size) if d == dim else slice(None) for d in range(dim + 1))
            part = target.at[at] if count > 1 else target
            self.copies.append(
                pltpu.make_async_copy(source.at[at] if count > 1 else source, part, sems[i])
            )
            self.parts.append(part)
        self.target = target
        self.waiting = [True] * count
        for copy in self.copies:
            copy.start()

    def chunk(self, i):
        if self.waiting[i]:
            self.waiting[i] = False
            self.copies[i].wait()
        return self.parts[i]

    def ready(self):
        for i in range(len(self.copies)):
            self.chunk(i)
        return self.target

    def __getitem__(self, index):
        return self.ready()[index]

    @property
    def shape(self):
        return self.target.shape


class Plain:
    def __init__(self, target):
        self.target = target

    def ready(self):
        return self.target

    def send(self):
        pass

    def __getitem__(self, index):
        return self.target[index]

    def __setitem__(self, index, value):
        self.target[index] = value

    @property
    def shape(self):
        return self.target.shape


class Result(Plain):
    def __init__(self, source, target, sem):
        self.copy = pltpu.make_async_copy(source, target, sem)
        self.target = source
        self.started = False

    def send(self):
        if not self.started:
            self.started = True
            self.copy.start()


def take_from(items, count):
    return [items.pop(0) for _ in range(count)]


def call(kernel, outs, args, manual=(), out_manual=(), scratch=(), smem=0, cuts={}, megabytes=16):
    manual = sorted(i % len(args) for i in manual)
    out_manual = sorted(i % len(outs) for i in out_manual)
    cuts = {i % len(args): cut for i, cut in cuts.items()}
    cuts = [cuts.get(i, (0, 1)) for i in manual]
    total = sum(n for _, n in cuts)

    def body(*refs):
        refs = list(refs)
        take = functools.partial(take_from, refs)
        given, results, extra = take(len(args)), take(len(outs)), take(len(scratch))
        here, there = take(len(manual)), take(len(out_manual))
        sems_in, sems_out = take(2)
        sems = [sems_in.at[i] for i in range(total)]
        values = given[:smem] + [Plain(ref) for ref in given[smem:]]
        writes = [Plain(ref) for ref in results]
        for i, dst, cut in zip(manual, here, cuts):
            source = given[i].at[pl.ds(0, args[i].rows)] if isinstance(args[i], Rows) else given[i]
            values[i] = Held(source, dst, take_from(sems, cut[1]), cut)
        for n, (i, src) in enumerate(zip(out_manual, there)):
            writes[i] = Result(src, results[i], sems_out.at[n])
        kernel(*values, *writes, *extra)
        for i in out_manual:
            writes[i].send()
        for i in manual:
            values[i].ready()
        for i in out_manual:
            writes[i].copy.wait()

    def spec(i, far):
        return pl.BlockSpec(memory_space=pltpu.HBM if i in far else pltpu.VMEM)

    hbm = lambda a: pltpu.with_memory_space_constraint(a, pltpu.HBM)
    return pl.pallas_call(
        body,
        out_shape=[
            pltpu.HBM(*out) if i in out_manual else jax.ShapeDtypeStruct(*out)
            for i, out in enumerate(outs)
        ],
        in_specs=[pl.BlockSpec(memory_space=pltpu.SMEM)] * smem
        + [spec(i, manual) for i in range(smem, len(args))],
        out_specs=[spec(i, out_manual) for i in range(len(outs))],
        scratch_shapes=list(scratch)
        + [pltpu.VMEM(args[i].shape, args[i].dtype) for i in manual]
        + [pltpu.VMEM(*outs[i]) for i in out_manual]
        + [pltpu.SemaphoreType.DMA((max(total, 1),)), pltpu.SemaphoreType.DMA((max(len(out_manual), 1),))],
        compiler_params=pltpu.CompilerParams(vmem_limit_bytes=megabytes * 2**20),
    )(*[hbm(getattr(a, "array", a)) if i in manual else a for i, a in enumerate(args)])


def head_lanes(head):
    return slice(head * LANES, (head + 1) * LANES)


def two_parts(value):
    high = value.astype(bf16).astype(f32)
    return high, value - high


def at_lanes(base, lane, first, value):
    high, low = two_parts(value)
    return jnp.where(lane == first, -high, jnp.where(lane == first + 1, -low, base))


def head_of(pairs, head, section=0):
    first = section * C0 + (head // 2) * LANES
    pair = pairs[:, first : first + LANES]
    return pltpu.roll(pair, NA_DIM, 1) if head % 2 else pair


def as_pairs(heads):
    lane = lax.broadcasted_iota(jnp.int32, (1, LANES), 1)
    pairs = [
        jnp.where(lane < NA_DIM, heads[i], pltpu.roll(heads[i + 1], NA_DIM, 1))
        for i in range(0, len(heads), 2)
    ]
    return jnp.concatenate(pairs, 1).astype(bf16)


def fill_halo(target, parts):
    first = 0
    for part in parts:
        rows = part.shape[0]
        target[first : first + rows, :] = part[...]
        first += rows
    rest = target.shape[0] - first
    target[first:, :] = jnp.zeros((rest, target.shape[1]), target.dtype)


def corner_kernel(corner_ref, before_ref, after_ref, left_ref, right_ref, left_out, right_out):
    for i, (side, out) in enumerate([(left_ref, left_out), (right_ref, right_out)]):
        pick = corner_ref[i * ROWS : (i + 1) * ROWS]
        rows = side.shape[0]
        out[:ROWS] = dot(pick, before_ref[...]).astype(bf16)
        out[ROWS : ROWS + rows] = side[...]
        out[ROWS + rows :] = dot(pick, after_ref[...]).astype(bf16)


def na_forward_kernel(
    x_ref,
    perm_ref,
    w_ref,
    before_ref,
    after_ref,
    left_ref,
    right_ref,
    hot_ref,
    band_own_ref,
    band_halo_ref,
    w_out_ref,
    one_ref,
    two_ref,
    wqkv_ref,
    dout_ref,
    head_out,
    m2_out,
    x_out,
    q_one,
    q_two,
    k_one,
    k_two,
    v_one,
    v_two,
    q_halo_out,
    a0_out,
    halo_ref,
):
    own = x_ref.shape[0]
    x = dot(perm_ref[...], x_ref[...])
    x_out[...] = x.astype(bf16)
    x_out.send()
    xn = (x * rms_stat(x)).astype(bf16)
    fill_halo(halo_ref, [before_ref, after_ref, left_ref, right_ref])
    xh = halo_ref[...].astype(f32)
    xhn = (xh * rms_stat(xh)).astype(bf16)
    mine = dot(xn, w_ref[...])
    beside = dot(xhn, w_ref[...])
    lane = lax.broadcasted_iota(jnp.int32, (1, LANES), 1)
    is_lse = (lane == LSE_LANE) | (lane == LSE_LANE + 1)
    is_delta = (lane == DELTA_LANE) | (lane == DELTA_LANE + 1)
    one_lse = jnp.where(is_lse, 1.0, 0.0)
    one_delta = jnp.where(is_delta, 1.0, 0.0)
    hot = hot_ref[...].astype(f32)
    band_own = band_own_ref[...].astype(f32) + one_lse
    band_halo = band_halo_ref[...].astype(f32)
    channel = lane < NA_DIM
    scale = 1.0 / math.sqrt(NA_DIM)
    outs = []
    for h in range(NA_HEADS):
        at = head_lanes(h)
        to = head_lanes(h % 2)
        q_out, k_out, v_out = (q_two, k_two, v_two) if h // 2 else (q_one, k_one, v_one)
        q = jnp.where(channel, head_of(mine, h) * scale, hot)
        k_out[:own, to] = jnp.where(channel, head_of(mine, h, 1), band_own).astype(bf16)
        k_out[own:, to] = jnp.where(channel, head_of(beside, h, 1), band_halo + one_lse).astype(bf16)
        v_out[:own, to] = jnp.where(channel, head_of(mine, h, 2), one_delta).astype(bf16)
        v_out[own:, to] = jnp.where(channel, head_of(beside, h, 2), one_delta).astype(bf16)
        q_halo_out[:, at] = jnp.where(channel, head_of(beside, h) * scale, band_halo).astype(bf16)
        score = dot_last(q.astype(bf16), k_out[:, to])
        top = jnp.max(score, -1, keepdims=True)
        weight = jnp.exp(score - top).astype(bf16)
        out = dot(weight, v_out[:, to])
        norm = out[:, DELTA_LANE : DELTA_LANE + 1]
        q_out[:, to] = at_lanes(q, lane, LSE_LANE, top + jnp.log(norm)).astype(bf16)
        out = jnp.where(channel, out / norm, 0.0)
        a0_out[:, at] = out.astype(bf16)
        outs.append(out)
    for result in (q_one, q_two, k_one, k_two, v_one, v_two, q_halo_out, a0_out):
        result.send()
    y = (x + dot(as_pairs(outs), w_out_ref[...])).astype(bf16)
    quarter = own // 4
    m1 = dot(y[:quarter], one_ref[:C0])
    for part in range(1, 4):
        m1 += dot(y[part * quarter : (part + 1) * quarter], one_ref[part * C0 : (part + 1) * C0])
    m1 = m1.astype(bf16)
    tokens = own // 16
    m2 = dot(m1[:tokens], two_ref[:C1])
    for part in range(1, 4):
        m2 += dot(m1[part * tokens : (part + 1) * tokens], two_ref[part * C1 : (part + 1) * C1])
    m2 = m2.astype(bf16)
    m2_out[...] = m2
    m2f = m2.astype(f32)
    mn = (m2f * rms_stat(m2f)).astype(bf16)
    dim = C2 // GHEADS
    for part, place in enumerate((2, 0, 1, 3)):
        if part < 3:
            value = dot(mn, wqkv_ref.chunk(part)[...]).astype(bf16)
        else:
            value = dout_ref[...]
        for h in range(GHEADS):
            head_out[h, :, place * dim : (place + 1) * dim] = value[:, h * dim : (h + 1) * dim]


def attention_kernel(scale, grad_ref, query_ref, *refs):
    pieces, (out_ref, col_ref, send_ref) = refs[:-3], refs[-3:]
    owned, dim = out_ref.shape
    query, dout = query_ref[:owned, :dim], query_ref[:owned, dim:]
    scores = [dot_last(query, piece[:, :dim]) * scale for piece in pieces]
    top = functools.reduce(jnp.maximum, [jnp.max(s, -1, keepdims=True) for s in scores])
    norm, out = 0.0, 0.0
    for score, piece in zip(scores, pieces):
        weight = jnp.exp(score - top)
        norm += jnp.sum(weight, -1, keepdims=True)
        out += dot(weight.astype(bf16), piece[:, dim:])
    out = (out / norm).astype(bf16)
    out_ref[...] = out
    lse = top + jnp.log(norm)
    delta = jnp.sum(dout.astype(f32) * out.astype(f32), -1, keepdims=True)
    lane = lax.broadcasted_iota(jnp.int32, (1, LANES), 1)
    col_ref[...] = jnp.where(lane == 0, lse, jnp.where(lane == 1, delta, 0.0))
    parts = [*two_parts(lse), *two_parts(delta)]
    table = jnp.zeros((query.shape[0], LANES), f32)
    for i, part in enumerate(parts):
        table = jnp.where(lane == i, part, table)
    table = table.T
    halves = query.shape[0] // LANES
    stats = [
        table[i : i + 1, half * LANES : (half + 1) * LANES]
        for i in range(len(parts))
        for half in range(halves)
    ]
    stats = jnp.concatenate(stats, 0).astype(bf16)
    partial = dot_first(out, grad_ref[...])
    count, rows = send_ref.shape[0], send_ref.shape[1]
    for i in range(count):
        send_ref[i, :, :C2] = partial[i * rows : (i + 1) * rows].astype(bf16)
        send_ref[i, :, C2:] = stats


def query_grad_kernel(scale, col_ref, query_ref, *refs):
    pieces, dq_ref = refs[:-1], refs[-1]
    owned, dim = dq_ref.shape
    query, dout = query_ref[:owned, :dim], query_ref[:owned, dim:]
    lse, delta = col_ref[:, 0:1], col_ref[:, 1:2]
    total = 0.0
    for piece in pieces:
        keys = piece[:, :dim]
        prob = jnp.exp(dot_last(query, keys) * scale - lse)
        dprob = dot_last(dout, piece[:, dim:])
        total += dot((prob * (dprob - delta)).astype(bf16), keys)
    dq_ref[...] = (total * scale).astype(bf16)


def key_grad_kernel(scale, order_ref, stat_ref, dq_ref, heads_ref, pair_ref, *refs):
    pieces, (out_ref, lse_in, delta_in) = refs[:-3], refs[-3:]
    owned, dim = dq_ref.shape
    halves = owned // LANES
    keys, values = pair_ref[:owned, :dim], pair_ref[:owned, dim:]
    stat_ref = stat_ref.ready()
    dk, dv = 0.0, 0.0
    for i, piece in enumerate(pieces):
        each = piece.shape[0] // owned
        for j in range(each):
            stats = stat_ref[order_ref[each * i + j]][:, C2:].astype(f32)
            for half in range(halves):
                at = slice(j * owned + half * LANES, j * owned + (half + 1) * LANES)
                take = lambda n: stats[n * halves + half : n * halves + half + 1]
                lse_in[:, at] = take(0) + take(1)
                delta_in[:, at] = take(2) + take(3)
        queries, douts = piece[:, :dim], piece[:, dim:]
        prob = jnp.exp(dot_last(keys, queries) * scale - lse_in[...])
        dprob = dot_last(values, douts)
        dk += dot((prob * (dprob - delta_in[...])).astype(bf16), queries)
        dv += dot(prob.astype(bf16), douts)
    out_ref[:, :dim] = dq_ref[...]
    out_ref[:, dim : 2 * dim] = (dk * scale).astype(bf16)
    out_ref[:, 2 * dim : 3 * dim] = dv.astype(bf16)
    out_ref[:, 3 * dim :] = heads_ref[...]


def merge_back_kernel(
    dqkv_ref,
    wqkv_ref,
    m2_ref,
    grad_ref,
    two_ref,
    one_ref,
    w_out_ref,
    a0_ref,
    q_one,
    q_two,
    select_ref,
    dout_out,
    dy_out,
    *strip_outs,
):
    dim = C2 // GHEADS
    dmn = 0.0
    for part in range(3):
        at = slice(part * dim, (part + 1) * dim)
        grads = jnp.concatenate([dqkv_ref[h, :, at] for h in range(GHEADS)], 1)
        dmn += dot_last(grads, wqkv_ref.chunk(part)[...])
    m2 = m2_ref[...].astype(f32)
    dm2 = (grad_ref[...].astype(f32) + rms_back(m2, rms_stat(m2), dmn)).astype(bf16)
    dm1 = [dot_last(dm2, two_ref.chunk(part)[...]).astype(bf16) for part in range(4)]
    du1 = dot_last(jnp.concatenate(dm1, 0), one_ref[...]).astype(bf16)
    dy = jnp.concatenate([du1[:, part * C0 : (part + 1) * C0] for part in range(4)], 0)
    dy_out[...] = dy
    da0 = dot_last(dy, w_out_ref[...]).astype(bf16).astype(f32)
    lane = lax.broadcasted_iota(jnp.int32, (1, LANES), 1)
    is_lse = (lane == LSE_LANE) | (lane == LSE_LANE + 1)
    for h in range(NA_HEADS):
        at = head_lanes(h)
        mine = jnp.where(lane < NA_DIM, head_of(da0, h), 0.0)
        delta = jnp.sum(mine * a0_ref[:, at].astype(f32), -1, keepdims=True)
        q_ref = q_two if h // 2 else q_one
        mine = jnp.where(is_lse, q_ref[:, head_lanes(h % 2)].astype(f32), mine)
        dout_out[:, at] = at_lanes(mine, lane, DELTA_LANE, delta).astype(bf16)
    dout_out.send()
    strips = dot(select_ref[...], dout_out[...]).astype(bf16)
    first = 0
    for out in strip_outs:
        out[...] = strips[first : first + out.shape[0]]
        first += out.shape[0]


def through_projection(grads, section, first, w_ref):
    start = section * C0 + first * NA_DIM
    return dot_last(as_pairs(grads), w_ref[:, start : start + len(grads) * NA_DIM])


def na_own_kernel(heads, q_ref, k_ref, dout_ref, v_ref, w_ref, dxn_out):
    own = dout_ref.shape[0]
    dq, dk, dv = [], [], []
    for i, h in enumerate(heads):
        at = head_lanes(i)
        dout = dout_ref[:, head_lanes(h)]
        prob = jnp.exp(dot_last(q_ref[:, at], k_ref[:, at]))
        dprob = dot_last(dout, v_ref[:, at])
        dscore = (prob * dprob).astype(bf16)
        dq.append(dot(dscore, k_ref[:, at]) * (1.0 / math.sqrt(NA_DIM)))
        dk.append(dot_first(dscore[:, :own], q_ref[:, at]))
        dv.append(dot_first(prob[:, :own].astype(bf16), dout))
    dxn = through_projection(dq, 0, heads[0], w_ref)
    dxn += through_projection(dk, 1, heads[0], w_ref)
    dxn_out[...] = dxn + through_projection(dv, 2, heads[0], w_ref)


def na_rest_kernel(
    heads,
    q_ref,
    k_ref,
    dout_ref,
    v_ref,
    w_ref,
    heads_ref,
    wo_ref,
    m2_ref,
    dxn_out,
    merged_out,
):
    na_own_kernel(heads, q_ref, k_ref, dout_ref, v_ref, w_ref, dxn_out)
    merged = m2_ref[...].astype(f32)
    dim = C2 // GHEADS
    for h in range(GHEADS):
        merged += dot(heads_ref[h, :, 3 * dim :], wo_ref[h * dim : (h + 1) * dim])
    merged_out[...] = merged.astype(bf16)


def na_beside_kernel(
    k_one,
    v_one,
    k_two,
    v_two,
    hot_ref,
    before_ref,
    after_ref,
    left_ref,
    right_ref,
    q_halo_ref,
    w_ref,
    x_ref,
    dxn_one,
    dxn_two,
    dy_ref,
    perm_back_ref,
    grad_out,
    dout_halo_ref,
):
    lane = lax.broadcasted_iota(jnp.int32, (1, LANES), 1)
    is_mask = (lane >= NA_DIM) & (lane < DELTA_LANE)
    is_lse = (lane == LSE_LANE) | (lane == LSE_LANE + 1)
    fill_halo(dout_halo_ref, [before_ref, after_ref, left_ref, right_ref])
    hot = hot_ref[...].astype(f32)
    dk, dv = [], []
    for h in range(NA_HEADS):
        at = head_lanes(h)
        to = head_lanes(h % 2)
        k_ref, v_ref = (k_two, v_two) if h // 2 else (k_one, v_one)
        keys = jnp.where(is_mask, hot, k_ref[:, to].astype(f32)).astype(bf16)
        douts = dout_halo_ref[:, at]
        queries = jnp.where(
            is_lse, douts.astype(f32), q_halo_ref[:, at].astype(f32)
        ).astype(bf16)
        prob = jnp.exp(dot_last(keys, queries))
        dprob = dot_last(v_ref[:, to], douts)
        dk.append(dot((prob * dprob).astype(bf16), queries))
        dv.append(dot(prob.astype(bf16), douts))
    dxn = dxn_one[...] + dxn_two[...] + through_projection(dk, 1, 0, w_ref)
    dxn += through_projection(dv, 2, 0, w_ref)
    x = x_ref[...].astype(f32)
    grad = (dy_ref[...].astype(f32) + rms_back(x, rms_stat(x), dxn)).astype(bf16)
    grad_out[...] = dot(perm_back_ref[...], grad).astype(bf16)


def per_device(image, na_qkv, na_out, merge_one, merge_two, attn_qkv, attn_out, cotangent):
    rows, cols, _ = image.shape
    n_row = lax.axis_size("row")
    n_col = lax.axis_size("col")
    own = rows * cols
    tokens = own // 16
    dim = C2 // GHEADS
    owned = n_row * tokens
    scale = 1.0 / math.sqrt(dim)
    tables = token_tables(rows, cols)
    perm = jnp.asarray(tables["perm"], bf16)
    perm_back = jnp.asarray(tables["perm"].T, bf16)
    select = jnp.asarray(tables["select"], bf16)
    hot = jnp.asarray(tables["hot"], bf16)
    corner = jnp.asarray(tables["corner"], bf16)
    band_own = jnp.asarray(tables["band_own"], bf16)
    halo = tables["halo"]
    padded = halo.shape[0]

    flat = image.reshape(own, C0)
    before, after = row_halo(image[:REACH].reshape(-1, C0), image[-REACH:].reshape(-1, C0))
    left, right = call(
        corner_kernel,
        [((REACH * rows + 2 * ROWS, C0), bf16)] * 2,
        (
            corner,
            before,
            after,
            image[:, :REACH].reshape(-1, C0),
            image[:, -REACH:].reshape(-1, C0),
        ),
        megabytes=8,
    )
    left, right = neighbours(right, left, "col")
    at_row = lax.axis_index("row") * rows + jnp.asarray(halo[:, 0], jnp.int32)
    at_col = lax.axis_index("col") * cols + jnp.asarray(halo[:, 1], jnp.int32)
    inside = (at_row >= 0) & (at_row < rows * n_row) & (at_col >= 0) & (at_col < cols * n_col)
    lane = jnp.arange(LANES)
    mask_lane = (lane >= NA_DIM) & (lane < NA_DIM + rows + cols)
    band_halo = jnp.where(
        ~inside[:, None] & mask_lane[None], MASKED, jnp.asarray(tables["band_halo"], f32)
    ).astype(bf16)

    grad = cotangent.reshape(tokens, C2)
    dout = dot_last(grad, attn_out).astype(bf16)

    heads, m2, xp, q_one, q_two, k_one, k_two, v_one, v_two, q0_halo, a0 = call(
        na_forward_kernel,
        [
            ((GHEADS, tokens, 4 * dim), bf16),
            ((tokens, C2), bf16),
            ((own, C0), bf16),
            ((own, WIDE // 2), bf16),
            ((own, WIDE // 2), bf16),
            ((own + padded, WIDE // 2), bf16),
            ((own + padded, WIDE // 2), bf16),
            ((own + padded, WIDE // 2), bf16),
            ((own + padded, WIDE // 2), bf16),
            ((padded, WIDE), bf16),
            ((own, WIDE), bf16),
        ],
        (
            flat,
            perm,
            na_qkv,
            before,
            after,
            left,
            right,
            hot,
            band_own,
            band_halo,
            na_out,
            merge_one,
            merge_two,
            attn_qkv,
            dout,
        ),
        manual=(0, 1, 2, 7, 8, 9, 10, 11, 12, 13),
        cuts={13: (1, 3)},
        out_manual=range(1, 11),
        scratch=(pltpu.VMEM((padded, C0), bf16),),
        megabytes=40,
    )

    mine = all_to_all(heads, "row").reshape(owned, 4 * dim)
    keyval, queries = mine[:, : 2 * dim], mine[:, 2 * dim :]
    keyval = jnp.concatenate([keyval, across(keyval)], 0)
    queries = jnp.concatenate(along_z(queries), 0)
    keyval, share = lax.optimization_barrier((keyval, grad))
    share = jnp.broadcast_to(share[None], (n_row, tokens, C2))
    grad_row = all_to_all(share, "row").reshape(owned, C2)
    keyval = along_z(keyval)
    keyval_core = other_core(keyval)
    queries = [queries, across(queries)]
    keyval += keyval_core
    out_heads, stats, send = call(
        functools.partial(attention_kernel, scale),
        [((owned, dim), bf16), ((owned, LANES), f32), ((n_col, dim // n_col, C2 + LANES), bf16)],
        (grad_row, queries[0], *keyval),
    )
    shares = all_to_all(send, "col")
    dq = call(
        functools.partial(query_grad_kernel, scale),
        [((owned, dim), bf16)],
        (stats, queries[0], *keyval),
    )[0]
    queries += other_core(queries)
    part = queries[0].shape[0]
    back = call(
        functools.partial(key_grad_kernel, scale),
        [((owned, 4 * dim), bf16)],
        (column_order(), shares, dq, out_heads, keyval[0], *queries),
        scratch=(pltpu.VMEM((1, part), f32), pltpu.VMEM((1, part), f32)),
        smem=1,
    )[0]
    grad_wo = jnp.sum(shares[:, :, :C2].astype(f32), 0)
    back = all_to_all(back.reshape(n_row, tokens, 4 * dim), "row")

    dout0, dy0, top, bottom, left, right = call(
        merge_back_kernel,
        [((own, WIDE), bf16), ((own, C0), bf16)]
        + [((REACH * n, WIDE), bf16) for n in (cols, cols, rows, rows)],
        (back, attn_qkv, m2, grad, merge_two, merge_one, na_out, a0, q_one, q_two, select),
        manual=range(1, 11),
        out_manual=(1,),
        cuts={1: (1, 3), 4: (0, 4)},
        megabytes=32,
    )
    before, after = row_halo(top, bottom)
    half = NA_HEADS // 2
    dxn_one = call(
        functools.partial(na_own_kernel, range(half)),
        [((own, C0), f32)],
        (q_one, k_one, dout0, v_one, na_qkv),
        manual=(0, 1, 3, 4),
    )[0]
    before, after, dxn_one = lax.optimization_barrier((before, after, dxn_one))
    left, right = call(
        corner_kernel,
        [((left.shape[0] + 2 * ROWS, WIDE), bf16)] * 2,
        (corner, before, after, left, right),
        megabytes=8,
    )
    left, right, q_two = lax.optimization_barrier((left, right, q_two))
    left, right = neighbours(right, left, "col")
    dxn_two, merged = call(
        functools.partial(na_rest_kernel, range(half, NA_HEADS)),
        [((own, C0), f32), ((tokens, C2), bf16)],
        (q_two, k_two, dout0, v_two, na_qkv, back, attn_out, m2),
        manual=(0, 1, 3, 4, 6, 7),
        megabytes=20,
    )
    grad_image = call(
        na_beside_kernel,
        [((own, C0), bf16)],
        (
            Rows(k_one, own),
            Rows(v_one, own),
            Rows(k_two, own),
            Rows(v_two, own),
            hot,
            before,
            after,
            left,
            right,
            q0_halo,
            na_qkv,
            xp,
            dxn_one,
            dxn_two,
            dy0,
            perm_back,
        ),
        manual=(0, 1, 2, 3, 4, 9, 10, 11, 14, 15),
        scratch=(pltpu.VMEM((padded, WIDE), bf16),),
    )[0]
    return (
        merged.reshape(rows // 4, cols // 4, C2),
        grad_image.reshape(rows, cols, C0),
        grad_wo,
    )


def solution(mesh):
    return jax.shard_map(
        per_device,
        mesh=mesh,
        in_specs=(P("row", "col", None), P(), P(), P(), P(), P(), P(), P("row", "col", None)),
        out_specs=(P("row", "col", None), P("row", "col", None), P(("row", "col"), None)),
        check_vma=False,
    )
```

```python
import functools
import math

import jax
import jax.numpy as jnp
import numpy as np
from jax import lax
from jax.experimental import pallas as pl
from jax.experimental.pallas import tpu as pltpu
from jax.sharding import PartitionSpec as P

C0 = 256
C1 = 512
C2 = 1024
NA_HEADS = 4
GHEADS = 8
KERNEL = 7
REACH = KERNEL // 2
EPSILON = 1e-06
LANES = 128
NA_DIM = C0 // NA_HEADS
WIDE = NA_HEADS * LANES
MASKED = -1e15
ROWS = 16
DELTA_LANE = 112
LSE_LANE = 114

f32 = jnp.float32
bf16 = jnp.bfloat16


def dot(left, right):
    return lax.dot_general(left, right, (((1,), (0,)), ((), ())), preferred_element_type=f32)


def dot_last(left, right):
    return lax.dot_general(left, right, (((1,), (1,)), ((), ())), preferred_element_type=f32)


def dot_first(left, right):
    return lax.dot_general(left, right, (((0,), (0,)), ((), ())), preferred_element_type=f32)


def rms_stat(x):
    return lax.rsqrt(jnp.mean(x * x, -1, keepdims=True) + EPSILON)


def rms_back(x, scale, grad):
    return scale * grad - x * scale**3 * jnp.mean(grad * x, -1, keepdims=True)


def token_tables(rows, cols):
    grid = np.arange(rows * cols).reshape(rows // 4, 2, 2, cols // 4, 2, 2)
    order = grid.transpose(2, 5, 1, 4, 0, 3).reshape(-1)
    own_row, own_col = order // cols, order % cols
    outside = [(-99, -99)]
    side = [
        ((r0, r1), pad)
        for (r0, r1), pad in [((-REACH, 0), True), ((0, rows), False), ((rows, rows + REACH), True)]
    ]
    halo = [(r, c) for r in range(-REACH, 0) for c in range(cols)]
    halo += [(r, c) for r in range(rows, rows + REACH) for c in range(cols)]
    for first in (-REACH, cols):
        for (r0, r1), pad in side:
            part = [(r, c) for r in range(r0, r1) for c in range(first, first + REACH)]
            halo += part + outside * (-len(part) % ROWS)
    count = len(halo)
    padded = -(-count // LANES) * LANES
    halo = np.array(halo + outside * (padded - count))

    def band(row, col):
        near_row = np.abs(row[:, None] - np.arange(rows)[None]) <= REACH
        near_col = np.abs(col[:, None] - np.arange(cols)[None]) <= REACH
        return np.where(np.concatenate([near_row, near_col], 1), 0.0, MASKED)

    def lanes(part):
        table = np.zeros((part.shape[0], LANES), np.float32)
        table[:, NA_DIM : NA_DIM + part.shape[1]] = part
        return table

    hot = np.concatenate(
        [own_row[:, None] == np.arange(rows)[None], own_col[:, None] == np.arange(cols)[None]], 1
    ).astype(np.float32)
    perm = np.zeros((rows * cols, rows * cols), np.float32)
    perm[np.arange(rows * cols), order] = 1.0
    place = np.argsort(order)
    natural = np.arange(rows * cols).reshape(rows, cols)
    strips = [natural[:REACH], natural[-REACH:], natural[:, :REACH], natural[:, -REACH:]]
    wanted = place[np.concatenate([s.reshape(-1) for s in strips])]
    select = np.zeros((wanted.size, rows * cols), np.float32)
    select[np.arange(wanted.size), wanted] = 1.0
    corner = np.zeros((2 * ROWS, REACH * cols), np.float32)
    for i, first in enumerate((0, cols - REACH)):
        for r in range(REACH):
            for c in range(REACH):
                corner[i * ROWS + r * REACH + c, r * cols + first + c] = 1.0
    return dict(
        corner=corner,
        perm=perm,
        select=select,
        hot=lanes(hot),
        band_own=lanes(band(own_row, own_col)),
        band_halo=lanes(band(halo[:, 0], halo[:, 1])),
        halo=halo,
        count=count,
    )


def shifted(array, axis, move):
    count = lax.axis_size(axis)
    return lax.ppermute(array, axis, [(i, move(i)) for i in range(count)])


def neighbours(to_next, to_previous, axis):
    count = lax.axis_size(axis)
    up = [(i, i + 1) for i in range(count - 1)]
    down = [(j, i) for i, j in up]
    return lax.ppermute(to_next, axis, up), lax.ppermute(to_previous, axis, down)


def row_halo(top, bottom):
    return neighbours(bottom, top, "row")


def along_z(pair):
    count = lax.axis_size("col")
    return [pair] + [shifted(pair, "col", lambda i: (i + 4 * step) % count) for step in (1, 3, 2)]


def other_core(pieces):
    return [shifted(piece, "col", lambda i: i ^ 1) for piece in pieces]


def across(shard):
    return shifted(shard, "col", lambda i: i ^ 2)


def column_order():
    count = lax.axis_size("col")
    place = jnp.arange(count, dtype=jnp.int32)
    step = jnp.asarray([0, 1, 3, 2], jnp.int32)[place % 4]
    source = (lax.axis_index("col") + count - 4 * step) % count
    return source ^ (2 * ((place // 4) % 2)) ^ (place // 8)


def all_to_all(array, axis):
    return lax.all_to_all(array, axis, split_axis=0, concat_axis=0, tiled=True)


class Rows:
    def __init__(self, array, rows):
        self.array, self.rows = array, rows
        self.shape, self.dtype = (rows, *array.shape[1:]), array.dtype


class Held:
    def __init__(self, source, target, sems, cut):
        dim, count = cut
        size = target.shape[dim] // count
        self.copies = []
        self.parts = []
        for i in range(count):
            at = tuple(pl.ds(i * size, size) if d == dim else slice(None) for d in range(dim + 1))
            part = target.at[at] if count > 1 else target
            self.copies.append(
                pltpu.make_async_copy(source.at[at] if count > 1 else source, part, sems[i])
            )
            self.parts.append(part)
        self.target = target
        self.waiting = [True] * count
        for copy in self.copies:
            copy.start()

    def chunk(self, i):
        if self.waiting[i]:
            self.waiting[i] = False
            self.copies[i].wait()
        return self.parts[i]

    def ready(self):
        for i in range(len(self.copies)):
            self.chunk(i)
        return self.target

    def __getitem__(self, index):
        return self.ready()[index]

    @property
    def shape(self):
        return self.target.shape


class Plain:
    def __init__(self, target):
        self.target = target

    def ready(self):
        return self.target

    def send(self):
        pass

    def __getitem__(self, index):
        return self.target[index]

    def __setitem__(self, index, value):
        self.target[index] = value

    @property
    def shape(self):
        return self.target.shape


class Result(Plain):
    def __init__(self, source, target, sem):
        self.copy = pltpu.make_async_copy(source, target, sem)
        self.target = source
        self.started = False

    def send(self):
        if not self.started:
            self.started = True
            self.copy.start()


def take_from(items, count):
    return [items.pop(0) for _ in range(count)]


def call(kernel, outs, args, manual=(), out_manual=(), scratch=(), smem=0, cuts={}, megabytes=16):
    manual = sorted(i % len(args) for i in manual)
    out_manual = sorted(i % len(outs) for i in out_manual)
    cuts = {i % len(args): cut for i, cut in cuts.items()}
    cuts = [cuts.get(i, (0, 1)) for i in manual]
    total = sum(n for _, n in cuts)

    def body(*refs):
        refs = list(refs)
        take = functools.partial(take_from, refs)
        given, results, extra = take(len(args)), take(len(outs)), take(len(scratch))
        here, there = take(len(manual)), take(len(out_manual))
        sems_in, sems_out = take(2)
        sems = [sems_in.at[i] for i in range(total)]
        values = given[:smem] + [Plain(ref) for ref in given[smem:]]
        writes = [Plain(ref) for ref in results]
        for i, dst, cut in zip(manual, here, cuts):
            source = given[i].at[pl.ds(0, args[i].rows)] if isinstance(args[i], Rows) else given[i]
            values[i] = Held(source, dst, take_from(sems, cut[1]), cut)
        for n, (i, src) in enumerate(zip(out_manual, there)):
            writes[i] = Result(src, results[i], sems_out.at[n])
        kernel(*values, *writes, *extra)
        for i in out_manual:
            writes[i].send()
        for i in manual:
            values[i].ready()
        for i in out_manual:
            writes[i].copy.wait()

    def spec(i, far):
        return pl.BlockSpec(memory_space=pltpu.HBM if i in far else pltpu.VMEM)

    hbm = lambda a: pltpu.with_memory_space_constraint(a, pltpu.HBM)
    return pl.pallas_call(
        body,
        out_shape=[
            pltpu.HBM(*out) if i in out_manual else jax.ShapeDtypeStruct(*out)
            for i, out in enumerate(outs)
        ],
        in_specs=[pl.BlockSpec(memory_space=pltpu.SMEM)] * smem
        + [spec(i, manual) for i in range(smem, len(args))],
        out_specs=[spec(i, out_manual) for i in range(len(outs))],
        scratch_shapes=list(scratch)
        + [pltpu.VMEM(args[i].shape, args[i].dtype) for i in manual]
        + [pltpu.VMEM(*outs[i]) for i in out_manual]
        + [pltpu.SemaphoreType.DMA((max(total, 1),)), pltpu.SemaphoreType.DMA((max(len(out_manual), 1),))],
        compiler_params=pltpu.CompilerParams(vmem_limit_bytes=megabytes * 2**20),
    )(*[hbm(getattr(a, "array", a)) if i in manual else a for i, a in enumerate(args)])


def head_lanes(head):
    return slice(head * LANES, (head + 1) * LANES)


def two_parts(value):
    high = value.astype(bf16).astype(f32)
    return high, value - high


def at_lanes(base, lane, first, value):
    high, low = two_parts(value)
    return jnp.where(lane == first, -high, jnp.where(lane == first + 1, -low, base))


def head_of(pairs, head, section=0):
    first = section * C0 + (head // 2) * LANES
    pair = pairs[:, first : first + LANES]
    return pltpu.roll(pair, NA_DIM, 1) if head % 2 else pair


def as_pairs(heads):
    lane = lax.broadcasted_iota(jnp.int32, (1, LANES), 1)
    pairs = [
        jnp.where(lane < NA_DIM, heads[i], pltpu.roll(heads[i + 1], NA_DIM, 1))
        for i in range(0, len(heads), 2)
    ]
    return jnp.concatenate(pairs, 1).astype(bf16)


def fill_halo(target, parts):
    first = 0
    for part in parts:
        rows = part.shape[0]
        target[first : first + rows, :] = part[...]
        first += rows
    rest = target.shape[0] - first
    target[first:, :] = jnp.zeros((rest, target.shape[1]), target.dtype)


def corner_kernel(corner_ref, before_ref, after_ref, left_ref, right_ref, left_out, right_out):
    for i, (side, out) in enumerate([(left_ref, left_out), (right_ref, right_out)]):
        pick = corner_ref[i * ROWS : (i + 1) * ROWS]
        rows = side.shape[0]
        out[:ROWS] = dot(pick, before_ref[...]).astype(bf16)
        out[ROWS : ROWS + rows] = side[...]
        out[ROWS + rows :] = dot(pick, after_ref[...]).astype(bf16)


def na_forward_kernel(
    x_ref,
    perm_ref,
    w_ref,
    before_ref,
    after_ref,
    left_ref,
    right_ref,
    hot_ref,
    band_own_ref,
    band_halo_ref,
    w_out_ref,
    one_ref,
    two_ref,
    wqkv_ref,
    dout_ref,
    head_out,
    m2_out,
    x_out,
    q_one,
    q_two,
    k_one,
    k_two,
    v_one,
    v_two,
    q_halo_out,
    a0_out,
    halo_ref,
):
    own = x_ref.shape[0]
    x = dot(perm_ref[...], x_ref[...])
    x_out[...] = x.astype(bf16)
    x_out.send()
    xn = (x * rms_stat(x)).astype(bf16)
    fill_halo(halo_ref, [before_ref, after_ref, left_ref, right_ref])
    xh = halo_ref[...].astype(f32)
    xhn = (xh * rms_stat(xh)).astype(bf16)
    mine = dot(xn, w_ref[...])
    beside = dot(xhn, w_ref[...])
    lane = lax.broadcasted_iota(jnp.int32, (1, LANES), 1)
    is_lse = (lane == LSE_LANE) | (lane == LSE_LANE + 1)
    is_delta = (lane == DELTA_LANE) | (lane == DELTA_LANE + 1)
    one_lse = jnp.where(is_lse, 1.0, 0.0)
    one_delta = jnp.where(is_delta, 1.0, 0.0)
    hot = hot_ref[...].astype(f32)
    band_own = band_own_ref[...].astype(f32) + one_lse
    band_halo = band_halo_ref[...].astype(f32)
    channel = lane < NA_DIM
    scale = 1.0 / math.sqrt(NA_DIM)
    outs = []
    for h in range(NA_HEADS):
        at = head_lanes(h)
        to = head_lanes(h % 2)
        q_out, k_out, v_out = (q_two, k_two, v_two) if h // 2 else (q_one, k_one, v_one)
        q = jnp.where(channel, head_of(mine, h) * scale, hot)
        k_out[:own, to] = jnp.where(channel, head_of(mine, h, 1), band_own).astype(bf16)
        k_out[own:, to] = jnp.where(channel, head_of(beside, h, 1), band_halo + one_lse).astype(bf16)
        v_out[:own, to] = jnp.where(channel, head_of(mine, h, 2), one_delta).astype(bf16)
        v_out[own:, to] = jnp.where(channel, head_of(beside, h, 2), one_delta).astype(bf16)
        q_halo_out[:, at] = jnp.where(channel, head_of(beside, h) * scale, band_halo).astype(bf16)
        score = dot_last(q.astype(bf16), k_out[:, to])
        top = jnp.max(score, -1, keepdims=True)
        weight = jnp.exp(score - top).astype(bf16)
        out = dot(weight, v_out[:, to])
        norm = out[:, DELTA_LANE : DELTA_LANE + 1]
        q_out[:, to] = at_lanes(q, lane, LSE_LANE, top + jnp.log(norm)).astype(bf16)
        out = jnp.where(channel, out / norm, 0.0)
        a0_out[:, at] = out.astype(bf16)
        outs.append(out)
    for result in (q_one, q_two, k_one, k_two, v_one, v_two, q_halo_out, a0_out):
        result.send()
    y = (x + dot(as_pairs(outs), w_out_ref[...])).astype(bf16)
    quarter = own // 4
    m1 = dot(y[:quarter], one_ref[:C0])
    for part in range(1, 4):
        m1 += dot(y[part * quarter : (part + 1) * quarter], one_ref[part * C0 : (part + 1) * C0])
    m1 = m1.astype(bf16)
    tokens = own // 16
    m2 = dot(m1[:tokens], two_ref[:C1])
    for part in range(1, 4):
        m2 += dot(m1[part * tokens : (part + 1) * tokens], two_ref[part * C1 : (part + 1) * C1])
    m2 = m2.astype(bf16)
    m2_out[...] = m2
    m2_out.send()
    m2f = m2.astype(f32)
    mn = (m2f * rms_stat(m2f)).astype(bf16)
    dim = C2 // GHEADS
    for part, place in enumerate((2, 0, 1, 3)):
        if part < 3:
            value = dot(mn, wqkv_ref.chunk(part)[...]).astype(bf16)
        else:
            value = dout_ref[...]
        for h in range(GHEADS):
            head_out[h, :, place * dim : (place + 1) * dim] = value[:, h * dim : (h + 1) * dim]


def attention_kernel(scale, grad_ref, query_ref, *refs):
    pieces, (out_ref, col_ref, send_ref) = refs[:-3], refs[-3:]
    owned, dim = out_ref.shape
    query, dout = query_ref[:owned, :dim], query_ref[:owned, dim:]
    scores = [dot_last(query, piece[:, :dim]) * scale for piece in pieces]
    top = functools.reduce(jnp.maximum, [jnp.max(s, -1, keepdims=True) for s in scores])
    norm, out = 0.0, 0.0
    for score, piece in zip(scores, pieces):
        weight = jnp.exp(score - top)
        norm += jnp.sum(weight, -1, keepdims=True)
        out += dot(weight.astype(bf16), piece[:, dim:])
    out = (out / norm).astype(bf16)
    out_ref[...] = out
    lse = top + jnp.log(norm)
    delta = jnp.sum(dout.astype(f32) * out.astype(f32), -1, keepdims=True)
    lane = lax.broadcasted_iota(jnp.int32, (1, LANES), 1)
    col_ref[...] = jnp.where(lane == 0, lse, jnp.where(lane == 1, delta, 0.0))
    parts = [*two_parts(lse), *two_parts(delta)]
    table = jnp.zeros((query.shape[0], LANES), f32)
    for i, part in enumerate(parts):
        table = jnp.where(lane == i, part, table)
    table = table.T
    halves = query.shape[0] // LANES
    stats = [
        table[i : i + 1, half * LANES : (half + 1) * LANES]
        for i in range(len(parts))
        for half in range(halves)
    ]
    stats = jnp.concatenate(stats, 0).astype(bf16)
    partial = dot_first(out, grad_ref[...])
    count, rows = send_ref.shape[0], send_ref.shape[1]
    for i in range(count):
        send_ref[i, :, :C2] = partial[i * rows : (i + 1) * rows].astype(bf16)
        send_ref[i, :, C2:] = stats


def query_grad_kernel(scale, col_ref, query_ref, *refs):
    pieces, dq_ref = refs[:-1], refs[-1]
    owned, dim = dq_ref.shape
    query, dout = query_ref[:owned, :dim], query_ref[:owned, dim:]
    lse, delta = col_ref[:, 0:1], col_ref[:, 1:2]
    total = 0.0
    for piece in pieces:
        keys = piece[:, :dim]
        prob = jnp.exp(dot_last(query, keys) * scale - lse)
        dprob = dot_last(dout, piece[:, dim:])
        total += dot((prob * (dprob - delta)).astype(bf16), keys)
    dq_ref[...] = (total * scale).astype(bf16)


def key_grad_kernel(scale, order_ref, stat_ref, dq_ref, heads_ref, pair_ref, *refs):
    pieces, (out_ref, lse_in, delta_in) = refs[:-3], refs[-3:]
    owned, dim = dq_ref.shape
    halves = owned // LANES
    keys, values = pair_ref[:owned, :dim], pair_ref[:owned, dim:]
    stat_ref = stat_ref.ready()
    dk, dv = 0.0, 0.0
    for i, piece in enumerate(pieces):
        each = piece.shape[0] // owned
        for j in range(each):
            stats = stat_ref[order_ref[each * i + j]][:, C2:].astype(f32)
            for half in range(halves):
                at = slice(j * owned + half * LANES, j * owned + (half + 1) * LANES)
                take = lambda n: stats[n * halves + half : n * halves + half + 1]
                lse_in[:, at] = take(0) + take(1)
                delta_in[:, at] = take(2) + take(3)
        queries, douts = piece[:, :dim], piece[:, dim:]
        prob = jnp.exp(dot_last(keys, queries) * scale - lse_in[...])
        dprob = dot_last(values, douts)
        dk += dot((prob * (dprob - delta_in[...])).astype(bf16), queries)
        dv += dot(prob.astype(bf16), douts)
    out_ref[:, :dim] = dq_ref[...]
    out_ref[:, dim : 2 * dim] = (dk * scale).astype(bf16)
    out_ref[:, 2 * dim : 3 * dim] = dv.astype(bf16)
    out_ref[:, 3 * dim :] = heads_ref[...]


def merge_back_kernel(
    dqkv_ref,
    wqkv_ref,
    m2_ref,
    grad_ref,
    two_ref,
    one_ref,
    w_out_ref,
    a0_ref,
    q_one,
    q_two,
    select_ref,
    dout_out,
    dy_out,
    *strip_outs,
):
    dim = C2 // GHEADS
    dmn = 0.0
    for part in range(3):
        at = slice(part * dim, (part + 1) * dim)
        grads = jnp.concatenate([dqkv_ref[h, :, at] for h in range(GHEADS)], 1)
        dmn += dot_last(grads, wqkv_ref.chunk(part)[...])
    m2 = m2_ref[...].astype(f32)
    dm2 = (grad_ref[...].astype(f32) + rms_back(m2, rms_stat(m2), dmn)).astype(bf16)
    dm1 = [dot_last(dm2, two_ref.chunk(part)[...]).astype(bf16) for part in range(4)]
    du1 = dot_last(jnp.concatenate(dm1, 0), one_ref[...]).astype(bf16)
    dy = jnp.concatenate([du1[:, part * C0 : (part + 1) * C0] for part in range(4)], 0)
    dy_out[...] = dy
    dy_out.send()
    da0 = dot_last(dy, w_out_ref[...]).astype(bf16).astype(f32)
    lane = lax.broadcasted_iota(jnp.int32, (1, LANES), 1)
    is_lse = (lane == LSE_LANE) | (lane == LSE_LANE + 1)
    for h in range(NA_HEADS):
        at = head_lanes(h)
        mine = jnp.where(lane < NA_DIM, head_of(da0, h), 0.0)
        delta = jnp.sum(mine * a0_ref[:, at].astype(f32), -1, keepdims=True)
        q_ref = q_two if h // 2 else q_one
        mine = jnp.where(is_lse, q_ref[:, head_lanes(h % 2)].astype(f32), mine)
        dout_out[:, at] = at_lanes(mine, lane, DELTA_LANE, delta).astype(bf16)
    dout_out.send()
    strips = dot(select_ref[...], dout_out[...]).astype(bf16)
    first = 0
    for out in strip_outs:
        out[...] = strips[first : first + out.shape[0]]
        first += out.shape[0]


def through_projection(grads, section, first, w_ref):
    start = section * C0 + first * NA_DIM
    return dot_last(as_pairs(grads), w_ref[:, start : start + len(grads) * NA_DIM])


def na_own_kernel(heads, q_ref, k_ref, dout_ref, v_ref, w_ref, dxn_out):
    own = dout_ref.shape[0]
    dq, dk, dv = [], [], []
    for i, h in enumerate(heads):
        at = head_lanes(i)
        dout = dout_ref[:, head_lanes(h)]
        prob = jnp.exp(dot_last(q_ref[:, at], k_ref[:, at]))
        dprob = dot_last(dout, v_ref[:, at])
        dscore = (prob * dprob).astype(bf16)
        dq.append(dot(dscore, k_ref[:, at]) * (1.0 / math.sqrt(NA_DIM)))
        dk.append(dot_first(dscore[:, :own], q_ref[:, at]))
        dv.append(dot_first(prob[:, :own].astype(bf16), dout))
    dxn = through_projection(dq, 0, heads[0], w_ref)
    dxn += through_projection(dk, 1, heads[0], w_ref)
    dxn_out[...] = dxn + through_projection(dv, 2, heads[0], w_ref)


def na_rest_kernel(
    heads,
    q_ref,
    k_ref,
    dout_ref,
    v_ref,
    w_ref,
    heads_ref,
    wo_ref,
    m2_ref,
    dxn_out,
    merged_out,
):
    na_own_kernel(heads, q_ref, k_ref, dout_ref, v_ref, w_ref, dxn_out)
    merged = m2_ref[...].astype(f32)
    dim = C2 // GHEADS
    for h in range(GHEADS):
        merged += dot(heads_ref[h, :, 3 * dim :], wo_ref[h * dim : (h + 1) * dim])
    merged_out[...] = merged.astype(bf16)


def na_beside_kernel(
    hot_ref,
    q_halo_ref,
    k_one,
    v_one,
    k_two,
    v_two,
    before_ref,
    after_ref,
    left_ref,
    right_ref,
    w_ref,
    x_ref,
    dxn_one,
    dxn_two,
    dy_ref,
    perm_back_ref,
    grad_out,
    dout_halo_ref,
):
    lane = lax.broadcasted_iota(jnp.int32, (1, LANES), 1)
    is_mask = (lane >= NA_DIM) & (lane < DELTA_LANE)
    is_lse = (lane == LSE_LANE) | (lane == LSE_LANE + 1)
    fill_halo(dout_halo_ref, [before_ref, after_ref, left_ref, right_ref])
    hot = hot_ref[...].astype(f32)
    dk, dv = [], []
    for h in range(NA_HEADS):
        at = head_lanes(h)
        to = head_lanes(h % 2)
        k_ref, v_ref = (k_two, v_two) if h // 2 else (k_one, v_one)
        keys = jnp.where(is_mask, hot, k_ref[:, to].astype(f32)).astype(bf16)
        douts = dout_halo_ref[:, at]
        queries = jnp.where(
            is_lse, douts.astype(f32), q_halo_ref[:, at].astype(f32)
        ).astype(bf16)
        prob = jnp.exp(dot_last(keys, queries))
        dprob = dot_last(v_ref[:, to], douts)
        dk.append(dot((prob * dprob).astype(bf16), queries))
        dv.append(dot(prob.astype(bf16), douts))
    dxn = dxn_one[...] + dxn_two[...] + through_projection(dk, 1, 0, w_ref)
    dxn += through_projection(dv, 2, 0, w_ref)
    x = x_ref[...].astype(f32)
    grad = (dy_ref[...].astype(f32) + rms_back(x, rms_stat(x), dxn)).astype(bf16)
    grad_out[...] = dot(perm_back_ref[...], grad).astype(bf16)


def per_device(image, na_qkv, na_out, merge_one, merge_two, attn_qkv, attn_out, cotangent):
    rows, cols, _ = image.shape
    n_row = lax.axis_size("row")
    n_col = lax.axis_size("col")
    own = rows * cols
    tokens = own // 16
    dim = C2 // GHEADS
    owned = n_row * tokens
    scale = 1.0 / math.sqrt(dim)
    tables = token_tables(rows, cols)
    perm = jnp.asarray(tables["perm"], bf16)
    perm_back = jnp.asarray(tables["perm"].T, bf16)
    select = jnp.asarray(tables["select"], bf16)
    hot = jnp.asarray(tables["hot"], bf16)
    corner = jnp.asarray(tables["corner"], bf16)
    band_own = jnp.asarray(tables["band_own"], bf16)
    halo = tables["halo"]
    padded = halo.shape[0]

    flat = image.reshape(own, C0)
    before, after = row_halo(image[:REACH].reshape(-1, C0), image[-REACH:].reshape(-1, C0))
    left, right = call(
        corner_kernel,
        [((REACH * rows + 2 * ROWS, C0), bf16)] * 2,
        (
            corner,
            before,
            after,
            image[:, :REACH].reshape(-1, C0),
            image[:, -REACH:].reshape(-1, C0),
        ),
        megabytes=8,
    )
    left, right = neighbours(right, left, "col")
    at_row = lax.axis_index("row") * rows + jnp.asarray(halo[:, 0], jnp.int32)
    at_col = lax.axis_index("col") * cols + jnp.asarray(halo[:, 1], jnp.int32)
    inside = (at_row >= 0) & (at_row < rows * n_row) & (at_col >= 0) & (at_col < cols * n_col)
    lane = jnp.arange(LANES)
    mask_lane = (lane >= NA_DIM) & (lane < NA_DIM + rows + cols)
    band_halo = jnp.where(
        ~inside[:, None] & mask_lane[None], MASKED, jnp.asarray(tables["band_halo"], f32)
    ).astype(bf16)

    grad = cotangent.reshape(tokens, C2)
    dout = dot_last(grad, attn_out).astype(bf16)

    heads, m2, xp, q_one, q_two, k_one, k_two, v_one, v_two, q0_halo, a0 = call(
        na_forward_kernel,
        [
            ((GHEADS, tokens, 4 * dim), bf16),
            ((tokens, C2), bf16),
            ((own, C0), bf16),
            ((own, WIDE // 2), bf16),
            ((own, WIDE // 2), bf16),
            ((own + padded, WIDE // 2), bf16),
            ((own + padded, WIDE // 2), bf16),
            ((own + padded, WIDE // 2), bf16),
            ((own + padded, WIDE // 2), bf16),
            ((padded, WIDE), bf16),
            ((own, WIDE), bf16),
        ],
        (
            flat,
            perm,
            na_qkv,
            before,
            after,
            left,
            right,
            hot,
            band_own,
            band_halo,
            na_out,
            merge_one,
            merge_two,
            attn_qkv,
            dout,
        ),
        manual=(0, 1, 2, 7, 8, 9, 10, 11, 12, 13),
        cuts={13: (1, 3)},
        out_manual=range(1, 11),
        scratch=(pltpu.VMEM((padded, C0), bf16),),
        megabytes=40,
    )

    mine = all_to_all(heads, "row").reshape(owned, 4 * dim)
    keyval, queries = mine[:, : 2 * dim], mine[:, 2 * dim :]
    keyval = jnp.concatenate([keyval, across(keyval)], 0)
    queries = jnp.concatenate(along_z(queries), 0)
    keyval, share = lax.optimization_barrier((keyval, grad))
    share = jnp.broadcast_to(share[None], (n_row, tokens, C2))
    grad_row = all_to_all(share, "row").reshape(owned, C2)
    keyval = along_z(keyval)
    keyval_core = other_core(keyval)
    queries = [queries, across(queries)]
    keyval += keyval_core
    out_heads, stats, send = call(
        functools.partial(attention_kernel, scale),
        [((owned, dim), bf16), ((owned, LANES), f32), ((n_col, dim // n_col, C2 + LANES), bf16)],
        (grad_row, queries[0], *keyval),
    )
    shares = all_to_all(send, "col")
    dq = call(
        functools.partial(query_grad_kernel, scale),
        [((owned, dim), bf16)],
        (stats, queries[0], *keyval),
    )[0]
    queries += other_core(queries)
    part = queries[0].shape[0]
    back = call(
        functools.partial(key_grad_kernel, scale),
        [((owned, 4 * dim), bf16)],
        (column_order(), shares, dq, out_heads, keyval[0], *queries),
        scratch=(pltpu.VMEM((1, part), f32), pltpu.VMEM((1, part), f32)),
        smem=1,
    )[0]
    grad_wo = jnp.sum(shares[:, :, :C2].astype(f32), 0)
    back = all_to_all(back.reshape(n_row, tokens, 4 * dim), "row")

    dout0, dy0, top, bottom, left, right = call(
        merge_back_kernel,
        [((own, WIDE), bf16), ((own, C0), bf16)]
        + [((REACH * n, WIDE), bf16) for n in (cols, cols, rows, rows)],
        (back, attn_qkv, m2, grad, merge_two, merge_one, na_out, a0, q_one, q_two, select),
        manual=range(1, 11),
        out_manual=(1,),
        cuts={1: (1, 3), 4: (0, 4)},
        megabytes=32,
    )
    before, after = row_halo(top, bottom)
    half = NA_HEADS // 2
    dxn_one = call(
        functools.partial(na_own_kernel, range(half)),
        [((own, C0), f32)],
        (q_one, k_one, dout0, v_one, na_qkv),
        manual=(0, 1, 3, 4),
    )[0]
    before, after, dxn_one = lax.optimization_barrier((before, after, dxn_one))
    left, right = call(
        corner_kernel,
        [((left.shape[0] + 2 * ROWS, WIDE), bf16)] * 2,
        (corner, before, after, left, right),
        megabytes=8,
    )
    left, right, q_two = lax.optimization_barrier((left, right, q_two))
    left, right = neighbours(right, left, "col")
    dxn_two, merged = call(
        functools.partial(na_rest_kernel, range(half, NA_HEADS)),
        [((own, C0), f32), ((tokens, C2), bf16)],
        (q_two, k_two, dout0, v_two, na_qkv, back, attn_out, m2),
        manual=(0, 1, 3, 4, 6, 7),
        megabytes=20,
    )
    grad_image = call(
        na_beside_kernel,
        [((own, C0), bf16)],
        (
            hot,
            q0_halo,
            Rows(k_one, own),
            Rows(v_one, own),
            Rows(k_two, own),
            Rows(v_two, own),
            before,
            after,
            left,
            right,
            na_qkv,
            xp,
            dxn_one,
            dxn_two,
            dy0,
            perm_back,
        ),
        manual=(0, 1, 2, 3, 4, 5, 10, 11, 14, 15),
        scratch=(pltpu.VMEM((padded, WIDE), bf16),),
    )[0]
    return (
        merged.reshape(rows // 4, cols // 4, C2),
        grad_image.reshape(rows, cols, C0),
        grad_wo,
    )


def solution(mesh):
    return jax.shard_map(
        per_device,
        mesh=mesh,
        in_specs=(P("row", "col", None), P(), P(), P(), P(), P(), P(), P("row", "col", None)),
        out_specs=(P("row", "col", None), P("row", "col", None), P(("row", "col"), None)),
        check_vma=False,
    )
```

```python
import functools
import math

import jax
import jax.numpy as jnp
import numpy as np
from jax import lax
from jax.experimental import pallas as pl
from jax.experimental.pallas import tpu as pltpu
from jax.sharding import PartitionSpec as P

C0 = 256
C1 = 512
C2 = 1024
NA_HEADS = 4
GHEADS = 8
KERNEL = 7
REACH = KERNEL // 2
EPSILON = 1e-06
LANES = 128
NA_DIM = C0 // NA_HEADS
WIDE = NA_HEADS * LANES
MASKED = -1e15
ROWS = 16
DELTA_LANE = 112
LSE_LANE = 114

f32 = jnp.float32
bf16 = jnp.bfloat16


def dot(left, right):
    return lax.dot_general(left, right, (((1,), (0,)), ((), ())), preferred_element_type=f32)


def dot_last(left, right):
    return lax.dot_general(left, right, (((1,), (1,)), ((), ())), preferred_element_type=f32)


def dot_first(left, right):
    return lax.dot_general(left, right, (((0,), (0,)), ((), ())), preferred_element_type=f32)


def rms_stat(x):
    return lax.rsqrt(jnp.mean(x * x, -1, keepdims=True) + EPSILON)


def rms_back(x, scale, grad):
    return scale * grad - x * scale**3 * jnp.mean(grad * x, -1, keepdims=True)


def token_tables(rows, cols):
    grid = np.arange(rows * cols).reshape(rows // 4, 2, 2, cols // 4, 2, 2)
    order = grid.transpose(2, 5, 1, 4, 0, 3).reshape(-1)
    own_row, own_col = order // cols, order % cols
    outside = [(-99, -99)]
    side = [
        ((r0, r1), pad)
        for (r0, r1), pad in [((-REACH, 0), True), ((0, rows), False), ((rows, rows + REACH), True)]
    ]
    halo = [(r, c) for r in range(-REACH, 0) for c in range(cols)]
    halo += [(r, c) for r in range(rows, rows + REACH) for c in range(cols)]
    for first in (-REACH, cols):
        for (r0, r1), pad in side:
            part = [(r, c) for r in range(r0, r1) for c in range(first, first + REACH)]
            halo += part + outside * (-len(part) % ROWS)
    count = len(halo)
    padded = -(-count // LANES) * LANES
    halo = np.array(halo + outside * (padded - count))

    def band(row, col):
        near_row = np.abs(row[:, None] - np.arange(rows)[None]) <= REACH
        near_col = np.abs(col[:, None] - np.arange(cols)[None]) <= REACH
        return np.where(np.concatenate([near_row, near_col], 1), 0.0, MASKED)

    def lanes(part):
        table = np.zeros((part.shape[0], LANES), np.float32)
        table[:, NA_DIM : NA_DIM + part.shape[1]] = part
        return table

    hot = np.concatenate(
        [own_row[:, None] == np.arange(rows)[None], own_col[:, None] == np.arange(cols)[None]], 1
    ).astype(np.float32)
    perm = np.zeros((rows * cols, rows * cols), np.float32)
    perm[np.arange(rows * cols), order] = 1.0
    place = np.argsort(order)
    natural = np.arange(rows * cols).reshape(rows, cols)
    strips = [natural[:REACH], natural[-REACH:], natural[:, :REACH], natural[:, -REACH:]]
    wanted = place[np.concatenate([s.reshape(-1) for s in strips])]
    select = np.zeros((wanted.size, rows * cols), np.float32)
    select[np.arange(wanted.size), wanted] = 1.0
    corner = np.zeros((2 * ROWS, REACH * cols), np.float32)
    for i, first in enumerate((0, cols - REACH)):
        for r in range(REACH):
            for c in range(REACH):
                corner[i * ROWS + r * REACH + c, r * cols + first + c] = 1.0
    return dict(
        corner=corner,
        perm=perm,
        select=select,
        hot=lanes(hot),
        band_own=lanes(band(own_row, own_col)),
        band_halo=lanes(band(halo[:, 0], halo[:, 1])),
        halo=halo,
        count=count,
    )


def shifted(array, axis, move):
    count = lax.axis_size(axis)
    return lax.ppermute(array, axis, [(i, move(i)) for i in range(count)])


def neighbours(to_next, to_previous, axis):
    count = lax.axis_size(axis)
    up = [(i, i + 1) for i in range(count - 1)]
    down = [(j, i) for i, j in up]
    return lax.ppermute(to_next, axis, up), lax.ppermute(to_previous, axis, down)


def row_halo(top, bottom):
    return neighbours(bottom, top, "row")


def along_z(pair):
    count = lax.axis_size("col")
    return [pair] + [shifted(pair, "col", lambda i: (i + 4 * step) % count) for step in (1, 3, 2)]


def other_core(pieces):
    return [shifted(piece, "col", lambda i: i ^ 1) for piece in pieces]


def across(shard):
    return shifted(shard, "col", lambda i: i ^ 2)


def column_order():
    count = lax.axis_size("col")
    place = jnp.arange(count, dtype=jnp.int32)
    step = jnp.asarray([0, 1, 3, 2], jnp.int32)[place % 4]
    source = (lax.axis_index("col") + count - 4 * step) % count
    return source ^ (2 * ((place // 4) % 2)) ^ (place // 8)


def all_to_all(array, axis):
    return lax.all_to_all(array, axis, split_axis=0, concat_axis=0, tiled=True)


class Rows:
    def __init__(self, array, rows):
        self.array, self.rows = array, rows
        self.shape, self.dtype = (rows, *array.shape[1:]), array.dtype


class Held:
    def __init__(self, source, target, sems, cut):
        dim, count = cut
        size = target.shape[dim] // count
        self.copies = []
        self.parts = []
        for i in range(count):
            at = tuple(pl.ds(i * size, size) if d == dim else slice(None) for d in range(dim + 1))
            part = target.at[at] if count > 1 else target
            self.copies.append(
                pltpu.make_async_copy(source.at[at] if count > 1 else source, part, sems[i])
            )
            self.parts.append(part)
        self.target = target
        self.waiting = [True] * count
        for copy in self.copies:
            copy.start()

    def chunk(self, i):
        if self.waiting[i]:
            self.waiting[i] = False
            self.copies[i].wait()
        return self.parts[i]

    def ready(self):
        for i in range(len(self.copies)):
            self.chunk(i)
        return self.target

    def __getitem__(self, index):
        return self.ready()[index]

    @property
    def shape(self):
        return self.target.shape


class Plain:
    def __init__(self, target):
        self.target = target

    def ready(self):
        return self.target

    def send(self):
        pass

    def __getitem__(self, index):
        return self.target[index]

    def __setitem__(self, index, value):
        self.target[index] = value

    @property
    def shape(self):
        return self.target.shape


class Result(Plain):
    def __init__(self, source, target, sem):
        self.copy = pltpu.make_async_copy(source, target, sem)
        self.target = source
        self.started = False

    def send(self):
        if not self.started:
            self.started = True
            self.copy.start()


def take_from(items, count):
    return [items.pop(0) for _ in range(count)]


def call(kernel, outs, args, manual=(), out_manual=(), scratch=(), smem=0, cuts={}, megabytes=16):
    manual = sorted(i % len(args) for i in manual)
    out_manual = sorted(i % len(outs) for i in out_manual)
    cuts = {i % len(args): cut for i, cut in cuts.items()}
    cuts = [cuts.get(i, (0, 1)) for i in manual]
    total = sum(n for _, n in cuts)

    def body(*refs):
        refs = list(refs)
        take = functools.partial(take_from, refs)
        given, results, extra = take(len(args)), take(len(outs)), take(len(scratch))
        here, there = take(len(manual)), take(len(out_manual))
        sems_in, sems_out = take(2)
        sems = [sems_in.at[i] for i in range(total)]
        values = given[:smem] + [Plain(ref) for ref in given[smem:]]
        writes = [Plain(ref) for ref in results]
        for i, dst, cut in zip(manual, here, cuts):
            source = given[i].at[pl.ds(0, args[i].rows)] if isinstance(args[i], Rows) else given[i]
            values[i] = Held(source, dst, take_from(sems, cut[1]), cut)
        for n, (i, src) in enumerate(zip(out_manual, there)):
            writes[i] = Result(src, results[i], sems_out.at[n])
        kernel(*values, *writes, *extra)
        for i in out_manual:
            writes[i].send()
        for i in manual:
            values[i].ready()
        for i in out_manual:
            writes[i].copy.wait()

    def spec(i, far):
        return pl.BlockSpec(memory_space=pltpu.HBM if i in far else pltpu.VMEM)

    hbm = lambda a: pltpu.with_memory_space_constraint(a, pltpu.HBM)
    return pl.pallas_call(
        body,
        out_shape=[
            pltpu.HBM(*out) if i in out_manual else jax.ShapeDtypeStruct(*out)
            for i, out in enumerate(outs)
        ],
        in_specs=[pl.BlockSpec(memory_space=pltpu.SMEM)] * smem
        + [spec(i, manual) for i in range(smem, len(args))],
        out_specs=[spec(i, out_manual) for i in range(len(outs))],
        scratch_shapes=list(scratch)
        + [pltpu.VMEM(args[i].shape, args[i].dtype) for i in manual]
        + [pltpu.VMEM(*outs[i]) for i in out_manual]
        + [pltpu.SemaphoreType.DMA((max(total, 1),)), pltpu.SemaphoreType.DMA((max(len(out_manual), 1),))],
        compiler_params=pltpu.CompilerParams(vmem_limit_bytes=megabytes * 2**20),
    )(*[hbm(getattr(a, "array", a)) if i in manual else a for i, a in enumerate(args)])


def head_lanes(head):
    return slice(head * LANES, (head + 1) * LANES)


def two_parts(value):
    high = value.astype(bf16).astype(f32)
    return high, value - high


def at_lanes(base, lane, first, value):
    high, low = two_parts(value)
    return jnp.where(lane == first, -high, jnp.where(lane == first + 1, -low, base))


def head_of(pairs, head, section=0):
    first = section * C0 + (head // 2) * LANES
    pair = pairs[:, first : first + LANES]
    return pltpu.roll(pair, NA_DIM, 1) if head % 2 else pair


def as_pairs(heads):
    lane = lax.broadcasted_iota(jnp.int32, (1, LANES), 1)
    pairs = [
        jnp.where(lane < NA_DIM, heads[i], pltpu.roll(heads[i + 1], NA_DIM, 1))
        for i in range(0, len(heads), 2)
    ]
    return jnp.concatenate(pairs, 1).astype(bf16)


def fill_halo(target, parts):
    first = 0
    for part in parts:
        rows = part.shape[0]
        target[first : first + rows, :] = part[...]
        first += rows
    rest = target.shape[0] - first
    target[first:, :] = jnp.zeros((rest, target.shape[1]), target.dtype)


def corner_kernel(corner_ref, before_ref, after_ref, left_ref, right_ref, left_out, right_out):
    for i, (side, out) in enumerate([(left_ref, left_out), (right_ref, right_out)]):
        pick = corner_ref[i * ROWS : (i + 1) * ROWS]
        rows = side.shape[0]
        out[:ROWS] = dot(pick, before_ref[...]).astype(bf16)
        out[ROWS : ROWS + rows] = side[...]
        out[ROWS + rows :] = dot(pick, after_ref[...]).astype(bf16)


def na_forward_kernel(
    x_ref,
    perm_ref,
    w_ref,
    before_ref,
    after_ref,
    left_ref,
    right_ref,
    hot_ref,
    band_own_ref,
    band_halo_ref,
    w_out_ref,
    one_ref,
    two_ref,
    wqkv_ref,
    dout_ref,
    head_out,
    m2_out,
    x_out,
    q_one,
    q_two,
    k_one,
    k_two,
    v_one,
    v_two,
    q_halo_out,
    a0_out,
    halo_ref,
):
    own = x_ref.shape[0]
    x = dot(perm_ref[...], x_ref[...])
    x_out[...] = x.astype(bf16)
    x_out.send()
    xn = (x * rms_stat(x)).astype(bf16)
    fill_halo(halo_ref, [before_ref, after_ref, left_ref, right_ref])
    xh = halo_ref[...].astype(f32)
    xhn = (xh * rms_stat(xh)).astype(bf16)
    mine = dot(xn, w_ref[...])
    beside = dot(xhn, w_ref[...])
    lane = lax.broadcasted_iota(jnp.int32, (1, LANES), 1)
    is_lse = (lane == LSE_LANE) | (lane == LSE_LANE + 1)
    is_delta = (lane == DELTA_LANE) | (lane == DELTA_LANE + 1)
    one_lse = jnp.where(is_lse, 1.0, 0.0)
    one_delta = jnp.where(is_delta, 1.0, 0.0)
    hot = hot_ref[...].astype(f32)
    band_own = band_own_ref[...].astype(f32) + one_lse
    band_halo = band_halo_ref[...].astype(f32)
    channel = lane < NA_DIM
    scale = 1.0 / math.sqrt(NA_DIM)
    outs = []
    for h in range(NA_HEADS):
        at = head_lanes(h)
        to = head_lanes(h % 2)
        q_out, k_out, v_out = (q_two, k_two, v_two) if h // 2 else (q_one, k_one, v_one)
        q = jnp.where(channel, head_of(mine, h) * scale, hot)
        k_out[:own, to] = jnp.where(channel, head_of(mine, h, 1), band_own).astype(bf16)
        k_out[own:, to] = jnp.where(channel, head_of(beside, h, 1), band_halo + one_lse).astype(bf16)
        v_out[:own, to] = jnp.where(channel, head_of(mine, h, 2), one_delta).astype(bf16)
        v_out[own:, to] = jnp.where(channel, head_of(beside, h, 2), one_delta).astype(bf16)
        q_halo_out[:, at] = jnp.where(channel, head_of(beside, h) * scale, band_halo).astype(bf16)
        score = dot_last(q.astype(bf16), k_out[:, to])
        top = jnp.max(score, -1, keepdims=True)
        weight = jnp.exp(score - top).astype(bf16)
        out = dot(weight, v_out[:, to])
        norm = out[:, DELTA_LANE : DELTA_LANE + 1]
        q_out[:, to] = at_lanes(q, lane, LSE_LANE, top + jnp.log(norm)).astype(bf16)
        outs.append(out / norm)
    a0 = as_pairs(outs)
    a0_out[...] = a0
    for result in (q_one, q_two, k_one, k_two, v_one, v_two, q_halo_out, a0_out):
        result.send()
    y = (x + dot(a0, w_out_ref[...])).astype(bf16)
    quarter = own // 4
    m1 = dot(y[:quarter], one_ref[:C0])
    for part in range(1, 4):
        m1 += dot(y[part * quarter : (part + 1) * quarter], one_ref[part * C0 : (part + 1) * C0])
    m1 = m1.astype(bf16)
    tokens = own // 16
    m2 = dot(m1[:tokens], two_ref[:C1])
    for part in range(1, 4):
        m2 += dot(m1[part * tokens : (part + 1) * tokens], two_ref[part * C1 : (part + 1) * C1])
    m2 = m2.astype(bf16)
    m2_out[...] = m2
    m2_out.send()
    m2f = m2.astype(f32)
    mn = (m2f * rms_stat(m2f)).astype(bf16)
    dim = C2 // GHEADS
    for part, place in enumerate((2, 0, 1, 3)):
        if part < 3:
            value = dot(mn, wqkv_ref.chunk(part)[...]).astype(bf16)
        else:
            value = dout_ref[...]
        for h in range(GHEADS):
            head_out[h, :, place * dim : (place + 1) * dim] = value[:, h * dim : (h + 1) * dim]


def attention_kernel(scale, grad_ref, query_ref, *refs):
    pieces, (out_ref, col_ref, send_ref) = refs[:-3], refs[-3:]
    owned, dim = out_ref.shape
    query, dout = query_ref[:owned, :dim], query_ref[:owned, dim:]
    scores = [dot_last(query, piece[:, :dim]) * scale for piece in pieces]
    top = functools.reduce(jnp.maximum, [jnp.max(s, -1, keepdims=True) for s in scores])
    norm, out = 0.0, 0.0
    for score, piece in zip(scores, pieces):
        weight = jnp.exp(score - top)
        norm += jnp.sum(weight, -1, keepdims=True)
        out += dot(weight.astype(bf16), piece[:, dim:])
    out = (out / norm).astype(bf16)
    out_ref[...] = out
    lse = top + jnp.log(norm)
    delta = jnp.sum(dout.astype(f32) * out.astype(f32), -1, keepdims=True)
    lane = lax.broadcasted_iota(jnp.int32, (1, LANES), 1)
    col_ref[...] = jnp.where(lane == 0, lse, jnp.where(lane == 1, delta, 0.0))
    parts = [*two_parts(lse), *two_parts(delta)]
    table = jnp.zeros((query.shape[0], LANES), f32)
    for i, part in enumerate(parts):
        table = jnp.where(lane == i, part, table)
    table = table.T
    halves = query.shape[0] // LANES
    stats = [
        table[i : i + 1, half * LANES : (half + 1) * LANES]
        for i in range(len(parts))
        for half in range(halves)
    ]
    stats = jnp.concatenate(stats, 0).astype(bf16)
    partial = dot_first(out, grad_ref[...])
    count, rows = send_ref.shape[0], send_ref.shape[1]
    for i in range(count):
        send_ref[i, :, :C2] = partial[i * rows : (i + 1) * rows].astype(bf16)
        send_ref[i, :, C2:] = stats


def query_grad_kernel(scale, col_ref, query_ref, *refs):
    pieces, dq_ref = refs[:-1], refs[-1]
    owned, dim = dq_ref.shape
    query, dout = query_ref[:owned, :dim], query_ref[:owned, dim:]
    lse, delta = col_ref[:, 0:1], col_ref[:, 1:2]
    total = 0.0
    for piece in pieces:
        keys = piece[:, :dim]
        prob = jnp.exp(dot_last(query, keys) * scale - lse)
        dprob = dot_last(dout, piece[:, dim:])
        total += dot((prob * (dprob - delta)).astype(bf16), keys)
    dq_ref[...] = (total * scale).astype(bf16)


def key_grad_kernel(scale, order_ref, stat_ref, dq_ref, heads_ref, pair_ref, *refs):
    pieces, (out_ref, lse_in, delta_in) = refs[:-3], refs[-3:]
    owned, dim = dq_ref.shape
    halves = owned // LANES
    keys, values = pair_ref[:owned, :dim], pair_ref[:owned, dim:]
    stat_ref = stat_ref.ready()
    dk, dv = 0.0, 0.0
    for i, piece in enumerate(pieces):
        each = piece.shape[0] // owned
        for j in range(each):
            stats = stat_ref[order_ref[each * i + j]][:, C2:].astype(f32)
            for half in range(halves):
                at = slice(j * owned + half * LANES, j * owned + (half + 1) * LANES)
                take = lambda n: stats[n * halves + half : n * halves + half + 1]
                lse_in[:, at] = take(0) + take(1)
                delta_in[:, at] = take(2) + take(3)
        queries, douts = piece[:, :dim], piece[:, dim:]
        prob = jnp.exp(dot_last(keys, queries) * scale - lse_in[...])
        dprob = dot_last(values, douts)
        dk += dot((prob * (dprob - delta_in[...])).astype(bf16), queries)
        dv += dot(prob.astype(bf16), douts)
    out_ref[:, :dim] = dq_ref[...]
    out_ref[:, dim : 2 * dim] = (dk * scale).astype(bf16)
    out_ref[:, 2 * dim : 3 * dim] = dv.astype(bf16)
    out_ref[:, 3 * dim :] = heads_ref[...]


def merge_back_kernel(
    dqkv_ref,
    wqkv_ref,
    m2_ref,
    grad_ref,
    two_ref,
    one_ref,
    w_out_ref,
    a0_ref,
    q_one,
    q_two,
    select_ref,
    dout_out,
    dy_out,
    *strip_outs,
):
    dim = C2 // GHEADS
    dmn = 0.0
    for part in range(3):
        at = slice(part * dim, (part + 1) * dim)
        grads = jnp.concatenate([dqkv_ref[h, :, at] for h in range(GHEADS)], 1)
        dmn += dot_last(grads, wqkv_ref.chunk(part)[...])
    m2 = m2_ref[...].astype(f32)
    dm2 = (grad_ref[...].astype(f32) + rms_back(m2, rms_stat(m2), dmn)).astype(bf16)
    dm1 = [dot_last(dm2, two_ref.chunk(part)[...]).astype(bf16) for part in range(4)]
    du1 = dot_last(jnp.concatenate(dm1, 0), one_ref[...]).astype(bf16)
    dy = jnp.concatenate([du1[:, part * C0 : (part + 1) * C0] for part in range(4)], 0)
    dy_out[...] = dy
    dy_out.send()
    da0 = dot_last(dy, w_out_ref[...]).astype(bf16).astype(f32)
    a0 = a0_ref[...].astype(f32)
    lane = lax.broadcasted_iota(jnp.int32, (1, LANES), 1)
    is_lse = (lane == LSE_LANE) | (lane == LSE_LANE + 1)
    for h in range(NA_HEADS):
        at = head_lanes(h)
        mine = jnp.where(lane < NA_DIM, head_of(da0, h), 0.0)
        delta = jnp.sum(mine * head_of(a0, h), -1, keepdims=True)
        q_ref = q_two if h // 2 else q_one
        mine = jnp.where(is_lse, q_ref[:, head_lanes(h % 2)].astype(f32), mine)
        dout_out[:, at] = at_lanes(mine, lane, DELTA_LANE, delta).astype(bf16)
    dout_out.send()
    strips = dot(select_ref[...], dout_out[...]).astype(bf16)
    first = 0
    for out in strip_outs:
        out[...] = strips[first : first + out.shape[0]]
        first += out.shape[0]


def through_projection(grads, section, first, w_ref):
    start = section * C0 + first * NA_DIM
    return dot_last(as_pairs(grads), w_ref[:, start : start + len(grads) * NA_DIM])


def na_own_kernel(heads, q_ref, k_ref, dout_ref, v_ref, w_ref, dxn_out):
    own = dout_ref.shape[0]
    dq, dk, dv = [], [], []
    for i, h in enumerate(heads):
        at = head_lanes(i)
        dout = dout_ref[:, head_lanes(h)]
        prob = jnp.exp(dot_last(q_ref[:, at], k_ref[:, at]))
        dprob = dot_last(dout, v_ref[:, at])
        dscore = (prob * dprob).astype(bf16)
        dq.append(dot(dscore, k_ref[:, at]) * (1.0 / math.sqrt(NA_DIM)))
        dk.append(dot_first(dscore[:, :own], q_ref[:, at]))
        dv.append(dot_first(prob[:, :own].astype(bf16), dout))
    dxn = through_projection(dq, 0, heads[0], w_ref)
    dxn += through_projection(dk, 1, heads[0], w_ref)
    dxn_out[...] = dxn + through_projection(dv, 2, heads[0], w_ref)


def na_first_kernel(heads, q_ref, k_ref, dout_ref, v_ref, w_ref, part_ref, dxn_out, grad_out):
    na_own_kernel(heads, q_ref, k_ref, dout_ref, v_ref, w_ref, dxn_out)
    grad_out[...] = jnp.sum(part_ref[:, :, :C2].astype(f32), 0)


def na_rest_kernel(
    heads,
    q_ref,
    k_ref,
    dout_ref,
    v_ref,
    w_ref,
    heads_ref,
    wo_ref,
    m2_ref,
    dxn_out,
    merged_out,
):
    na_own_kernel(heads, q_ref, k_ref, dout_ref, v_ref, w_ref, dxn_out)
    merged = m2_ref[...].astype(f32)
    dim = C2 // GHEADS
    for h in range(GHEADS):
        merged += dot(heads_ref[h, :, 3 * dim :], wo_ref[h * dim : (h + 1) * dim])
    merged_out[...] = merged.astype(bf16)


def na_beside_kernel(
    hot_ref,
    q_halo_ref,
    k_one,
    v_one,
    k_two,
    v_two,
    before_ref,
    after_ref,
    left_ref,
    right_ref,
    w_ref,
    x_ref,
    dxn_one,
    dxn_two,
    dy_ref,
    perm_back_ref,
    grad_out,
    dout_halo_ref,
):
    lane = lax.broadcasted_iota(jnp.int32, (1, LANES), 1)
    is_mask = (lane >= NA_DIM) & (lane < DELTA_LANE)
    is_lse = (lane == LSE_LANE) | (lane == LSE_LANE + 1)
    fill_halo(dout_halo_ref, [before_ref, after_ref, left_ref, right_ref])
    hot = hot_ref[...].astype(f32)
    dk, dv = [], []
    for h in range(NA_HEADS):
        at = head_lanes(h)
        to = head_lanes(h % 2)
        k_ref, v_ref = (k_two, v_two) if h // 2 else (k_one, v_one)
        keys = jnp.where(is_mask, hot, k_ref[:, to].astype(f32)).astype(bf16)
        douts = dout_halo_ref[:, at]
        queries = jnp.where(
            is_lse, douts.astype(f32), q_halo_ref[:, at].astype(f32)
        ).astype(bf16)
        prob = jnp.exp(dot_last(keys, queries))
        dprob = dot_last(v_ref[:, to], douts)
        dk.append(dot((prob * dprob).astype(bf16), queries))
        dv.append(dot(prob.astype(bf16), douts))
    dxn = dxn_one[...] + dxn_two[...] + through_projection(dk, 1, 0, w_ref)
    dxn += through_projection(dv, 2, 0, w_ref)
    x = x_ref[...].astype(f32)
    grad = (dy_ref[...].astype(f32) + rms_back(x, rms_stat(x), dxn)).astype(bf16)
    grad_out[...] = dot(perm_back_ref[...], grad).astype(bf16)


def per_device(image, na_qkv, na_out, merge_one, merge_two, attn_qkv, attn_out, cotangent):
    rows, cols, _ = image.shape
    n_row = lax.axis_size("row")
    n_col = lax.axis_size("col")
    own = rows * cols
    tokens = own // 16
    dim = C2 // GHEADS
    owned = n_row * tokens
    scale = 1.0 / math.sqrt(dim)
    tables = token_tables(rows, cols)
    perm = jnp.asarray(tables["perm"], bf16)
    perm_back = jnp.asarray(tables["perm"].T, bf16)
    select = jnp.asarray(tables["select"], bf16)
    hot = jnp.asarray(tables["hot"], bf16)
    corner = jnp.asarray(tables["corner"], bf16)
    band_own = jnp.asarray(tables["band_own"], bf16)
    halo = tables["halo"]
    padded = halo.shape[0]

    flat = image.reshape(own, C0)
    before, after = row_halo(image[:REACH].reshape(-1, C0), image[-REACH:].reshape(-1, C0))
    left, right = call(
        corner_kernel,
        [((REACH * rows + 2 * ROWS, C0), bf16)] * 2,
        (
            corner,
            before,
            after,
            image[:, :REACH].reshape(-1, C0),
            image[:, -REACH:].reshape(-1, C0),
        ),
        megabytes=8,
    )
    left, right = neighbours(right, left, "col")
    at_row = lax.axis_index("row") * rows + jnp.asarray(halo[:, 0], jnp.int32)
    at_col = lax.axis_index("col") * cols + jnp.asarray(halo[:, 1], jnp.int32)
    inside = (at_row >= 0) & (at_row < rows * n_row) & (at_col >= 0) & (at_col < cols * n_col)
    lane = jnp.arange(LANES)
    mask_lane = (lane >= NA_DIM) & (lane < NA_DIM + rows + cols)
    band_halo = jnp.where(
        ~inside[:, None] & mask_lane[None], MASKED, jnp.asarray(tables["band_halo"], f32)
    ).astype(bf16)

    grad = cotangent.reshape(tokens, C2)
    dout = dot_last(grad, attn_out).astype(bf16)

    heads, m2, xp, q_one, q_two, k_one, k_two, v_one, v_two, q0_halo, a0 = call(
        na_forward_kernel,
        [
            ((GHEADS, tokens, 4 * dim), bf16),
            ((tokens, C2), bf16),
            ((own, C0), bf16),
            ((own, WIDE // 2), bf16),
            ((own, WIDE // 2), bf16),
            ((own + padded, WIDE // 2), bf16),
            ((own + padded, WIDE // 2), bf16),
            ((own + padded, WIDE // 2), bf16),
            ((own + padded, WIDE // 2), bf16),
            ((padded, WIDE), bf16),
            ((own, C0), bf16),
        ],
        (
            flat,
            perm,
            na_qkv,
            before,
            after,
            left,
            right,
            hot,
            band_own,
            band_halo,
            na_out,
            merge_one,
            merge_two,
            attn_qkv,
            dout,
        ),
        manual=(0, 1, 2, 7, 8, 9, 10, 11, 12, 13),
        cuts={13: (1, 3)},
        out_manual=range(1, 11),
        scratch=(pltpu.VMEM((padded, C0), bf16),),
        megabytes=40,
    )

    mine = all_to_all(heads, "row").reshape(owned, 4 * dim)
    keyval, queries = mine[:, : 2 * dim], mine[:, 2 * dim :]
    keyval = jnp.concatenate([keyval, across(keyval)], 0)
    queries = jnp.concatenate(along_z(queries), 0)
    keyval, share = lax.optimization_barrier((keyval, grad))
    share = jnp.broadcast_to(share[None], (n_row, tokens, C2))
    grad_row = all_to_all(share, "row").reshape(owned, C2)
    keyval = along_z(keyval)
    keyval_core = other_core(keyval)
    queries = [queries, across(queries)]
    keyval += keyval_core
    out_heads, stats, send = call(
        functools.partial(attention_kernel, scale),
        [((owned, dim), bf16), ((owned, LANES), f32), ((n_col, dim // n_col, C2 + LANES), bf16)],
        (grad_row, queries[0], *keyval),
    )
    shares = all_to_all(send, "col")
    dq = call(
        functools.partial(query_grad_kernel, scale),
        [((owned, dim), bf16)],
        (stats, queries[0], *keyval),
    )[0]
    queries += other_core(queries)
    part = queries[0].shape[0]
    back = call(
        functools.partial(key_grad_kernel, scale),
        [((owned, 4 * dim), bf16)],
        (column_order(), shares, dq, out_heads, keyval[0], *queries),
        scratch=(pltpu.VMEM((1, part), f32), pltpu.VMEM((1, part), f32)),
        smem=1,
    )[0]
    back = all_to_all(back.reshape(n_row, tokens, 4 * dim), "row")

    dout0, dy0, top, bottom, left, right = call(
        merge_back_kernel,
        [((own, WIDE), bf16), ((own, C0), bf16)]
        + [((REACH * n, WIDE), bf16) for n in (cols, cols, rows, rows)],
        (back, attn_qkv, m2, grad, merge_two, merge_one, na_out, a0, q_one, q_two, select),
        manual=range(1, 11),
        out_manual=(1,),
        cuts={1: (1, 3), 4: (0, 4)},
        megabytes=32,
    )
    before, after = row_halo(top, bottom)
    half = NA_HEADS // 2
    dxn_one, grad_wo = call(
        functools.partial(na_first_kernel, range(half)),
        [((own, C0), f32), ((dim // n_col, C2), f32)],
        (q_one, k_one, dout0, v_one, na_qkv, shares),
        manual=(0, 1, 3, 4, 5),
    )
    before, after, dxn_one = lax.optimization_barrier((before, after, dxn_one))
    left, right = call(
        corner_kernel,
        [((left.shape[0] + 2 * ROWS, WIDE), bf16)] * 2,
        (corner, before, after, left, right),
        megabytes=8,
    )
    left, right, q_two = lax.optimization_barrier((left, right, q_two))
    left, right = neighbours(right, left, "col")
    dxn_two, merged = call(
        functools.partial(na_rest_kernel, range(half, NA_HEADS)),
        [((own, C0), f32), ((tokens, C2), bf16)],
        (q_two, k_two, dout0, v_two, na_qkv, back, attn_out, m2),
        manual=(0, 1, 3, 4, 6, 7),
        megabytes=20,
    )
    grad_image = call(
        na_beside_kernel,
        [((own, C0), bf16)],
        (
            hot,
            q0_halo,
            Rows(k_one, own),
            Rows(v_one, own),
            Rows(k_two, own),
            Rows(v_two, own),
            before,
            after,
            left,
            right,
            na_qkv,
            xp,
            dxn_one,
            dxn_two,
            dy0,
            perm_back,
        ),
        manual=(0, 1, 2, 3, 4, 5, 10, 11, 14, 15),
        scratch=(pltpu.VMEM((padded, WIDE), bf16),),
    )[0]
    return (
        merged.reshape(rows // 4, cols // 4, C2),
        grad_image.reshape(rows, cols, C0),
        grad_wo,
    )


def solution(mesh):
    return jax.shard_map(
        per_device,
        mesh=mesh,
        in_specs=(P("row", "col", None), P(), P(), P(), P(), P(), P(), P("row", "col", None)),
        out_specs=(P("row", "col", None), P("row", "col", None), P(("row", "col"), None)),
        check_vma=False,
    )
```

```python
import functools
import math

import jax
import jax.numpy as jnp
import numpy as np
from jax import lax
from jax.experimental import pallas as pl
from jax.experimental.pallas import tpu as pltpu
from jax.sharding import PartitionSpec as P

C0 = 256
C1 = 512
C2 = 1024
NA_HEADS = 4
GHEADS = 8
KERNEL = 7
REACH = KERNEL // 2
EPSILON = 1e-06
LANES = 128
NA_DIM = C0 // NA_HEADS
WIDE = NA_HEADS * LANES
MASKED = -1e15
ROWS = 16
DELTA_LANE = 112
LSE_LANE = 114

f32 = jnp.float32
bf16 = jnp.bfloat16


def dot(left, right):
    return lax.dot_general(left, right, (((1,), (0,)), ((), ())), preferred_element_type=f32)


def dot_last(left, right):
    return lax.dot_general(left, right, (((1,), (1,)), ((), ())), preferred_element_type=f32)


def dot_first(left, right):
    return lax.dot_general(left, right, (((0,), (0,)), ((), ())), preferred_element_type=f32)


def rms_stat(x):
    return lax.rsqrt(jnp.mean(x * x, -1, keepdims=True) + EPSILON)


def rms_back(x, scale, grad):
    return scale * grad - x * scale**3 * jnp.mean(grad * x, -1, keepdims=True)


def token_tables(rows, cols):
    grid = np.arange(rows * cols).reshape(rows // 4, 2, 2, cols // 4, 2, 2)
    order = grid.transpose(2, 5, 1, 4, 0, 3).reshape(-1)
    own_row, own_col = order // cols, order % cols
    outside = [(-99, -99)]
    side = [
        ((r0, r1), pad)
        for (r0, r1), pad in [((-REACH, 0), True), ((0, rows), False), ((rows, rows + REACH), True)]
    ]
    halo = [(r, c) for r in range(-REACH, 0) for c in range(cols)]
    halo += [(r, c) for r in range(rows, rows + REACH) for c in range(cols)]
    for first in (-REACH, cols):
        for (r0, r1), pad in side:
            part = [(r, c) for r in range(r0, r1) for c in range(first, first + REACH)]
            halo += part + outside * (-len(part) % ROWS)
    count = len(halo)
    padded = -(-count // LANES) * LANES
    halo = np.array(halo + outside * (padded - count))

    def band(row, col):
        near_row = np.abs(row[:, None] - np.arange(rows)[None]) <= REACH
        near_col = np.abs(col[:, None] - np.arange(cols)[None]) <= REACH
        return np.where(np.concatenate([near_row, near_col], 1), 0.0, MASKED)

    def lanes(part):
        table = np.zeros((part.shape[0], LANES), np.float32)
        table[:, NA_DIM : NA_DIM + part.shape[1]] = part
        return table

    hot = np.concatenate(
        [own_row[:, None] == np.arange(rows)[None], own_col[:, None] == np.arange(cols)[None]], 1
    ).astype(np.float32)
    perm = np.zeros((rows * cols, rows * cols), np.float32)
    perm[np.arange(rows * cols), order] = 1.0
    place = np.argsort(order)
    natural = np.arange(rows * cols).reshape(rows, cols)
    strips = [natural[:REACH], natural[-REACH:], natural[:, :REACH], natural[:, -REACH:]]
    wanted = place[np.concatenate([s.reshape(-1) for s in strips])]
    select = np.zeros((wanted.size, rows * cols), np.float32)
    select[np.arange(wanted.size), wanted] = 1.0
    corner = np.zeros((2 * ROWS, REACH * cols), np.float32)
    for i, first in enumerate((0, cols - REACH)):
        for r in range(REACH):
            for c in range(REACH):
                corner[i * ROWS + r * REACH + c, r * cols + first + c] = 1.0
    return dict(
        corner=corner,
        perm=perm,
        select=select,
        hot=lanes(hot),
        band_own=lanes(band(own_row, own_col)),
        band_halo=lanes(band(halo[:, 0], halo[:, 1])),
        halo=halo,
        count=count,
    )


def shifted(array, axis, move):
    count = lax.axis_size(axis)
    return lax.ppermute(array, axis, [(i, move(i)) for i in range(count)])


def neighbours(to_next, to_previous, axis):
    count = lax.axis_size(axis)
    up = [(i, i + 1) for i in range(count - 1)]
    down = [(j, i) for i, j in up]
    return lax.ppermute(to_next, axis, up), lax.ppermute(to_previous, axis, down)


def row_halo(top, bottom):
    return neighbours(bottom, top, "row")


def along_z(pair):
    count = lax.axis_size("col")
    return [pair] + [shifted(pair, "col", lambda i: (i + 4 * step) % count) for step in (1, 3, 2)]


def other_core(pieces):
    return [shifted(piece, "col", lambda i: i ^ 1) for piece in pieces]


def across(shard):
    return shifted(shard, "col", lambda i: i ^ 2)


def column_order():
    count = lax.axis_size("col")
    place = jnp.arange(count, dtype=jnp.int32)
    step = jnp.asarray([0, 1, 3, 2], jnp.int32)[place % 4]
    source = (lax.axis_index("col") + count - 4 * step) % count
    return source ^ (2 * ((place // 4) % 2)) ^ (place // 8)


def all_to_all(array, axis):
    return lax.all_to_all(array, axis, split_axis=0, concat_axis=0, tiled=True)


class Rows:
    def __init__(self, array, rows):
        self.array, self.rows = array, rows
        self.shape, self.dtype = (rows, *array.shape[1:]), array.dtype


class Held:
    def __init__(self, source, target, sems, cut):
        dim, count = cut
        size = target.shape[dim] // count
        self.copies = []
        self.parts = []
        for i in range(count):
            at = tuple(pl.ds(i * size, size) if d == dim else slice(None) for d in range(dim + 1))
            part = target.at[at] if count > 1 else target
            self.copies.append(
                pltpu.make_async_copy(source.at[at] if count > 1 else source, part, sems[i])
            )
            self.parts.append(part)
        self.target = target
        self.waiting = [True] * count
        for copy in self.copies:
            copy.start()

    def chunk(self, i):
        if self.waiting[i]:
            self.waiting[i] = False
            self.copies[i].wait()
        return self.parts[i]

    def ready(self):
        for i in range(len(self.copies)):
            self.chunk(i)
        return self.target

    def __getitem__(self, index):
        return self.ready()[index]

    @property
    def shape(self):
        return self.target.shape


class Plain:
    def __init__(self, target):
        self.target = target

    def ready(self):
        return self.target

    def send(self):
        pass

    def __getitem__(self, index):
        return self.target[index]

    def __setitem__(self, index, value):
        self.target[index] = value

    @property
    def shape(self):
        return self.target.shape


class Result(Plain):
    def __init__(self, source, target, sem):
        self.copy = pltpu.make_async_copy(source, target, sem)
        self.target = source
        self.started = False

    def send(self):
        if not self.started:
            self.started = True
            self.copy.start()


def take_from(items, count):
    return [items.pop(0) for _ in range(count)]


def call(kernel, outs, args, manual=(), out_manual=(), scratch=(), smem=0, cuts={}, megabytes=16):
    manual = sorted(i % len(args) for i in manual)
    out_manual = sorted(i % len(outs) for i in out_manual)
    cuts = {i % len(args): cut for i, cut in cuts.items()}
    cuts = [cuts.get(i, (0, 1)) for i in manual]
    total = sum(n for _, n in cuts)

    def body(*refs):
        refs = list(refs)
        take = functools.partial(take_from, refs)
        given, results, extra = take(len(args)), take(len(outs)), take(len(scratch))
        here, there = take(len(manual)), take(len(out_manual))
        sems_in, sems_out = take(2)
        sems = [sems_in.at[i] for i in range(total)]
        values = given[:smem] + [Plain(ref) for ref in given[smem:]]
        writes = [Plain(ref) for ref in results]
        for i, dst, cut in zip(manual, here, cuts):
            source = given[i].at[pl.ds(0, args[i].rows)] if isinstance(args[i], Rows) else given[i]
            values[i] = Held(source, dst, take_from(sems, cut[1]), cut)
        for n, (i, src) in enumerate(zip(out_manual, there)):
            writes[i] = Result(src, results[i], sems_out.at[n])
        kernel(*values, *writes, *extra)
        for i in out_manual:
            writes[i].send()
        for i in manual:
            values[i].ready()
        for i in out_manual:
            writes[i].copy.wait()

    def spec(i, far):
        return pl.BlockSpec(memory_space=pltpu.HBM if i in far else pltpu.VMEM)

    hbm = lambda a: pltpu.with_memory_space_constraint(a, pltpu.HBM)
    return pl.pallas_call(
        body,
        out_shape=[
            pltpu.HBM(*out) if i in out_manual else jax.ShapeDtypeStruct(*out)
            for i, out in enumerate(outs)
        ],
        in_specs=[pl.BlockSpec(memory_space=pltpu.SMEM)] * smem
        + [spec(i, manual) for i in range(smem, len(args))],
        out_specs=[spec(i, out_manual) for i in range(len(outs))],
        scratch_shapes=list(scratch)
        + [pltpu.VMEM(args[i].shape, args[i].dtype) for i in manual]
        + [pltpu.VMEM(*outs[i]) for i in out_manual]
        + [pltpu.SemaphoreType.DMA((max(total, 1),)), pltpu.SemaphoreType.DMA((max(len(out_manual), 1),))],
        compiler_params=pltpu.CompilerParams(vmem_limit_bytes=megabytes * 2**20),
    )(*[hbm(getattr(a, "array", a)) if i in manual else a for i, a in enumerate(args)])


def head_lanes(head):
    return slice(head * LANES, (head + 1) * LANES)


def two_parts(value):
    high = value.astype(bf16).astype(f32)
    return high, value - high


def at_lanes(base, lane, first, value):
    high, low = two_parts(value)
    return jnp.where(lane == first, -high, jnp.where(lane == first + 1, -low, base))


def head_of(pairs, head, section=0):
    first = section * C0 + (head // 2) * LANES
    pair = pairs[:, first : first + LANES]
    return pltpu.roll(pair, NA_DIM, 1) if head % 2 else pair


def as_pairs(heads):
    lane = lax.broadcasted_iota(jnp.int32, (1, LANES), 1)
    pairs = [
        jnp.where(lane < NA_DIM, heads[i], pltpu.roll(heads[i + 1], NA_DIM, 1))
        for i in range(0, len(heads), 2)
    ]
    return jnp.concatenate(pairs, 1).astype(bf16)


def fill_halo(target, parts):
    first = 0
    for part in parts:
        rows = part.shape[0]
        target[first : first + rows, :] = part[...]
        first += rows
    rest = target.shape[0] - first
    target[first:, :] = jnp.zeros((rest, target.shape[1]), target.dtype)


def corner_kernel(corner_ref, before_ref, after_ref, left_ref, right_ref, left_out, right_out):
    for i, (side, out) in enumerate([(left_ref, left_out), (right_ref, right_out)]):
        pick = corner_ref[i * ROWS : (i + 1) * ROWS]
        rows = side.shape[0]
        out[:ROWS] = dot(pick, before_ref[...]).astype(bf16)
        out[ROWS : ROWS + rows] = side[...]
        out[ROWS + rows :] = dot(pick, after_ref[...]).astype(bf16)


def na_forward_kernel(
    x_ref,
    perm_ref,
    w_ref,
    before_ref,
    after_ref,
    left_ref,
    right_ref,
    hot_ref,
    band_own_ref,
    band_halo_ref,
    w_out_ref,
    one_ref,
    two_ref,
    wqkv_ref,
    dout_ref,
    head_out,
    m2_out,
    x_out,
    q_one,
    q_two,
    k_one,
    k_two,
    v_one,
    v_two,
    q_halo_out,
    a0_out,
    halo_ref,
):
    own = x_ref.shape[0]
    x = dot(perm_ref[...], x_ref[...])
    x_out[...] = x.astype(bf16)
    x_out.send()
    xn = (x * rms_stat(x)).astype(bf16)
    fill_halo(halo_ref, [before_ref, after_ref, left_ref, right_ref])
    xh = halo_ref[...].astype(f32)
    xhn = (xh * rms_stat(xh)).astype(bf16)
    mine = dot(xn, w_ref[...])
    beside = dot(xhn, w_ref[...])
    lane = lax.broadcasted_iota(jnp.int32, (1, LANES), 1)
    is_lse = (lane == LSE_LANE) | (lane == LSE_LANE + 1)
    is_delta = (lane == DELTA_LANE) | (lane == DELTA_LANE + 1)
    one_lse = jnp.where(is_lse, 1.0, 0.0)
    one_delta = jnp.where(is_delta, 1.0, 0.0)
    hot = hot_ref[...].astype(f32)
    band_own = band_own_ref[...].astype(f32) + one_lse
    band_halo = band_halo_ref[...].astype(f32)
    channel = lane < NA_DIM
    scale = 1.0 / math.sqrt(NA_DIM)
    outs = []
    for h in range(NA_HEADS):
        at = head_lanes(h)
        to = head_lanes(h % 2)
        q_out, k_out, v_out = (q_two, k_two, v_two) if h // 2 else (q_one, k_one, v_one)
        q = jnp.where(channel, head_of(mine, h) * scale, hot)
        k_out[:own, to] = jnp.where(channel, head_of(mine, h, 1), band_own).astype(bf16)
        k_out[own:, to] = jnp.where(channel, head_of(beside, h, 1), band_halo + one_lse).astype(bf16)
        v_out[:own, to] = jnp.where(channel, head_of(mine, h, 2), one_delta).astype(bf16)
        v_out[own:, to] = jnp.where(channel, head_of(beside, h, 2), one_delta).astype(bf16)
        q_halo_out[:, at] = jnp.where(channel, head_of(beside, h) * scale, band_halo).astype(bf16)
        score = dot_last(q.astype(bf16), k_out[:, to])
        top = jnp.max(score, -1, keepdims=True)
        weight = jnp.exp(score - top).astype(bf16)
        out = dot(weight, v_out[:, to])
        norm = out[:, DELTA_LANE : DELTA_LANE + 1]
        q_out[:, to] = at_lanes(q, lane, LSE_LANE, top + jnp.log(norm)).astype(bf16)
        outs.append(out / norm)
    a0 = as_pairs(outs)
    a0_out[...] = a0
    for result in (q_one, q_two, k_one, k_two, v_one, v_two, q_halo_out, a0_out):
        result.send()
    y = (x + dot(a0, w_out_ref[...])).astype(bf16)
    quarter = own // 4
    m1 = dot(y[:quarter], one_ref[:C0])
    for part in range(1, 4):
        m1 += dot(y[part * quarter : (part + 1) * quarter], one_ref[part * C0 : (part + 1) * C0])
    m1 = m1.astype(bf16)
    tokens = own // 16
    m2 = dot(m1[:tokens], two_ref[:C1])
    for part in range(1, 4):
        m2 += dot(m1[part * tokens : (part + 1) * tokens], two_ref[part * C1 : (part + 1) * C1])
    m2 = m2.astype(bf16)
    m2_out[...] = m2
    m2_out.send()
    m2f = m2.astype(f32)
    mn = (m2f * rms_stat(m2f)).astype(bf16)
    dim = C2 // GHEADS
    for part, place in enumerate((2, 0, 1, 3)):
        if part < 3:
            value = dot(mn, wqkv_ref.chunk(part)[...]).astype(bf16)
        else:
            value = dout_ref[...]
        for h in range(GHEADS):
            head_out[h, :, place * dim : (place + 1) * dim] = value[:, h * dim : (h + 1) * dim]


def attention_kernel(scale, grad_ref, query_ref, *refs):
    pieces, (out_ref, col_ref, send_ref) = refs[:-3], refs[-3:]
    owned, dim = out_ref.shape
    query, dout = query_ref[:owned, :dim], query_ref[:owned, dim:]
    scores = [dot_last(query, piece[:, :dim]) * scale for piece in pieces]
    top = functools.reduce(jnp.maximum, [jnp.max(s, -1, keepdims=True) for s in scores])
    norm, out = 0.0, 0.0
    for score, piece in zip(scores, pieces):
        weight = jnp.exp(score - top)
        norm += jnp.sum(weight, -1, keepdims=True)
        out += dot(weight.astype(bf16), piece[:, dim:])
    out = (out / norm).astype(bf16)
    out_ref[...] = out
    lse = top + jnp.log(norm)
    delta = jnp.sum(dout.astype(f32) * out.astype(f32), -1, keepdims=True)
    lane = lax.broadcasted_iota(jnp.int32, (1, LANES), 1)
    col_ref[...] = jnp.where(lane == 0, lse, jnp.where(lane == 1, delta, 0.0))
    parts = [*two_parts(lse), *two_parts(delta)]
    table = jnp.zeros((query.shape[0], LANES), f32)
    for i, part in enumerate(parts):
        table = jnp.where(lane == i, part, table)
    table = table.T
    halves = query.shape[0] // LANES
    stats = [
        table[i : i + 1, half * LANES : (half + 1) * LANES]
        for i in range(len(parts))
        for half in range(halves)
    ]
    stats = jnp.concatenate(stats, 0).astype(bf16)
    partial = dot_first(out, grad_ref[...])
    count, rows = send_ref.shape[0], send_ref.shape[1]
    for i in range(count):
        send_ref[i, :, :C2] = partial[i * rows : (i + 1) * rows].astype(bf16)
        send_ref[i, :, C2:] = stats


def query_grad_kernel(scale, col_ref, query_ref, *refs):
    pieces, dq_ref = refs[:-1], refs[-1]
    owned, dim = dq_ref.shape
    query, dout = query_ref[:owned, :dim], query_ref[:owned, dim:]
    lse, delta = col_ref[:, 0:1], col_ref[:, 1:2]
    total = 0.0
    for piece in pieces:
        keys = piece[:, :dim]
        prob = jnp.exp(dot_last(query, keys) * scale - lse)
        dprob = dot_last(dout, piece[:, dim:])
        total += dot((prob * (dprob - delta)).astype(bf16), keys)
    dq_ref[...] = (total * scale).astype(bf16)


def key_grad_kernel(scale, order_ref, stat_ref, dq_ref, heads_ref, pair_ref, *refs):
    pieces, (out_ref, lse_in, delta_in) = refs[:-3], refs[-3:]
    owned, dim = dq_ref.shape
    halves = owned // LANES
    keys, values = pair_ref[:owned, :dim], pair_ref[:owned, dim:]
    stat_ref = stat_ref.ready()
    dk, dv = 0.0, 0.0
    for i, piece in enumerate(pieces):
        each = piece.shape[0] // owned
        for j in range(each):
            stats = stat_ref[order_ref[each * i + j]][:, C2:].astype(f32)
            for half in range(halves):
                at = slice(j * owned + half * LANES, j * owned + (half + 1) * LANES)
                take = lambda n: stats[n * halves + half : n * halves + half + 1]
                lse_in[:, at] = take(0) + take(1)
                delta_in[:, at] = take(2) + take(3)
        queries, douts = piece[:, :dim], piece[:, dim:]
        prob = jnp.exp(dot_last(keys, queries) * scale - lse_in[...])
        dprob = dot_last(values, douts)
        dk += dot((prob * (dprob - delta_in[...])).astype(bf16), queries)
        dv += dot(prob.astype(bf16), douts)
    out_ref[:, :dim] = dq_ref[...]
    out_ref[:, dim : 2 * dim] = (dk * scale).astype(bf16)
    out_ref[:, 2 * dim : 3 * dim] = dv.astype(bf16)
    out_ref[:, 3 * dim :] = heads_ref[...]


def merge_back_kernel(
    dqkv_ref,
    wqkv_ref,
    m2_ref,
    grad_ref,
    two_ref,
    one_ref,
    w_out_ref,
    a0_ref,
    q_one,
    q_two,
    select_ref,
    dout_out,
    dy_out,
    *strip_outs,
):
    dim = C2 // GHEADS
    dmn = 0.0
    for part in range(3):
        at = slice(part * dim, (part + 1) * dim)
        grads = jnp.concatenate([dqkv_ref[h, :, at] for h in range(GHEADS)], 1)
        dmn += dot_last(grads, wqkv_ref.chunk(part)[...])
    m2 = m2_ref[...].astype(f32)
    dm2 = (grad_ref[...].astype(f32) + rms_back(m2, rms_stat(m2), dmn)).astype(bf16)
    dm1 = [dot_last(dm2, two_ref.chunk(part)[...]).astype(bf16) for part in range(4)]
    du1 = dot_last(jnp.concatenate(dm1, 0), one_ref[...]).astype(bf16)
    dy = jnp.concatenate([du1[:, part * C0 : (part + 1) * C0] for part in range(4)], 0)
    dy_out[...] = dy
    dy_out.send()
    da0 = dot_last(dy, w_out_ref[...]).astype(bf16).astype(f32)
    a0 = a0_ref[...].astype(f32)
    lane = lax.broadcasted_iota(jnp.int32, (1, LANES), 1)
    is_lse = (lane == LSE_LANE) | (lane == LSE_LANE + 1)
    for h in range(NA_HEADS):
        at = head_lanes(h)
        mine = jnp.where(lane < NA_DIM, head_of(da0, h), 0.0)
        delta = jnp.sum(mine * head_of(a0, h), -1, keepdims=True)
        q_ref = q_two if h // 2 else q_one
        mine = jnp.where(is_lse, q_ref[:, head_lanes(h % 2)].astype(f32), mine)
        dout_out[:, at] = at_lanes(mine, lane, DELTA_LANE, delta).astype(bf16)
    dout_out.send()
    strips = dot(select_ref[...], dout_out[...]).astype(bf16)
    first = 0
    for out in strip_outs:
        out[...] = strips[first : first + out.shape[0]]
        first += out.shape[0]


def through_projection(grads, section, first, w_ref):
    start = section * C0 + first * NA_DIM
    return dot_last(as_pairs(grads), w_ref[:, start : start + len(grads) * NA_DIM])


def na_own_kernel(heads, q_ref, k_ref, dout_ref, v_ref, w_ref, dxn_out):
    own = dout_ref.shape[0]
    dq, dk, dv = [], [], []
    for i, h in enumerate(heads):
        at = head_lanes(i)
        dout = dout_ref[:, head_lanes(h)]
        prob = jnp.exp(dot_last(q_ref[:, at], k_ref[:, at]))
        dprob = dot_last(dout, v_ref[:, at])
        dscore = (prob * dprob).astype(bf16)
        dq.append(dot(dscore, k_ref[:, at]) * (1.0 / math.sqrt(NA_DIM)))
        dk.append(dot_first(dscore[:, :own], q_ref[:, at]))
        dv.append(dot_first(prob[:, :own].astype(bf16), dout))
    dxn = through_projection(dq, 0, heads[0], w_ref)
    dxn += through_projection(dk, 1, heads[0], w_ref)
    dxn_out[...] = dxn + through_projection(dv, 2, heads[0], w_ref)


def na_rest_kernel(
    heads,
    q_ref,
    k_ref,
    dout_ref,
    v_ref,
    w_ref,
    heads_ref,
    wo_ref,
    m2_ref,
    dxn_out,
    merged_out,
):
    na_own_kernel(heads, q_ref, k_ref, dout_ref, v_ref, w_ref, dxn_out)
    merged = m2_ref[...].astype(f32)
    dim = C2 // GHEADS
    for h in range(GHEADS):
        merged += dot(heads_ref[h, :, 3 * dim :], wo_ref[h * dim : (h + 1) * dim])
    merged_out[...] = merged.astype(bf16)


def na_beside_kernel(
    hot_ref,
    q_halo_ref,
    k_one,
    v_one,
    k_two,
    v_two,
    before_ref,
    after_ref,
    left_ref,
    right_ref,
    w_ref,
    x_ref,
    dxn_one,
    dxn_two,
    dy_ref,
    perm_back_ref,
    grad_out,
    dout_halo_ref,
):
    lane = lax.broadcasted_iota(jnp.int32, (1, LANES), 1)
    is_mask = (lane >= NA_DIM) & (lane < DELTA_LANE)
    is_lse = (lane == LSE_LANE) | (lane == LSE_LANE + 1)
    fill_halo(dout_halo_ref, [before_ref, after_ref, left_ref, right_ref])
    hot = hot_ref[...].astype(f32)
    dk, dv = [], []
    for h in range(NA_HEADS):
        at = head_lanes(h)
        to = head_lanes(h % 2)
        k_ref, v_ref = (k_two, v_two) if h // 2 else (k_one, v_one)
        keys = jnp.where(is_mask, hot, k_ref[:, to].astype(f32)).astype(bf16)
        douts = dout_halo_ref[:, at]
        queries = jnp.where(
            is_lse, douts.astype(f32), q_halo_ref[:, at].astype(f32)
        ).astype(bf16)
        prob = jnp.exp(dot_last(keys, queries))
        dprob = dot_last(v_ref[:, to], douts)
        dk.append(dot((prob * dprob).astype(bf16), queries))
        dv.append(dot(prob.astype(bf16), douts))
    dxn = dxn_one[...] + dxn_two[...] + through_projection(dk, 1, 0, w_ref)
    dxn += through_projection(dv, 2, 0, w_ref)
    x = x_ref[...].astype(f32)
    grad = (dy_ref[...].astype(f32) + rms_back(x, rms_stat(x), dxn)).astype(bf16)
    grad_out[...] = dot(perm_back_ref[...], grad).astype(bf16)


def per_device(image, na_qkv, na_out, merge_one, merge_two, attn_qkv, attn_out, cotangent):
    rows, cols, _ = image.shape
    n_row = lax.axis_size("row")
    n_col = lax.axis_size("col")
    own = rows * cols
    tokens = own // 16
    dim = C2 // GHEADS
    owned = n_row * tokens
    scale = 1.0 / math.sqrt(dim)
    tables = token_tables(rows, cols)
    perm = jnp.asarray(tables["perm"], bf16)
    perm_back = jnp.asarray(tables["perm"].T, bf16)
    select = jnp.asarray(tables["select"], bf16)
    hot = jnp.asarray(tables["hot"], bf16)
    corner = jnp.asarray(tables["corner"], bf16)
    band_own = jnp.asarray(tables["band_own"], bf16)
    halo = tables["halo"]
    padded = halo.shape[0]

    flat = image.reshape(own, C0)
    before, after = row_halo(image[:REACH].reshape(-1, C0), image[-REACH:].reshape(-1, C0))
    left, right = call(
        corner_kernel,
        [((REACH * rows + 2 * ROWS, C0), bf16)] * 2,
        (
            corner,
            before,
            after,
            image[:, :REACH].reshape(-1, C0),
            image[:, -REACH:].reshape(-1, C0),
        ),
        megabytes=8,
    )
    left, right = neighbours(right, left, "col")
    at_row = lax.axis_index("row") * rows + jnp.asarray(halo[:, 0], jnp.int32)
    at_col = lax.axis_index("col") * cols + jnp.asarray(halo[:, 1], jnp.int32)
    inside = (at_row >= 0) & (at_row < rows * n_row) & (at_col >= 0) & (at_col < cols * n_col)
    lane = jnp.arange(LANES)
    mask_lane = (lane >= NA_DIM) & (lane < NA_DIM + rows + cols)
    band_halo = jnp.where(
        ~inside[:, None] & mask_lane[None], MASKED, jnp.asarray(tables["band_halo"], f32)
    ).astype(bf16)

    grad = cotangent.reshape(tokens, C2)
    dout = dot_last(grad, attn_out).astype(bf16)

    heads, m2, xp, q_one, q_two, k_one, k_two, v_one, v_two, q0_halo, a0 = call(
        na_forward_kernel,
        [
            ((GHEADS, tokens, 4 * dim), bf16),
            ((tokens, C2), bf16),
            ((own, C0), bf16),
            ((own, WIDE // 2), bf16),
            ((own, WIDE // 2), bf16),
            ((own + padded, WIDE // 2), bf16),
            ((own + padded, WIDE // 2), bf16),
            ((own + padded, WIDE // 2), bf16),
            ((own + padded, WIDE // 2), bf16),
            ((padded, WIDE), bf16),
            ((own, C0), bf16),
        ],
        (
            flat,
            perm,
            na_qkv,
            before,
            after,
            left,
            right,
            hot,
            band_own,
            band_halo,
            na_out,
            merge_one,
            merge_two,
            attn_qkv,
            dout,
        ),
        manual=(0, 1, 2, 7, 8, 9, 10, 11, 12, 13),
        cuts={13: (1, 3)},
        out_manual=range(1, 11),
        scratch=(pltpu.VMEM((padded, C0), bf16),),
        megabytes=40,
    )

    mine = all_to_all(heads, "row").reshape(owned, 4 * dim)
    keyval, queries = mine[:, : 2 * dim], mine[:, 2 * dim :]
    keyval = jnp.concatenate([keyval, across(keyval)], 0)
    queries = jnp.concatenate(along_z(queries), 0)
    keyval, share = lax.optimization_barrier((keyval, grad))
    share = jnp.broadcast_to(share[None], (n_row, tokens, C2))
    grad_row = all_to_all(share, "row").reshape(owned, C2)
    keyval = along_z(keyval)
    keyval_core = other_core(keyval)
    queries = [queries, across(queries)]
    keyval += keyval_core
    out_heads, stats, send = call(
        functools.partial(attention_kernel, scale),
        [((owned, dim), bf16), ((owned, LANES), f32), ((n_col, dim // n_col, C2 + LANES), bf16)],
        (grad_row, queries[0], *keyval),
    )
    shares = all_to_all(send, "col")
    dq = call(
        functools.partial(query_grad_kernel, scale),
        [((owned, dim), bf16)],
        (stats, queries[0], *keyval),
    )[0]
    queries += other_core(queries)
    part = queries[0].shape[0]
    back = call(
        functools.partial(key_grad_kernel, scale),
        [((owned, 4 * dim), bf16)],
        (column_order(), shares, dq, out_heads, keyval[0], *queries),
        scratch=(pltpu.VMEM((1, part), f32), pltpu.VMEM((1, part), f32)),
        smem=1,
    )[0]
    grad_wo = jnp.sum(shares[:, :, :C2].astype(f32), 0)
    back = all_to_all(back.reshape(n_row, tokens, 4 * dim), "row")

    dout0, dy0, top, bottom, left, right = call(
        merge_back_kernel,
        [((own, WIDE), bf16), ((own, C0), bf16)]
        + [((REACH * n, WIDE), bf16) for n in (cols, cols, rows, rows)],
        (back, attn_qkv, m2, grad, merge_two, merge_one, na_out, a0, q_one, q_two, select),
        manual=range(1, 11),
        out_manual=(1,),
        cuts={1: (1, 3), 4: (0, 4)},
        megabytes=32,
    )
    before, after = row_halo(top, bottom)
    half = NA_HEADS // 2
    dxn_one = call(
        functools.partial(na_own_kernel, range(half)),
        [((own, C0), f32)],
        (q_one, k_one, dout0, v_one, na_qkv),
        manual=(0, 1, 3, 4),
    )[0]
    before, after, dxn_one = lax.optimization_barrier((before, after, dxn_one))
    left, right = call(
        corner_kernel,
        [((left.shape[0] + 2 * ROWS, WIDE), bf16)] * 2,
        (corner, before, after, left, right),
        megabytes=8,
    )
    left, right, q_two = lax.optimization_barrier((left, right, q_two))
    left, right = neighbours(right, left, "col")
    dxn_two, merged = call(
        functools.partial(na_rest_kernel, range(half, NA_HEADS)),
        [((own, C0), f32), ((tokens, C2), bf16)],
        (q_two, k_two, dout0, v_two, na_qkv, back, attn_out, m2),
        manual=(0, 1, 3, 4, 6, 7),
        megabytes=20,
    )
    grad_image = call(
        na_beside_kernel,
        [((own, C0), bf16)],
        (
            hot,
            q0_halo,
            Rows(k_one, own),
            Rows(v_one, own),
            Rows(k_two, own),
            Rows(v_two, own),
            before,
            after,
            left,
            right,
            na_qkv,
            xp,
            dxn_one,
            dxn_two,
            dy0,
            perm_back,
        ),
        manual=(0, 1, 2, 3, 4, 5, 10, 11, 14, 15),
        scratch=(pltpu.VMEM((padded, WIDE), bf16),),
    )[0]
    return (
        merged.reshape(rows // 4, cols // 4, C2),
        grad_image.reshape(rows, cols, C0),
        grad_wo,
    )


def solution(mesh):
    return jax.shard_map(
        per_device,
        mesh=mesh,
        in_specs=(P("row", "col", None), P(), P(), P(), P(), P(), P(), P("row", "col", None)),
        out_specs=(P("row", "col", None), P("row", "col", None), P(("row", "col"), None)),
        check_vma=False,
    )
```
